32 devices in a mesh: groups: 2 (over x), wide: 4 (over y, core), narrow: 4 (over z).
Axes of the slice: x: 2, y: 2, z: 4, core: 2. Of those that a mesh axis runs over, the one named last changes fastest.
Arguments:
- activations: bfloat16 [128, 18432], P('groups', 'wide'), parts along dimension 0, may hold values from -160 to 160
- norm_gain: float32 [18432], P('wide'), may hold values from 0.1 to 1.9
- query_weight: bfloat16 [18432, 12288], P('wide', 'narrow'), may hold values from -0.046875 to 0.046875
- kv_weight: bfloat16 [18432, 512], P(('wide', 'narrow')), may hold values from -0.046875 to 0.046875
- out_weight: bfloat16 [12288, 18432], P('narrow', 'wide'), may hold values from -0.375 to 0.375
- kv_cache: bfloat16 [128, 1024, 512], P(('groups', 'wide', 'narrow')), parts along dimension 0, may hold values from -128 to 128
- lengths: int32 [128], P(('groups', 'wide', 'narrow')), parts along dimension 0, may hold values from 1 to 1024, as said below
Outputs:
- attended: bfloat16 [128, 18432], P(('groups', 'narrow'), 'wide'), parts along dimension 0
The draws below stay inside these ranges and needn't reach their ends.
There are 2 independent parts, one for each index of `groups`. The reference program is written for one: setup_inputs(seed, part) draws one part's arguments, and reference() takes and returns one part's arrays. A program takes and returns all parts, laid end to end along the dimension named above; an argument that names none is the same for every part. Nothing has to cross between parts.
Inputs may be any that keep to these rules, and one draw needn't show every extreme that they name: `lengths`: each row names how many leading cache positions hold its history; some row uses all 1024.
All inputs are finite; a program needn't handle non-finite values.
Results may differ from the reference program's by a relative error of at most 0.00585.
The reference program's roundings to bfloat16 on the way count: a program that leaves them out, or rounds other values in their place, can miss the bound.
Values may be sent and summed in bfloat16 or wider, within the bound.
No kernel may reach another device: no remote copies, remote signals or barrier semaphores. Data moves between devices by JAX's collectives and lax.ppermute only.
A program may use at most 128 MiB of HBM per device.

```python
import jax
import jax.numpy as jnp
from jax import lax

D = 18432
HEADS = 48
HD = 256
CTX = 1024
ROWS = 64


def draw_activations(key, part):
    key = jax.random.fold_in(key, 1)
    first, second, third = jax.random.split(key, 3)
    base = jnp.clip(jax.random.normal(first, (ROWS, D), jnp.float32), -6.0, 6.0)
    column = jnp.arange(D, dtype=jnp.float32) / D
    col_scale = 10.0 ** (0.5 * column + 0.5 * jax.random.uniform(second, (D,), jnp.float32))
    row_scale = 10.0 ** jax.random.uniform(third, (ROWS, 1), jnp.float32)
    return (base * col_scale[None, :] * row_scale * 0.25).astype(jnp.bfloat16)


def draw_kv_cache(key, part):
    key = jax.random.fold_in(key, 2)
    first = jax.random.fold_in(key, 0)
    base = jnp.clip(jax.random.normal(first, (ROWS, CTX, 2 * HD), jnp.float32), -6.0, 6.0)
    return base.astype(jnp.bfloat16)


def draw_lengths(key, part):
    key = jax.random.fold_in(key, 3)
    first, second = jax.random.split(key, 2)
    drawn = jax.random.randint(first, (ROWS,), 1, CTX + 1, dtype=jnp.int32)
    picked = jax.random.randint(second, (), 0, ROWS, dtype=jnp.int32)
    return drawn.at[picked].set(CTX)


def block_levels(rng, extent, cuts, least, largest):
    gain = 1.0
    for dim, shards_of in cuts:
        heights = jax.random.uniform(jax.random.fold_in(jax.random.fold_in(rng, 6), dim), (shards_of,), jnp.float32, least / len(cuts), largest / len(cuts))
        gain = gain * jnp.repeat(jnp.exp(heights), extent[dim] // shards_of).reshape((-1,) + (1,) * (len(extent) - 1 - dim))
    return gain


def bell_draw(key, dims, deviation, reach, cuts=(), held_as=jnp.bfloat16):
    loudness = block_levels(key, dims, cuts, -0.22, 0.18) if cuts else 1.0
    result = jax.random.normal(key, dims, jnp.float32) * deviation * loudness
    return jnp.minimum(jnp.maximum(result, -reach), reach).astype(held_as)


def setup_inputs(seed: int = 0, part: int = 0) -> dict:
    arg_keys = jax.random.split(jax.random.key(seed), 8)
    part_splits = jax.random.split(jax.random.fold_in(arg_keys[7], part), 8)
    activations = draw_activations(jax.random.fold_in(jax.random.fold_in(arg_keys[7], part), 71), part)
    norm_gain = jnp.clip(1.0 + 0.18 * jax.random.normal(arg_keys[1], (D,), jnp.float32), 0.1, 1.9)
    query_weight = bell_draw(arg_keys[2], (D, HEADS * HD), D ** -0.5, 0.046875, ((0, 4), (1, 4)))
    kv_weight = bell_draw(arg_keys[3], (D, 2 * HD), D ** -0.5, 0.046875, ((0, 16),))
    out_weight = bell_draw(arg_keys[4], (HEADS * HD, D), HD ** -0.5, 0.375, ((0, 4), (1, 4)))
    kv_cache = draw_kv_cache(jax.random.fold_in(jax.random.fold_in(arg_keys[7], part), 71), part)
    lengths = draw_lengths(jax.random.fold_in(jax.random.fold_in(arg_keys[7], part), 71), part)
    return {"activations": activations, "norm_gain": norm_gain, "query_weight": query_weight, "kv_weight": kv_weight, "out_weight": out_weight, "kv_cache": kv_cache, "lengths": lengths}


def reference(activations, norm_gain, query_weight, kv_weight, out_weight, kv_cache, lengths):
    values = activations.astype(jnp.float32)
    center = lax.optimization_barrier(jnp.mean(values, axis=1, keepdims=True))
    spread = lax.optimization_barrier(jnp.mean((values - center) * (values - center), axis=1, keepdims=True))
    normed = ((values - center) * lax.rsqrt(spread + 1e-05) * norm_gain[None, :]).astype(jnp.bfloat16)
    queries = jnp.dot(normed, query_weight, preferred_element_type=jnp.float32).astype(jnp.bfloat16)
    fresh = jnp.dot(normed, kv_weight, preferred_element_type=jnp.float32).astype(jnp.bfloat16)
    scaling = 1.0 / HD ** 0.5
    query_heads = queries.reshape(ROWS, HEADS, HD).astype(jnp.float32)
    new_keys = fresh[:, :HD].astype(jnp.float32)
    new_values = fresh[:, HD:].astype(jnp.float32)
    cache_keys = kv_cache[:, :, :HD].astype(jnp.float32)
    scores = jnp.einsum('rhd,rld->rhl', query_heads, cache_keys) * scaling
    positions = jnp.arange(CTX, dtype=jnp.int32)
    valid = (positions[None, :] < lengths[:, None])[:, None, :]
    own_score = lax.optimization_barrier(jnp.sum(query_heads * new_keys[:, None, :], axis=2)) * scaling
    top = jnp.maximum(lax.optimization_barrier(jnp.max(jnp.where(valid, scores, -jnp.inf), axis=2)), own_score)
    weights = jnp.where(valid, jnp.exp(scores - top[..., None]), 0.0)
    own_weight = jnp.exp(own_score - top)
    total = lax.optimization_barrier(jnp.sum(weights, axis=2)) + own_weight
    cache_values = kv_cache[:, :, HD:].astype(jnp.float32)
    numer = jnp.einsum('rhl,rld->rhd', weights.astype(jnp.bfloat16).astype(jnp.float32), cache_values)
    own_rounded = lax.optimization_barrier(own_weight.astype(jnp.bfloat16)).astype(jnp.float32)
    numer = numer + own_rounded[..., None] * new_values[:, None, :]
    context = (numer / total[..., None]).astype(jnp.bfloat16).reshape(ROWS, HEADS * HD)
    return jnp.dot(context, out_weight, preferred_element_type=jnp.float32).astype(jnp.bfloat16)
```

```python
import math

import jax
import jax.numpy as jnp
from jax import lax
from jax.sharding import PartitionSpec as P


def swap(x, axis, distance):
    count = lax.axis_size(axis)
    return lax.ppermute(x, axis, [(i, i ^ distance) for i in range(count)])


def sum_over(x, axis):
    count = lax.axis_size(axis)
    if count <= 4:
        parts = [swap(x, axis, d) for d in range(1, count)]
        for part in parts:
            x = x + part
        return x
    d = 1
    while d < count:
        x = x + swap(x, axis, d)
        d *= 2
    return x


def scatter_sum(x, axis):
    count = lax.axis_size(axis)
    me = lax.axis_index(axis)
    rows, columns = x.shape[0] // count, x.shape[1]
    left, d = count, 1
    while d < count:
        bit = (me // d) % 2
        x = x.reshape(left // 2, 2, rows, columns)
        sent = lax.dynamic_index_in_dim(x, 1 - bit, 1, keepdims=False)
        kept = lax.dynamic_index_in_dim(x, bit, 1, keepdims=False)
        x = kept + swap(sent, axis, d)
        left //= 2
        d *= 2
    return x.reshape(rows, columns)


def exchange(blocks, axis):
    return [blocks[0]] + [swap(b, axis, d) for d, b in enumerate(blocks) if d]


def in_order(blocks, axis):
    me = lax.axis_index(axis)
    out = jnp.zeros((len(blocks),) + blocks[0].shape, blocks[0].dtype)
    for d, b in enumerate(blocks):
        out = lax.dynamic_update_index_in_dim(out, b, me ^ d, 0)
    return out.reshape((-1,) + blocks[0].shape[1:])


def gather(x, axis):
    count = lax.axis_size(axis)
    blocks = {0: x}
    d = count // 2
    while d:
        blocks |= {k ^ d: swap(b, axis, d) for k, b in blocks.items()}
        d //= 2
    return in_order([blocks[k] for k in range(count)], axis)


def attend(query_heads, kv_cache, fresh, lengths):
    row_count, head_count, head_dim = query_heads.shape
    scaling = 1.0 / math.sqrt(head_dim)
    new_keys = fresh[:, :head_dim]
    new_values = fresh[:, head_dim:]
    own_score = (
        jnp.einsum("rhd,rd->rh", query_heads, new_keys, preferred_element_type=jnp.float32)
        * scaling
    )
    scores = (
        jnp.einsum("rhd,rld->rhl", query_heads, kv_cache[:, :, :head_dim], preferred_element_type=jnp.float32)
        * scaling
    )
    positions = jnp.arange(kv_cache.shape[1], dtype=jnp.int32)
    valid = (positions[None, :] < lengths[:, None])[:, None, :]
    top = jnp.maximum(jnp.max(jnp.where(valid, scores, -jnp.inf), axis=2), own_score)
    weights = jnp.where(valid, jnp.exp(scores - top[..., None]), 0.0)
    numer = jnp.einsum(
        "rhl,rld->rhd",
        weights.astype(jnp.bfloat16),
        kv_cache[:, :, head_dim:],
        preferred_element_type=jnp.float32,
    )
    own_weight = jnp.exp(own_score - top)
    total = jnp.sum(weights, axis=2) + own_weight
    own_rounded = lax.optimization_barrier(own_weight.astype(jnp.bfloat16)).astype(jnp.float32)
    numer = numer + own_rounded[..., None] * new_values.astype(jnp.float32)[:, None, :]
    return (numer / total[..., None]).astype(jnp.bfloat16)


def local(activations, norm_gain, query_weight, kv_weight, out_weight, kv_cache, lengths):
    wide_count = lax.axis_size("wide")
    narrow_count = lax.axis_size("narrow")
    narrow = lax.axis_index("narrow")
    own_rows, head_dim = kv_cache.shape[0], kv_cache.shape[2] // 2
    values = activations.astype(jnp.float32)
    width_all = activations.shape[1] * wide_count
    sums = jnp.stack([jnp.sum(values, axis=1), jnp.sum(values * values, axis=1)])
    sums, squares = sum_over(sums, "wide")
    center = sums / width_all
    spread = squares / width_all - center * center
    normed = (
        (values - center[:, None]) * lax.rsqrt(spread + 1e-05)[:, None] * norm_gain[None, :]
    ).astype(jnp.bfloat16)
    sub_width = normed.shape[1] // narrow_count
    own_columns = lax.dynamic_slice_in_dim(normed, narrow * sub_width, sub_width, 1)
    fresh_part = jnp.dot(own_columns, kv_weight, preferred_element_type=jnp.float32)
    query_part = jnp.dot(normed, query_weight, preferred_element_type=jnp.float32)
    fresh_part = scatter_sum(fresh_part, "wide")
    summed = scatter_sum(query_part, "wide").astype(jnp.bfloat16)
    fresh = scatter_sum(fresh_part, "narrow").astype(jnp.bfloat16)
    by_owner = summed.reshape(narrow_count, own_rows, -1, head_dim)
    blocks = [lax.dynamic_index_in_dim(by_owner, narrow ^ d, 0, keepdims=False) for d in range(narrow_count)]
    heads = jnp.concatenate(exchange(blocks, "narrow"), axis=1)
    context = attend(heads, kv_cache, fresh, lengths)
    context = context.reshape(own_rows, narrow_count, -1)
    returned = in_order(exchange([context[:, d] for d in range(narrow_count)], "narrow"), "narrow")
    gathered = gather(returned, "wide")
    columns = out_weight.shape[1]
    cuts = 2
    outs = []
    for c in range(cuts):
        part = out_weight[:, c * columns // cuts : (c + 1) * columns // cuts]
        product = jnp.dot(gathered, part, preferred_element_type=jnp.float32)
        outs.append(scatter_sum(product, "narrow").astype(jnp.bfloat16))
    return jnp.concatenate(outs, axis=1)


def solution(mesh):
    return jax.shard_map(
        local,
        mesh=mesh,
        in_specs=(
            P("groups", "wide"),
            P("wide"),
            P("wide", "narrow"),
            P(("wide", "narrow"), None),
            P("narrow", "wide"),
            P(("groups", "wide", "narrow"), None, None),
            P(("groups", "wide", "narrow")),
        ),
        out_specs=P(("groups", "narrow"), "wide"),
        check_vma=False,
    )
```

```python
import functools
import math

import jax
import jax.numpy as jnp
from jax import lax
from jax.experimental import pallas as pl
from jax.experimental.pallas import tpu as pltpu
from jax.sharding import PartitionSpec as P

MIB = 1 << 20
FULL = pl.BlockSpec(memory_space=pltpu.VMEM)
ANY = pl.BlockSpec(memory_space=pl.ANY)
SCALAR = pl.BlockSpec(memory_space=pltpu.SMEM)
STEPS = 32700.0
TINY = 1e-37
LANES = 128


def call(kernel, outs, ins, specs, name, scratch=(), limit=4, flops=0, moved=0):
    return pl.pallas_call(
        kernel,
        out_shape=outs,
        in_specs=specs,
        out_specs=jax.tree.map(lambda _: FULL, outs),
        scratch_shapes=list(scratch),
        compiler_params=pltpu.CompilerParams(vmem_limit_bytes=limit * MIB),
        cost_estimate=pl.CostEstimate(flops=flops, bytes_accessed=moved, transcendentals=0),
        name=name,
    )(*ins)


def held(shape, dtype):
    return pltpu.VMEM(shape, dtype)


def in_vmem(x):
    return pltpu.with_memory_space_constraint(x, pltpu.VMEM)


def in_hbm(x):
    return pltpu.with_memory_space_constraint(x, pltpu.HBM)


def swap(x, axis, distance):
    count = lax.axis_size(axis)
    return lax.ppermute(x, axis, [(i, i ^ distance) for i in range(count)])


def sent_apart(x, axis):
    count = lax.axis_size(axis)
    if count <= 4:
        return [x] + [swap(x, axis, d) for d in range(1, count)]
    d = 1
    while d < count:
        x = x + swap(x, axis, d)
        d *= 2
    return [x]


def exchange(blocks, axis):
    return [blocks[0]] + [swap(b, axis, d) for d, b in enumerate(blocks) if d]


def gather(x, axis):
    count = lax.axis_size(axis)
    blocks = {0: x}
    d = count // 2
    while d:
        blocks |= {k ^ d: swap(b, axis, d) for k, b in blocks.items()}
        d //= 2
    return [blocks[k] for k in range(count)]


def halving_order(count):
    bits = count.bit_length() - 1
    return [sum(((k >> b) & 1) << (bits - 1 - b) for b in range(bits)) for k in range(count)]


def thirds(tiles):
    first, second = tiles // 6, tiles // 2
    return first, second, tiles - first - second


def stats_kernel(me_ref, gain_ref, x_ref, w_ref, out_ref, part_ref, sem):
    rows, width = x_ref.shape
    fetch = pltpu.make_async_copy(w_ref.at[:, : part_ref.shape[1]], part_ref, sem)
    fetch.start()
    total = jnp.zeros((rows, LANES), jnp.float32)
    squares = jnp.zeros((rows, LANES), jnp.float32)
    for c in range(0, width, LANES):
        part = x_ref[:, c : c + LANES].astype(jnp.float32)
        total += part
        squares += part * part
    total = jnp.sum(total, axis=1, keepdims=True)
    squares = jnp.sum(squares, axis=1, keepdims=True)
    row = lax.broadcasted_iota(jnp.int32, (rows, rows), 0)
    column = lax.broadcasted_iota(jnp.int32, (rows, rows), 1)
    out_ref[0:1, :] = jnp.sum(jnp.where(row == column, total, 0.0), axis=0, keepdims=True)
    out_ref[1:2, :] = jnp.sum(jnp.where(row == column, squares, 0.0), axis=0, keepdims=True)
    fetch.wait()


def fetch_kernel(starts, *refs):
    count = len(starts)
    sources, shares, sems = refs[:count], refs[count + 1 : 2 * count + 1], refs[-1]
    fetches = []
    for k, start in enumerate(starts):
        source = sources[k] if start is None else sources[k].at[:, pl.ds(start, shares[k].shape[1])]
        fetches.append(pltpu.make_async_copy(source, shares[k], sems.at[k]))
    for fetch in fetches:
        fetch.start()
    for fetch in fetches:
        fetch.wait()


def fetch(items, after, name):
    shapes = [x.shape if start is None else (x.shape[0], width) for x, start, width in items]
    return call(
        functools.partial(fetch_kernel, [start for _, start, _ in items]),
        [held(shape, x.dtype) for shape, (x, _, _) in zip(shapes, items)],
        (*[in_hbm(x) for x, _, _ in items], after),
        [ANY] * (len(items) + 1),
        name,
        scratch=[pltpu.SemaphoreType.DMA((len(items),))],
        moved=sum(2 * math.prod(shape) for shape in shapes),
    )


def project_kernel(width_all, count, narrow_count, tile, me_ref, *refs):
    stat_refs = refs[:-12]
    x_ref, gain_ref, w_ref, kv_ref, first_ref, second_ref, kept_ref, sent_ref, normed, own, rest, sems = refs[-12:]
    rows, width = x_ref.shape
    half = rows // 2
    block = rows // count
    sub_width = width // narrow_count
    done = first_ref.shape[1] + second_ref.shape[1]
    fetches = [
        pltpu.make_async_copy(
            w_ref.at[:, done + t * tile : done + (t + 1) * tile], rest.at[:, t * tile : (t + 1) * tile], sems.at[t]
        )
        for t in range(rest.shape[1] // tile)
    ]
    for fetch in fetches:
        fetch.start()
    me, narrow = me_ref[0], me_ref[1]
    stats = stat_refs[0][...]
    for ref in stat_refs[1:]:
        stats = stats + ref[...]
    row = lax.broadcasted_iota(jnp.int32, (rows, rows), 0)
    column = lax.broadcasted_iota(jnp.int32, (rows, rows), 1)
    sums = jnp.sum(jnp.where(row == column, stats[0:1, :], 0.0), axis=1, keepdims=True)
    squares = jnp.sum(jnp.where(row == column, stats[1:2, :], 0.0), axis=1, keepdims=True)
    center = sums / width_all
    spread = squares / width_all - center * center
    inverse = lax.rsqrt(spread + 1e-05)
    order = halving_order(count)
    for j in range(count):
        pick = slice(j * block, (j + 1) * block)
        place = jnp.int32(0)
        for k, d in enumerate(order):
            place = jnp.where((me ^ d) == j, k, place)
        place = pl.multiple_of(place * block, 16)
        scaled = (x_ref[pick, :].astype(jnp.float32) - center[pick]) * inverse[pick] * gain_ref[...]
        normed[pl.ds(place, block), :] = scaled.astype(jnp.bfloat16)
    for j in range(narrow_count):
        @pl.when(narrow == j)
        def _(j=j):
            own[...] = normed[:, j * sub_width : (j + 1) * sub_width]

    def put(got, at):
        kept_ref[:, at] = got[:half, :]
        sent_ref[:, at] = got[half:, :]

    def products(source, start):
        @pl.loop(0, source.shape[1] // tile)
        def _(t):
            got = jnp.dot(
                normed[...], source[:, pl.ds(pl.multiple_of(t * tile, tile), tile)], preferred_element_type=jnp.float32
            )
            put(got, pl.ds(pl.multiple_of(start + t * tile, tile), tile))

    put(jnp.dot(own[...], kv_ref[...], preferred_element_type=jnp.float32), slice(w_ref.shape[1], kept_ref.shape[1]))
    products(first_ref, 0)
    products(second_ref, first_ref.shape[1])
    for fetch in fetches:
        fetch.wait()
    products(rest, done)


def project(me, stats, x, gain, w, kv, first, second, width_all, count, narrow_count, tile):
    rows, width = x.shape
    queries = w.shape[1]
    rest = queries - first.shape[1] - second.shape[1]
    half = jax.ShapeDtypeStruct((rows // 2, queries + kv.shape[1]), jnp.float32)
    return call(
        functools.partial(project_kernel, width_all, count, narrow_count, tile),
        (half, half),
        (me, *stats, x, gain, in_hbm(w), in_vmem(kv), in_vmem(first), in_vmem(second)),
        [SCALAR] + [FULL] * (len(stats) + 2) + [ANY] + [FULL] * 3,
        "project",
        scratch=[
            pltpu.VMEM((rows, width), jnp.bfloat16),
            pltpu.VMEM((rows, width // narrow_count), jnp.bfloat16),
            pltpu.VMEM((width, rest), jnp.bfloat16),
            pltpu.SemaphoreType.DMA((rest // tile,)),
        ],
        limit=18,
        flops=2 * rows * width * queries,
        moved=2 * width * rest,
    )


def fold_kernel(guards, kept_ref, came_ref, *refs):
    still_ref, sent_ref = refs[guards:]
    half = still_ref.shape[0]
    still_ref[...] = kept_ref[:half, :] + came_ref[:half, :]
    sent_ref[...] = kept_ref[half:, :] + came_ref[half:, :]


def fold(kept, came, guards):
    half = jax.ShapeDtypeStruct((kept.shape[0] // 2, kept.shape[1]), jnp.float32)
    return call(
        functools.partial(fold_kernel, len(guards)),
        (half, half),
        (kept, came, *map(in_vmem, guards)),
        [FULL] * (2 + len(guards)),
        "fold",
        moved=16 * kept.size,
    )


def split_kernel(queries, guards, me_ref, kept_ref, came_ref, *refs):
    out_refs = refs[guards:]
    count, rows = len(out_refs), out_refs[0].shape[0]
    narrow = me_ref[1]
    total = kept_ref[...] + came_ref[...]
    parts = [total[j * rows : (j + 1) * rows, :] for j in range(count)]
    for d, out_ref in enumerate(out_refs):
        mine = parts[0]
        for j in range(1, count):
            mine = jnp.where((narrow ^ d) == j, parts[j], mine)
        out_ref[:, :queries] = mine[:, :queries].astype(jnp.bfloat16)
        left = mine[:, queries:]
        width = left.shape[1]
        for term in range(3):
            high = left.astype(jnp.bfloat16)
            out_ref[:, queries + term * width : queries + (term + 1) * width] = high
            left = left - high.astype(jnp.float32)


PAD = 8


def attend_kernel(head_dim, guards, lengths_ref, *refs):
    count = (len(refs) - guards - 3) // 2
    came_refs, kv_ref = refs[:count], refs[count]
    out_refs, heads, contexts = refs[count + 1 + guards : -2], refs[-2], refs[-1]
    rows, positions = kv_ref.shape[0], kv_ref.shape[1]
    queries = out_refs[0].shape[1]
    each = queries // head_dim
    total_heads = each * count
    slabs = head_dim // LANES
    scaling = 1.0 / math.sqrt(head_dim)
    for d, ref in enumerate(came_refs):
        for h in range(each):
            at = (d * each + h) * PAD
            for k in range(slabs):
                start = h * head_dim + k * LANES
                heads[k, at : at + rows, :] = ref[:, start : start + LANES].astype(jnp.float32)
    terms = came_refs[0][:, queries:].astype(jnp.float32)
    for ref in came_refs[1:]:
        terms = terms + ref[:, queries:].astype(jnp.float32)
    pair = 2 * head_dim
    fresh = terms[:, :pair] + (terms[:, pair : 2 * pair] + terms[:, 2 * pair :])
    fresh = fresh.astype(jnp.bfloat16).astype(jnp.float32)
    place = lax.broadcasted_iota(jnp.int32, (total_heads, positions), 1)
    for r in range(rows):
        query = jnp.concatenate([heads[k, pl.ds(r, total_heads, stride=PAD), :] for k in range(slabs)], axis=1)
        scores = (
            lax.dot_general(
                query.astype(jnp.bfloat16),
                kv_ref[r, :, :head_dim],
                (((1,), (1,)), ((), ())),
                preferred_element_type=jnp.float32,
            )
            * scaling
        )
        own_score = jnp.sum(query * fresh[r : r + 1, :head_dim], axis=1, keepdims=True) * scaling
        valid = place < lengths_ref[r]
        top = jnp.maximum(jnp.max(jnp.where(valid, scores, -jnp.inf), axis=1, keepdims=True), own_score)
        weights = jnp.where(valid, jnp.exp(scores - top), 0.0)
        own_weight = jnp.exp(own_score - top)
        total = jnp.sum(weights, axis=1, keepdims=True) + own_weight
        numer = jnp.dot(weights.astype(jnp.bfloat16), kv_ref[r, :, head_dim:], preferred_element_type=jnp.float32)
        numer = numer + own_weight.astype(jnp.bfloat16).astype(jnp.float32) * fresh[r : r + 1, head_dim:]
        context = numer / total
        for k in range(slabs):
            contexts[k, pl.ds(r, total_heads, stride=PAD), :] = context[:, k * LANES : (k + 1) * LANES]
    for d, ref in enumerate(out_refs):
        for h in range(each):
            at = (d * each + h) * PAD
            for k in range(slabs):
                start = h * head_dim + k * LANES
                ref[:, start : start + LANES] = contexts[k, at : at + rows, :].astype(jnp.bfloat16)


def attend(lengths, came, kv, head_dim, queries, guards):
    rows = kv.shape[0]
    count = len(came)
    all_heads = count * queries // head_dim
    scratch = pltpu.VMEM((head_dim // LANES, all_heads * PAD, LANES), jnp.float32)
    return call(
        functools.partial(attend_kernel, head_dim, len(guards)),
        [jax.ShapeDtypeStruct((rows, queries), jnp.bfloat16)] * count,
        (lengths, *came, in_vmem(kv), *map(in_vmem, guards)),
        [SCALAR] + [FULL] * (count + 1 + len(guards)),
        "attend",
        scratch=[scratch, scratch],
        limit=8,
        flops=4 * rows * count * queries * kv.shape[1],
    )


def join_kernel(me_ref, *refs):
    came_refs, out_ref, joined = refs[:-2], refs[-2], refs[-1]
    rows = came_refs[0].shape[0]
    narrow = me_ref[1]
    came = [ref[...].astype(jnp.float32) for ref in came_refs]
    for j in range(len(came)):
        mine = came[0]
        for d in range(1, len(came)):
            mine = jnp.where((narrow ^ j) == d, came[d], mine)
        joined[j * rows : (j + 1) * rows, :] = mine
    out_ref[...] = joined[...].astype(jnp.bfloat16)


def arrange_kernel(narrow_count, me_ref, *refs):
    came_refs, out_ref, natural = refs[:-2], refs[-2], refs[-1]
    block = came_refs[0].shape[0]
    for d, ref in enumerate(came_refs):
        natural[pl.ds(pl.multiple_of((me_ref[0] ^ d) * block, 16), block), :] = ref[...]
    block = out_ref.shape[0] // narrow_count
    for k, d in enumerate(halving_order(narrow_count)):
        at = pl.ds(pl.multiple_of((me_ref[1] ^ d) * block, 16), block)
        out_ref[k * block : (k + 1) * block, :] = natural[at, :]


def code(x, ref):
    largest = jnp.maximum(jnp.max(jnp.abs(x), axis=1, keepdims=True), TINY)
    power = jnp.floor(jnp.log2(largest)) + 1.0
    steps = jnp.round(x * (STEPS * jnp.exp2(-power)))
    ref[:, : x.shape[1]] = steps.astype(jnp.int32).astype(jnp.int16)
    ref[:, x.shape[1] :] = jnp.broadcast_to(power, (x.shape[0], LANES)).astype(jnp.int32).astype(jnp.int16)


def decode(ref, width):
    power = ref[:, width:].astype(jnp.int32).astype(jnp.float32)[:, 0:1]
    return ref[:, :width].astype(jnp.int32).astype(jnp.float32) * (jnp.exp2(power) * (1.0 / STEPS))


def output_kernel(tile, x_ref, w_ref, kept_ref, sent_ref, product):
    half = kept_ref.shape[0]

    @pl.loop(0, w_ref.shape[1] // tile)
    def _(t):
        at = pl.ds(pl.multiple_of(t * tile, tile), tile)
        product[:, at] = jnp.dot(x_ref[...], w_ref[:, at], preferred_element_type=jnp.float32)

    kept_ref[...] = product[:half, :]
    code(product[half:, :], sent_ref)


def output_part(x, w):
    rows, columns = x.shape[0], w.shape[1]
    return call(
        functools.partial(output_kernel, 256 if columns % 256 == 0 else LANES),
        (
            jax.ShapeDtypeStruct((rows // 2, columns), jnp.float32),
            jax.ShapeDtypeStruct((rows // 2, columns + LANES), jnp.int16),
        ),
        (x, in_vmem(w)),
        [FULL, FULL],
        "output_part",
        scratch=[pltpu.VMEM((rows, columns), jnp.float32)],
        limit=6,
        flops=2 * rows * w.size,
        moved=2 * x.size,
    )


def halve_kernel(kept_ref, came_ref, still_ref, sent_ref):
    half = still_ref.shape[0]
    total = kept_ref[...] + decode(came_ref, kept_ref.shape[1])
    still_ref[...] = total[:half, :]
    code(total[half:, :], sent_ref)


def halve(kept, came):
    rows, columns = kept.shape
    return call(
        halve_kernel,
        (
            jax.ShapeDtypeStruct((rows // 2, columns), jnp.float32),
            jax.ShapeDtypeStruct((rows // 2, columns + LANES), jnp.int16),
        ),
        (kept, came),
        [FULL, FULL],
        "halve",
        moved=16 * kept.size,
    )


def finish_kernel(*refs):
    out_ref = refs[-1]
    at = 0
    for kept_ref, came_ref in zip(refs[:-1:2], refs[1:-1:2]):
        width = kept_ref.shape[1]
        out_ref[:, at : at + width] = (kept_ref[...] + decode(came_ref, width)).astype(jnp.bfloat16)
        at += width


def local(activations, norm_gain, query_weight, kv_weight, out_weight, kv_cache, lengths):
    wide_count = lax.axis_size("wide")
    narrow_count = lax.axis_size("narrow")
    me = jnp.stack([lax.axis_index("wide"), lax.axis_index("narrow")]).astype(jnp.int32)
    own_rows, head_dim = kv_cache.shape[0], kv_cache.shape[2] // 2
    rows, width = activations.shape
    queries = query_weight.shape[1]
    columns = out_weight.shape[1]
    cuts = 3
    cut = columns // cuts
    tile = 256
    first, second, _ = thirds(queries // tile)
    gain = norm_gain[None]
    stats, first_part = call(
        stats_kernel,
        (jax.ShapeDtypeStruct((2, rows), jnp.float32), held((width, first * tile), jnp.bfloat16)),
        (me, gain, activations, in_hbm(query_weight)),
        [SCALAR, FULL, FULL, ANY],
        "row_sums",
        scratch=[pltpu.SemaphoreType.DMA],
        moved=2 * width * first * tile,
    )
    second_part, kv_part = fetch(
        [(query_weight, first * tile, second * tile), (kv_weight, None, None)], stats, "fetch_query_weight"
    )
    kept, sent = project(
        me,
        sent_apart(stats, "wide"),
        activations,
        gain,
        query_weight,
        kv_part,
        first_part,
        second_part,
        width * wide_count,
        wide_count,
        narrow_count,
        tile,
    )
    out_parts = list(fetch([(out_weight, 0, cut)], sent, "fetch_out_weight_0"))
    guards = [out_parts[0]]
    d = 1
    while 2 * d < wide_count:
        kept, sent = fold(kept, swap(sent, "wide", d), guards)
        guards = []
        d *= 2
    fetched = fetch([(out_weight, cut, cut), (kv_cache, None, None)], sent, "fetch_out_weight_1")
    out_parts.append(fetched[0])
    split = call(
        functools.partial(split_kernel, queries, 1),
        [jax.ShapeDtypeStruct((own_rows, queries + 6 * head_dim), jnp.bfloat16)] * narrow_count,
        (me, kept, swap(sent, "wide", d), in_vmem(fetched[0])),
        [SCALAR] + [FULL] * 3,
        "split",
        moved=16 * kept.size,
    )
    out_parts += fetch([(out_weight, 2 * cut, cut)], split[0], "fetch_out_weight_2")
    context = attend(lengths, exchange(split, "narrow"), fetched[1], head_dim, queries, [out_parts[2]])
    returned = call(
        join_kernel,
        jax.ShapeDtypeStruct((narrow_count * own_rows, queries), jnp.bfloat16),
        (me, *exchange(context, "narrow")),
        [SCALAR] + [FULL] * narrow_count,
        "join",
        scratch=[pltpu.VMEM((narrow_count * own_rows, queries), jnp.float32)],
        moved=4 * narrow_count * own_rows * queries,
    )
    arranged = call(
        functools.partial(arrange_kernel, narrow_count),
        jax.ShapeDtypeStruct((rows, queries), jnp.bfloat16),
        (me, *gather(returned, "wide")),
        [SCALAR] + [FULL] * wide_count,
        "arrange",
        scratch=[pltpu.VMEM((rows, queries), jnp.bfloat16)],
        moved=4 * rows * queries,
    )
    pairs = []
    for part in out_parts:
        kept, sent = output_part(arranged, part)
        d = 1
        while d < narrow_count:
            came = swap(sent, "narrow", d)
            d *= 2
            if d < narrow_count:
                kept, sent = halve(kept, came)
        pairs += [kept, came]
    return call(
        finish_kernel,
        jax.ShapeDtypeStruct((rows // narrow_count, columns), jnp.bfloat16),
        pairs,
        [FULL] * len(pairs),
        "finish",
        moved=8 * columns * rows // narrow_count,
    )


def solution(mesh):
    return jax.shard_map(
        local,
        mesh=mesh,
        in_specs=(
            P("groups", "wide"),
            P("wide"),
            P("wide", "narrow"),
            P(("wide", "narrow"), None),
            P("narrow", "wide"),
            P(("groups", "wide", "narrow"), None, None),
            P(("groups", "wide", "narrow")),
        ),
        out_specs=P(("groups", "narrow"), "wide"),
        check_vma=False,
    )
```

```python
import functools
import math

import jax
import jax.numpy as jnp
from jax import lax
from jax.experimental import pallas as pl
from jax.experimental.pallas import tpu as pltpu
from jax.sharding import PartitionSpec as P

MIB = 1 << 20
FULL = pl.BlockSpec(memory_space=pltpu.VMEM)
ANY = pl.BlockSpec(memory_space=pl.ANY)
SCALAR = pl.BlockSpec(memory_space=pltpu.SMEM)
STEPS = 32700.0
TINY = 1e-37
LANES = 128
PAD = 8
PIECES = 4


def call(kernel, outs, ins, specs, name, scratch=(), limit=4, flops=0, moved=0):
    return pl.pallas_call(
        kernel,
        out_shape=outs,
        in_specs=specs,
        out_specs=jax.tree.map(lambda _: FULL, outs),
        scratch_shapes=list(scratch),
        compiler_params=pltpu.CompilerParams(vmem_limit_bytes=limit * MIB),
        cost_estimate=pl.CostEstimate(flops=flops, bytes_accessed=moved, transcendentals=0),
        name=name,
    )(*ins)


def held(shape, dtype):
    return pltpu.VMEM(shape, dtype)


def in_vmem(x):
    return pltpu.with_memory_space_constraint(x, pltpu.VMEM)


def in_hbm(x):
    return pltpu.with_memory_space_constraint(x, pltpu.HBM)


def swap(x, axis, distance):
    count = lax.axis_size(axis)
    return lax.ppermute(x, axis, [(i, i ^ distance) for i in range(count)])


def sent_apart(x, axis):
    count = lax.axis_size(axis)
    if count <= 4:
        return [x] + [swap(x, axis, d) for d in range(1, count)]
    d = 1
    while d < count:
        x = x + swap(x, axis, d)
        d *= 2
    return [x]


def exchange(blocks, axis):
    return [blocks[0]] + [swap(b, axis, d) for d, b in enumerate(blocks) if d]


def gather(x, axis):
    count = lax.axis_size(axis)
    blocks = {0: x}
    d = count // 2
    while d:
        blocks |= {k ^ d: swap(b, axis, d) for k, b in blocks.items()}
        d //= 2
    return [blocks[k] for k in range(count)]


def halving_order(count):
    bits = count.bit_length() - 1
    return [sum(((k >> b) & 1) << (bits - 1 - b) for b in range(bits)) for k in range(count)]


def fetch_kernel(starts, *refs):
    count = len(starts)
    sources, shares, sems = refs[:count], refs[-count - 1 : -1], refs[-1]
    fetches = []
    for k, start in enumerate(starts):
        source, share = sources[k], shares[k]
        if start is not None:
            source = source.at[:, pl.ds(start, share.shape[1])]
        pieces = PIECES if len(share.shape) > 2 or share.shape[0] % (16 * PIECES) == 0 else 1
        step = share.shape[0] // pieces
        for p in range(pieces):
            at = pl.ds(p * step, step)
            fetches.append(pltpu.make_async_copy(source.at[at], share.at[at], sems.at[k, p]))
    for fetch in fetches:
        fetch.start()
    for fetch in fetches:
        fetch.wait()


def fetch(items, after, name):
    shapes = [x.shape if start is None else (x.shape[0], width) for x, start, width in items]
    return call(
        functools.partial(fetch_kernel, [start for _, start, _ in items]),
        [held(shape, x.dtype) for shape, (x, _, _) in zip(shapes, items)],
        (*[in_hbm(x) for x, _, _ in items], *after),
        [ANY] * (len(items) + len(after)),
        name,
        scratch=[pltpu.SemaphoreType.DMA((len(items), PIECES))],
        moved=sum(2 * math.prod(shape) for shape in shapes),
    )


def project_kernel(width_all, count, narrow_count, tile, me_ref, *refs):
    stat_refs = refs[:-11]
    x_ref, gain_ref, w_ref, kv_ref, first_ref, kept_ref, sent_ref, normed, own, rest, sems = refs[-11:]
    rows, width = x_ref.shape
    half = rows // 2
    block = rows // count
    sub_width = width // narrow_count
    done = first_ref.shape[1]
    fetches = [
        pltpu.make_async_copy(
            w_ref.at[:, done + t * tile : done + (t + 1) * tile], rest.at[:, t * tile : (t + 1) * tile], sems.at[t]
        )
        for t in range(rest.shape[1] // tile)
    ]
    for fetch in fetches:
        fetch.start()
    me, narrow = me_ref[0], me_ref[1]
    stats = stat_refs[0][...]
    for ref in stat_refs[1:]:
        stats = stats + ref[...]
    row = lax.broadcasted_iota(jnp.int32, (rows, rows), 0)
    column = lax.broadcasted_iota(jnp.int32, (rows, rows), 1)
    sums = jnp.sum(jnp.where(row == column, stats[0:1, :], 0.0), axis=1, keepdims=True)
    squares = jnp.sum(jnp.where(row == column, stats[1:2, :], 0.0), axis=1, keepdims=True)
    center = sums / width_all
    spread = squares / width_all - center * center
    inverse = lax.rsqrt(spread + 1e-05)
    gain = gain_ref[...].reshape(1, width)
    order = halving_order(count)
    for j in range(count):
        pick = slice(j * block, (j + 1) * block)
        place = jnp.int32(0)
        for k, d in enumerate(order):
            place = jnp.where((me ^ d) == j, k, place)
        place = pl.multiple_of(place * block, 16)
        scaled = (x_ref[pick, :].astype(jnp.float32) - center[pick]) * inverse[pick] * gain
        normed[pl.ds(place, block), :] = scaled.astype(jnp.bfloat16)
    for j in range(narrow_count):
        @pl.when(narrow == j)
        def _(j=j):
            own[...] = normed[:, j * sub_width : (j + 1) * sub_width]

    def put(got, at):
        kept_ref[:, at] = got[:half, :]
        sent_ref[:, at] = got[half:, :]

    def products(source, t, start):
        at = pl.ds(pl.multiple_of(t * tile, tile), tile)
        got = jnp.dot(normed[...], source[:, at], preferred_element_type=jnp.float32)
        put(got, pl.ds(pl.multiple_of(start + t * tile, tile), tile))

    put(jnp.dot(own[...], kv_ref[...], preferred_element_type=jnp.float32), slice(w_ref.shape[1], kept_ref.shape[1]))

    @pl.loop(0, done // tile)
    def _(t):
        products(first_ref, t, 0)

    for t, fetch in enumerate(fetches):
        fetch.wait()
        products(rest, t, done)


def project(me, stats, x, gain, w, kv, first, width_all, count, narrow_count, tile):
    rows, width = x.shape
    queries = w.shape[1]
    rest = queries - first.shape[1]
    half = jax.ShapeDtypeStruct((rows // 2, queries + kv.shape[1]), jnp.float32)
    return call(
        functools.partial(project_kernel, width_all, count, narrow_count, tile),
        (half, half),
        (me, *stats, x, gain, in_hbm(w), in_vmem(kv), in_vmem(first)),
        [SCALAR] + [FULL] * (len(stats) + 2) + [ANY] + [FULL] * 2,
        "project",
        scratch=[
            pltpu.VMEM((rows, width), jnp.bfloat16),
            pltpu.VMEM((rows, width // narrow_count), jnp.bfloat16),
            pltpu.VMEM((width, rest), jnp.bfloat16),
            pltpu.SemaphoreType.DMA((rest // tile,)),
        ],
        limit=30,
        flops=2 * rows * width * queries,
        moved=2 * width * rest,
    )


def fold_kernel(guards, kept_ref, came_ref, *refs):
    still_ref, sent_ref = refs[guards:]
    half = still_ref.shape[0]
    still_ref[...] = kept_ref[:half, :] + came_ref[:half, :]
    sent_ref[...] = kept_ref[half:, :] + came_ref[half:, :]


def fold(kept, came, guards):
    half = jax.ShapeDtypeStruct((kept.shape[0] // 2, kept.shape[1]), jnp.float32)
    return call(
        functools.partial(fold_kernel, len(guards)),
        (half, half),
        (kept, came, *map(in_vmem, guards)),
        [FULL] * (2 + len(guards)),
        "fold",
        moved=16 * kept.size,
    )


def split_kernel(queries, guards, me_ref, kept_ref, came_ref, *refs):
    out_refs = refs[guards:]
    count, rows = len(out_refs), out_refs[0].shape[0]
    narrow = me_ref[1]
    total = kept_ref[...] + came_ref[...]
    parts = [total[j * rows : (j + 1) * rows, :] for j in range(count)]
    for d, out_ref in enumerate(out_refs):
        mine = parts[0]
        for j in range(1, count):
            mine = jnp.where((narrow ^ d) == j, parts[j], mine)
        out_ref[:, :queries] = mine[:, :queries].astype(jnp.bfloat16)
        left = mine[:, queries:]
        width = left.shape[1]
        for term in range(2):
            high = left.astype(jnp.bfloat16)
            out_ref[:, queries + term * width : queries + (term + 1) * width] = high
            left = left - high.astype(jnp.float32)


def attend_kernel(head_dim, guards, lengths_ref, *refs):
    count = (len(refs) - guards - 3) // 2
    came_refs, kv_ref = refs[:count], refs[count]
    out_refs, heads, contexts = refs[count + 1 + guards : -2], refs[-2], refs[-1]
    rows, positions = kv_ref.shape[0], kv_ref.shape[1]
    queries = out_refs[0].shape[1]
    each = queries // head_dim
    total_heads = each * count
    slabs = head_dim // LANES
    scaling = 1.0 / math.sqrt(head_dim)
    for d, ref in enumerate(came_refs):
        for h in range(each):
            at = (d * each + h) * PAD
            for k in range(slabs):
                start = h * head_dim + k * LANES
                heads[k, at : at + rows, :] = ref[:, start : start + LANES].astype(jnp.float32)
    terms = came_refs[0][:, queries:].astype(jnp.float32)
    for ref in came_refs[1:]:
        terms = terms + ref[:, queries:].astype(jnp.float32)
    pair = 2 * head_dim
    fresh = terms[:, :pair] + terms[:, pair:]
    fresh = fresh.astype(jnp.bfloat16).astype(jnp.float32)
    place = lax.broadcasted_iota(jnp.int32, (total_heads, positions), 1)
    for r in range(rows):
        query = jnp.concatenate([heads[k, pl.ds(r, total_heads, stride=PAD), :] for k in range(slabs)], axis=1)
        scores = (
            lax.dot_general(
                query.astype(jnp.bfloat16),
                kv_ref[r, :, :head_dim],
                (((1,), (1,)), ((), ())),
                preferred_element_type=jnp.float32,
            )
            * scaling
        )
        own_score = jnp.sum(query * fresh[r : r + 1, :head_dim], axis=1, keepdims=True) * scaling
        valid = place < lengths_ref[r]
        top = jnp.maximum(jnp.max(jnp.where(valid, scores, -jnp.inf), axis=1, keepdims=True), own_score)
        weights = jnp.where(valid, jnp.exp(scores - top), 0.0)
        own_weight = jnp.exp(own_score - top)
        total = jnp.sum(weights, axis=1, keepdims=True) + own_weight
        numer = jnp.dot(weights.astype(jnp.bfloat16), kv_ref[r, :, head_dim:], preferred_element_type=jnp.float32)
        numer = numer + own_weight.astype(jnp.bfloat16).astype(jnp.float32) * fresh[r : r + 1, head_dim:]
        context = numer / total
        for k in range(slabs):
            contexts[k, pl.ds(r, total_heads, stride=PAD), :] = context[:, k * LANES : (k + 1) * LANES]
    for d, ref in enumerate(out_refs):
        for h in range(each):
            at = (d * each + h) * PAD
            for k in range(slabs):
                start = h * head_dim + k * LANES
                ref[:, start : start + LANES] = contexts[k, at : at + rows, :].astype(jnp.bfloat16)


def attend(lengths, came, kv, head_dim, queries, guards):
    rows = kv.shape[0]
    count = len(came)
    all_heads = count * queries // head_dim
    scratch = pltpu.VMEM((head_dim // LANES, all_heads * PAD, LANES), jnp.float32)
    return call(
        functools.partial(attend_kernel, head_dim, len(guards)),
        [jax.ShapeDtypeStruct((rows, queries), jnp.bfloat16)] * count,
        (lengths, *came, in_vmem(kv), *map(in_vmem, guards)),
        [SCALAR] + [FULL] * (count + 1 + len(guards)),
        "attend",
        scratch=[scratch, scratch],
        limit=8,
        flops=4 * rows * count * queries * kv.shape[1],
    )


def join_kernel(guards, me_ref, *refs):
    count = len(refs) - guards - 2
    out_ref, joined = refs[-2:]
    rows = refs[0].shape[0]
    for d in range(count):
        at = pl.ds(pl.multiple_of((me_ref[1] ^ d) * PAD, PAD), rows)
        joined[at, :] = refs[d][...].astype(jnp.float32)
    came = [joined[j * PAD : j * PAD + rows, :] for j in range(count)]
    out_ref[...] = jnp.concatenate(came, axis=0).astype(jnp.bfloat16)


def arrange_kernel(narrow_count, guards, me_ref, *refs):
    count = len(refs) - guards - 1
    out_ref = refs[-1]
    block = refs[0].shape[0]
    ratio = count // narrow_count
    for d in range(count):
        block_of = me_ref[0] ^ d
        apart = (block_of // ratio) ^ me_ref[1]
        place = jnp.int32(0)
        for k, distance in enumerate(halving_order(narrow_count)):
            place = jnp.where(apart == distance, k, place)
        place = place * ratio + block_of % ratio
        out_ref[pl.ds(pl.multiple_of(place * block, 16), block), :] = refs[d][...]


def code(x, ref):
    largest = jnp.maximum(jnp.max(jnp.abs(x), axis=1, keepdims=True), TINY)
    power = jnp.floor(jnp.log2(largest)) + 1.0
    steps = jnp.round(x * (STEPS * jnp.exp2(-power)))
    ref[:, : x.shape[1]] = steps.astype(jnp.int32).astype(jnp.int16)
    ref[:, x.shape[1] :] = jnp.broadcast_to(power, (x.shape[0], LANES)).astype(jnp.int32).astype(jnp.int16)


def decode(ref, width):
    power = ref[:, width:].astype(jnp.int32).astype(jnp.float32)[:, 0:1]
    return ref[:, :width].astype(jnp.int32).astype(jnp.float32) * (jnp.exp2(power) * (1.0 / STEPS))


def output_kernel(tile, x_ref, w_ref, *refs):
    kept_ref, sent_ref, product = refs[-3:]
    half = kept_ref.shape[0]

    @pl.loop(0, w_ref.shape[1] // tile)
    def _(t):
        at = pl.ds(pl.multiple_of(t * tile, tile), tile)
        product[:, at] = jnp.dot(x_ref[...], w_ref[:, at], preferred_element_type=jnp.float32)

    kept_ref[...] = product[:half, :]
    code(product[half:, :], sent_ref)


def output_part(x, w, after):
    rows, columns = x.shape[0], w.shape[1]
    return call(
        functools.partial(output_kernel, 256 if columns % 256 == 0 else LANES),
        (
            jax.ShapeDtypeStruct((rows // 2, columns), jnp.float32),
            jax.ShapeDtypeStruct((rows // 2, columns + LANES), jnp.int16),
        ),
        (x, in_vmem(w), *after),
        [FULL, FULL] + [ANY] * len(after),
        "output_part",
        scratch=[pltpu.VMEM((rows, columns), jnp.float32)],
        limit=6,
        flops=2 * rows * w.size,
        moved=2 * x.size,
    )


def halve_kernel(kept_ref, came_ref, *refs):
    still_ref, sent_ref = refs[-2:]
    half = still_ref.shape[0]
    total = kept_ref[...] + decode(came_ref, kept_ref.shape[1])
    still_ref[...] = total[:half, :]
    code(total[half:, :], sent_ref)


def halve(kept, came, after):
    rows, columns = kept.shape
    return call(
        halve_kernel,
        (
            jax.ShapeDtypeStruct((rows // 2, columns), jnp.float32),
            jax.ShapeDtypeStruct((rows // 2, columns + LANES), jnp.int16),
        ),
        (kept, came, *after),
        [FULL, FULL] + [ANY] * len(after),
        "halve",
        moved=16 * kept.size,
    )


def finish_kernel(kinds, *refs):
    out_ref = refs[-1]
    at = k = 0
    for kind in kinds:
        width = refs[k].shape[1]
        done = refs[k][...]
        if kind == 2:
            done = (done + decode(refs[k + 1], width)).astype(jnp.bfloat16)
        out_ref[:, at : at + width] = done
        at += width
        k += kind


def finish(cuts, after=()):
    parts = [x for cut in cuts for x in cut]
    rows, columns = parts[0].shape[0], sum(cut[0].shape[1] for cut in cuts)
    return call(
        functools.partial(finish_kernel, [len(cut) for cut in cuts]),
        jax.ShapeDtypeStruct((rows, columns), jnp.bfloat16),
        (*parts, *after),
        [FULL] * len(parts) + [ANY] * len(after),
        "finish",
        moved=8 * columns * rows,
    )


def cut_widths(columns):
    tile = 256 if columns % 256 == 0 else LANES
    tiles = columns // tile
    outer = tiles // 4
    inner = (tiles - 2 * outer + 1) // 2
    return [tile * n for n in (outer, inner, tiles - 2 * outer - inner, outer)]


def local(activations, norm_gain, query_weight, kv_weight, out_weight, kv_cache, lengths):
    wide_count = lax.axis_size("wide")
    narrow_count = lax.axis_size("narrow")
    me = jnp.stack([lax.axis_index("wide"), lax.axis_index("narrow")]).astype(jnp.int32)
    own_rows, head_dim = kv_cache.shape[0], kv_cache.shape[2] // 2
    rows, width = activations.shape
    queries = query_weight.shape[1]
    columns = out_weight.shape[1]
    tile = 256
    values = activations.astype(jnp.float32)
    stats = jnp.stack([jnp.sum(values, axis=1), jnp.sum(values * values, axis=1)])
    first_part, kv_part = fetch(
        [(query_weight, 0, queries // tile // 3 * tile), (kv_weight, None, None)], [stats, me], "fetch_query_weight"
    )
    kept, sent = project(
        me,
        sent_apart(stats, "wide"),
        activations,
        norm_gain,
        query_weight,
        kv_part,
        first_part,
        width * wide_count,
        wide_count,
        narrow_count,
        tile,
    )
    widths = cut_widths(columns)
    cuts = [(out_weight, sum(widths[:k]), w) for k, w in enumerate(widths)]
    d = 1
    while 2 * d < wide_count:
        kept, sent = fold(kept, swap(sent, "wide", d), [])
        d *= 2
    out_parts = [None] * 4
    out_parts[0], cache = fetch([cuts[0], (kv_cache, None, None)], [sent], "fetch_out_weight_0")
    split = call(
        functools.partial(split_kernel, queries, 1),
        [jax.ShapeDtypeStruct((own_rows, queries + 4 * head_dim), jnp.bfloat16)] * narrow_count,
        (me, kept, swap(sent, "wide", d), in_vmem(out_parts[0])),
        [SCALAR] + [FULL] * 3,
        "split",
        moved=16 * kept.size,
    )
    [out_parts[1]] = fetch([cuts[1]], [split[0]], "fetch_out_weight_1")
    context = attend(lengths, exchange(split, "narrow"), cache, head_dim, queries, [out_parts[1]])
    [out_parts[2]] = fetch([cuts[2]], [context[0]], "fetch_out_weight_2")
    returned = call(
        functools.partial(join_kernel, 1),
        jax.ShapeDtypeStruct((narrow_count * own_rows, queries), jnp.bfloat16),
        (me, *exchange(context, "narrow"), in_vmem(out_parts[2])),
        [SCALAR] + [FULL] * (narrow_count + 1),
        "join",
        scratch=[pltpu.VMEM((narrow_count * PAD, queries), jnp.float32)],
        moved=4 * narrow_count * own_rows * queries,
    )
    [out_parts[3]] = fetch([cuts[3]], [returned], "fetch_out_weight_3")
    arranged = call(
        functools.partial(arrange_kernel, narrow_count, 1),
        jax.ShapeDtypeStruct((rows, queries), jnp.bfloat16),
        (me, *gather(returned, "wide"), in_vmem(out_parts[3])),
        [SCALAR] + [FULL] * (wide_count + 1),
        "arrange",
        moved=4 * rows * queries,
    )
    kepts, sents, halved, summed = [], [], [], []

    def exchange_cut(k, after):
        kept, sent, d = kepts[k], sents[k], 1
        while 2 * d < narrow_count:
            kept, sent = halve(kept, swap(sent, "narrow", d), after)
            after = []
            d *= 2
        halved.append(kept)
        summed.append((kept, swap(sent, "narrow", d)))

    def finish_cut(k, after):
        summed[k] = (finish([summed[k]], after),)
        return [summed[k][0]]

    for k, part in enumerate(out_parts):
        kept, sent = output_part(arranged, part, halved[-1:])
        kepts.append(kept)
        sents.append(sent)
        after = [kept]
        if k > 2:
            after = after + finish_cut(k - 3, [kept])
        if k:
            exchange_cut(k - 1, after)
    exchange_cut(len(out_parts) - 1, finish_cut(len(out_parts) - 3, []))
    return finish(summed)


def solution(mesh):
    return jax.shard_map(
        local,
        mesh=mesh,
        in_specs=(
            P("groups", "wide"),
            P("wide"),
            P("wide", "narrow"),
            P(("wide", "narrow"), None),
            P("narrow", "wide"),
            P(("groups", "wide", "narrow"), None, None),
            P(("groups", "wide", "narrow")),
        ),
        out_specs=P(("groups", "narrow"), "wide"),
        check_vma=False,
    )
```

```python
import functools
import math

import jax
import jax.numpy as jnp
from jax import lax
from jax.experimental import pallas as pl
from jax.experimental.pallas import tpu as pltpu
from jax.sharding import PartitionSpec as P

MIB = 1 << 20
FULL = pl.BlockSpec(memory_space=pltpu.VMEM)
ANY = pl.BlockSpec(memory_space=pl.ANY)
SCALAR = pl.BlockSpec(memory_space=pltpu.SMEM)
STEPS = 32700.0
TINY = 1e-37
LANES = 128
PAD = 8
PIECES = 4


def call(kernel, outs, ins, specs, name, scratch=(), limit=4, flops=0, moved=0):
    return pl.pallas_call(
        kernel,
        out_shape=outs,
        in_specs=specs,
        out_specs=jax.tree.map(lambda _: FULL, outs),
        scratch_shapes=list(scratch),
        compiler_params=pltpu.CompilerParams(vmem_limit_bytes=limit * MIB),
        cost_estimate=pl.CostEstimate(flops=flops, bytes_accessed=moved, transcendentals=0),
        name=name,
    )(*ins)


def held(shape, dtype):
    return pltpu.VMEM(shape, dtype)


def in_vmem(x):
    return pltpu.with_memory_space_constraint(x, pltpu.VMEM)


def in_hbm(x):
    return pltpu.with_memory_space_constraint(x, pltpu.HBM)


def swap(x, axis, distance):
    count = lax.axis_size(axis)
    return lax.ppermute(x, axis, [(i, i ^ distance) for i in range(count)])


def sent_apart(x, axis):
    count = lax.axis_size(axis)
    if count <= 4:
        return [x] + [swap(x, axis, d) for d in range(1, count)]
    d = 1
    while d < count:
        x = x + swap(x, axis, d)
        d *= 2
    return [x]


def exchange(blocks, axis):
    return [blocks[0]] + [swap(b, axis, d) for d, b in enumerate(blocks) if d]


def gather(x, axis):
    count = lax.axis_size(axis)
    blocks = {0: x}
    d = count // 2
    while d:
        blocks |= {k ^ d: swap(b, axis, d) for k, b in blocks.items()}
        d //= 2
    return [blocks[k] for k in range(count)]


def halving_order(count):
    bits = count.bit_length() - 1
    return [sum(((k >> b) & 1) << (bits - 1 - b) for b in range(bits)) for k in range(count)]


def fetches_of(starts, sources, shares, sems):
    fetches = []
    for k, start in enumerate(starts):
        source, share = sources[k], shares[k]
        if start is not None:
            source = source.at[:, pl.ds(start, share.shape[1])]
        pieces = PIECES if len(share.shape) > 2 or share.shape[0] % (16 * PIECES) == 0 else 1
        step = share.shape[0] // pieces
        for p in range(pieces):
            at = pl.ds(p * step, step)
            fetches.append(pltpu.make_async_copy(source.at[at], share.at[at], sems.at[k, p]))
    return fetches


def fetch_kernel(starts, *refs):
    count = len(starts)
    fetches = fetches_of(starts, refs[:count], refs[-count - 1 : -1], refs[-1])
    for fetch in fetches:
        fetch.start()
    for fetch in fetches:
        fetch.wait()


def fetch(items, after, name):
    shapes = [x.shape if start is None else (x.shape[0], width) for x, start, width in items]
    return call(
        functools.partial(fetch_kernel, [start for _, start, _ in items]),
        [held(shape, x.dtype) for shape, (x, _, _) in zip(shapes, items)],
        (*[in_hbm(x) for x, _, _ in items], *after),
        [ANY] * (len(items) + len(after)),
        name,
        scratch=[pltpu.SemaphoreType.DMA((len(items), PIECES))],
        moved=sum(2 * math.prod(shape) for shape in shapes),
    )


def project_kernel(many, width_all, count, narrow_count, tile, me_ref, *refs):
    stat_refs, refs = refs[:many], refs[many:]
    x_ref, gain_ref, w_ref, kv_ref, first_ref, kept_ref, sent_ref, normed, own, *groups, sems = refs
    rows, width = x_ref.shape
    half = rows // 2
    block = rows // count
    sub_width = width // narrow_count
    done = first_ref.shape[1]
    starts = [done + sum(ref.shape[1] for ref in groups[:g]) for g in range(len(groups))]
    fetches = [fetches_of([start], [w_ref], [ref], sems.at[pl.ds(g, 1)]) for g, (start, ref) in enumerate(zip(starts, groups))]
    for fetch in fetches:
        for piece in fetch:
            piece.start()
    me, narrow = me_ref[0], me_ref[1]
    stats = stat_refs[0][...]
    for ref in stat_refs[1:]:
        stats = stats + ref[...]
    row = lax.broadcasted_iota(jnp.int32, (rows, rows), 0)
    column = lax.broadcasted_iota(jnp.int32, (rows, rows), 1)
    sums = jnp.sum(jnp.where(row == column, stats[0:1, :], 0.0), axis=1, keepdims=True)
    squares = jnp.sum(jnp.where(row == column, stats[1:2, :], 0.0), axis=1, keepdims=True)
    center = sums / width_all
    spread = squares / width_all - center * center
    inverse = lax.rsqrt(spread + 1e-05)
    gain = gain_ref[...].reshape(1, width)
    order = halving_order(count)
    for j in range(count):
        pick = slice(j * block, (j + 1) * block)
        place = jnp.int32(0)
        for k, d in enumerate(order):
            place = jnp.where((me ^ d) == j, k, place)
        place = pl.multiple_of(place * block, 16)
        scaled = (x_ref[pick, :].astype(jnp.float32) - center[pick]) * inverse[pick] * gain
        normed[pl.ds(place, block), :] = scaled.astype(jnp.bfloat16)
    for j in range(narrow_count):
        @pl.when(narrow == j)
        def _(j=j):
            own[...] = normed[:, j * sub_width : (j + 1) * sub_width]

    def put(got, at):
        kept_ref[:, at] = got[:half, :]
        sent_ref[:, at] = got[half:, :]

    def products(source, start):
        @pl.loop(0, source.shape[1] // tile)
        def _(t):
            at = pl.ds(pl.multiple_of(t * tile, tile), tile)
            got = jnp.dot(normed[...], source[:, at], preferred_element_type=jnp.float32)
            put(got, pl.ds(pl.multiple_of(start + t * tile, tile), tile))

    put(jnp.dot(own[...], kv_ref[...], preferred_element_type=jnp.float32), slice(w_ref.shape[1], kept_ref.shape[1]))
    products(first_ref, 0)
    for start, fetch, ref in zip(starts, fetches, groups):
        for piece in fetch:
            piece.wait()
        products(ref, start)


def project(me, stats, x, gain, w, kv, first, width_all, count, narrow_count, tile):
    rows, width = x.shape
    queries = w.shape[1]
    tiles = (queries - first.shape[1]) // tile
    groups = [tiles * 4 // 9, (tiles - tiles * 4 // 9 + 1) // 2]
    groups.append(tiles - sum(groups))
    half = jax.ShapeDtypeStruct((rows // 2, queries + kv.shape[1]), jnp.float32)
    return call(
        functools.partial(project_kernel, len(stats), width_all, count, narrow_count, tile),
        (half, half),
        (me, *stats, x, gain, in_hbm(w), in_vmem(kv), in_vmem(first)),
        [SCALAR] + [FULL] * (len(stats) + 2) + [ANY] + [FULL] * 2,
        "project",
        scratch=[
            pltpu.VMEM((rows, width), jnp.bfloat16),
            pltpu.VMEM((rows, width // narrow_count), jnp.bfloat16),
            *[pltpu.VMEM((width, n * tile), jnp.bfloat16) for n in groups],
            pltpu.SemaphoreType.DMA((len(groups), PIECES)),
        ],
        limit=30,
        flops=2 * rows * width * queries,
        moved=2 * width * tiles * tile,
    )


def fold_kernel(guards, kept_ref, came_ref, *refs):
    still_ref, sent_ref = refs[guards:]
    half = still_ref.shape[0]
    still_ref[...] = kept_ref[:half, :] + came_ref[:half, :]
    sent_ref[...] = kept_ref[half:, :] + came_ref[half:, :]


def fold(kept, came, guards):
    half = jax.ShapeDtypeStruct((kept.shape[0] // 2, kept.shape[1]), jnp.float32)
    return call(
        functools.partial(fold_kernel, len(guards)),
        (half, half),
        (kept, came, *map(in_vmem, guards)),
        [FULL] * (2 + len(guards)),
        "fold",
        moved=16 * kept.size,
    )


def split_kernel(queries, guards, me_ref, kept_ref, came_ref, *refs):
    out_refs, slots = refs[guards:-1], refs[-1]
    count, rows = len(out_refs), out_refs[0].shape[0]
    narrow = me_ref[1]
    total = kept_ref[...] + came_ref[...]
    for j in range(count):
        slots[j * PAD : j * PAD + rows, :] = total[j * rows : (j + 1) * rows, :]
    for d, out_ref in enumerate(out_refs):
        mine = slots[pl.ds(pl.multiple_of((narrow ^ d) * PAD, PAD), rows), :]
        high = mine.astype(jnp.bfloat16)
        out_ref[:, : mine.shape[1]] = high
        out_ref[:, mine.shape[1] :] = (mine - high.astype(jnp.float32))[:, queries:].astype(jnp.bfloat16)


def attend_kernel(head_dim, count, guards, start, lengths_ref, *refs):
    came_refs, kv_ref, w_ref = refs[:count], refs[count], refs[count + 1]
    refs = refs[count + 2 + guards :]
    out_refs, share, (heads, contexts, sems) = refs[:count], refs[count], refs[count + 1 :]
    fetches = fetches_of([start], [w_ref], [share], sems)
    for fetch in fetches:
        fetch.start()
    rows, positions = kv_ref.shape[0], kv_ref.shape[1]
    queries = out_refs[0].shape[1]
    each = queries // head_dim
    total_heads = each * count
    slabs = head_dim // LANES
    scaling = 1.0 / math.sqrt(head_dim)
    for d, ref in enumerate(came_refs):
        for h in range(each):
            at = (d * each + h) * PAD
            for k in range(slabs):
                start = h * head_dim + k * LANES
                heads[k, at : at + rows, :] = ref[:, start : start + LANES].astype(jnp.float32)
    terms = came_refs[0][:, queries:].astype(jnp.float32)
    for ref in came_refs[1:]:
        terms = terms + ref[:, queries:].astype(jnp.float32)
    pair = 2 * head_dim
    fresh = terms[:, :pair] + terms[:, pair:]
    fresh = fresh.astype(jnp.bfloat16).astype(jnp.float32)
    place = lax.broadcasted_iota(jnp.int32, (total_heads, positions), 1)
    for r in range(rows):
        query = jnp.concatenate([heads[k, pl.ds(r, total_heads, stride=PAD), :] for k in range(slabs)], axis=1)
        scores = (
            lax.dot_general(
                query.astype(jnp.bfloat16),
                kv_ref[r, :, :head_dim],
                (((1,), (1,)), ((), ())),
                preferred_element_type=jnp.float32,
            )
            * scaling
        )
        own_score = jnp.sum(query * fresh[r : r + 1, :head_dim], axis=1, keepdims=True) * scaling
        valid = place < lengths_ref[r]
        top = jnp.maximum(jnp.max(jnp.where(valid, scores, -jnp.inf), axis=1, keepdims=True), own_score)
        weights = jnp.where(valid, jnp.exp(scores - top), 0.0)
        own_weight = jnp.exp(own_score - top)
        total = jnp.sum(weights, axis=1, keepdims=True) + own_weight
        numer = jnp.dot(weights.astype(jnp.bfloat16), kv_ref[r, :, head_dim:], preferred_element_type=jnp.float32)
        numer = numer + own_weight.astype(jnp.bfloat16).astype(jnp.float32) * fresh[r : r + 1, head_dim:]
        context = numer / total
        for k in range(slabs):
            contexts[k, pl.ds(r, total_heads, stride=PAD), :] = context[:, k * LANES : (k + 1) * LANES]
    for d, ref in enumerate(out_refs):
        for h in range(each):
            at = (d * each + h) * PAD
            for k in range(slabs):
                start = h * head_dim + k * LANES
                ref[:, start : start + LANES] = contexts[k, at : at + rows, :].astype(jnp.bfloat16)
    for fetch in fetches:
        fetch.wait()


def attend(lengths, came, kv, cut, head_dim, queries, guards):
    rows = kv.shape[0]
    count = len(came)
    all_heads = count * queries // head_dim
    scratch = pltpu.VMEM((head_dim // LANES, all_heads * PAD, LANES), jnp.float32)
    w, start, width = cut
    return call(
        functools.partial(attend_kernel, head_dim, count, len(guards), start),
        [jax.ShapeDtypeStruct((rows, queries), jnp.bfloat16)] * count + [held((w.shape[0], width), w.dtype)],
        (lengths, *came, in_vmem(kv), in_hbm(w), *map(in_vmem, guards)),
        [SCALAR] + [FULL] * (count + 1) + [ANY] + [FULL] * len(guards),
        "attend",
        scratch=[scratch, scratch, pltpu.SemaphoreType.DMA((1, PIECES))],
        limit=8,
        flops=4 * rows * count * queries * kv.shape[1],
    )


def join_kernel(guards, me_ref, *refs):
    count = len(refs) - guards - 2
    out_ref, joined = refs[-2:]
    rows = refs[0].shape[0]
    for d in range(count):
        at = pl.ds(pl.multiple_of((me_ref[1] ^ d) * PAD, PAD), rows)
        joined[at, :] = refs[d][...].astype(jnp.float32)
    came = [joined[j * PAD : j * PAD + rows, :] for j in range(count)]
    out_ref[...] = jnp.concatenate(came, axis=0).astype(jnp.bfloat16)


def code(x, ref):
    largest = jnp.maximum(jnp.max(jnp.abs(x), axis=1, keepdims=True), TINY)
    power = jnp.floor(jnp.log2(largest)) + 1.0
    steps = jnp.round(x * (STEPS * jnp.exp2(-power)))
    ref[:, : x.shape[1]] = steps.astype(jnp.int32).astype(jnp.int16)
    ref[:, x.shape[1] :] = jnp.broadcast_to(power, (x.shape[0], LANES)).astype(jnp.int32).astype(jnp.int16)


def decode(ref, width):
    power = ref[:, width:].astype(jnp.int32).astype(jnp.float32)[:, 0:1]
    return ref[:, :width].astype(jnp.int32).astype(jnp.float32) * (jnp.exp2(power) * (1.0 / STEPS))


def output_kernel(count, narrow_count, tile, me_ref, *refs):
    x_refs, w_ref = refs[:count], refs[count]
    kept_ref, sent_ref, x, product = refs[-4:]
    block = x_refs[0].shape[0]
    ratio = count // narrow_count
    for d, ref in enumerate(x_refs):
        x[d * block : (d + 1) * block, :] = ref[...]

    @pl.loop(0, w_ref.shape[1] // tile)
    def _(t):
        at = pl.ds(pl.multiple_of(t * tile, tile), tile)
        product[:, at] = jnp.dot(x[...], w_ref[:, at], preferred_element_type=jnp.float32)

    parts = []
    for distance in halving_order(narrow_count):
        for k in range(ratio):
            wide = (me_ref[1] ^ distance) * ratio + k
            parts.append(product[pl.ds(pl.multiple_of((wide ^ me_ref[0]) * block, block), block), :])
    half = count // 2
    for k, part in enumerate(parts[:half]):
        kept_ref[k * block : (k + 1) * block, :] = part
    code(jnp.concatenate(parts[half:], axis=0), sent_ref)


def output_part(me, blocks, w, narrow_count, after):
    count = len(blocks)
    block, depth = blocks[0].shape
    rows, columns = count * block, w.shape[1]
    return call(
        functools.partial(output_kernel, count, narrow_count, 256 if columns % 256 == 0 else LANES),
        (
            jax.ShapeDtypeStruct((rows // 2, columns), jnp.float32),
            jax.ShapeDtypeStruct((rows // 2, columns + LANES), jnp.int16),
        ),
        (me, *blocks, in_vmem(w), *after),
        [SCALAR] + [FULL] * (count + 1) + [ANY] * len(after),
        "output_part",
        scratch=[pltpu.VMEM((rows, depth), jnp.bfloat16), pltpu.VMEM((rows, columns), jnp.float32)],
        limit=6,
        flops=2 * rows * w.size,
        moved=2 * rows * depth,
    )


def halve_kernel(kept_ref, came_ref, *refs):
    still_ref, sent_ref = refs[-2:]
    half = still_ref.shape[0]
    total = kept_ref[...] + decode(came_ref, kept_ref.shape[1])
    still_ref[...] = total[:half, :]
    code(total[half:, :], sent_ref)


def halve(kept, came, after):
    rows, columns = kept.shape
    return call(
        halve_kernel,
        (
            jax.ShapeDtypeStruct((rows // 2, columns), jnp.float32),
            jax.ShapeDtypeStruct((rows // 2, columns + LANES), jnp.int16),
        ),
        (kept, came, *after),
        [FULL, FULL] + [ANY] * len(after),
        "halve",
        moved=16 * kept.size,
    )


def finish_kernel(*refs):
    out_ref = refs[-1]
    at = 0
    for kept_ref, came_ref in zip(refs[:-1:2], refs[1:-1:2]):
        width = kept_ref.shape[1]
        out_ref[:, at : at + width] = (kept_ref[...] + decode(came_ref, width)).astype(jnp.bfloat16)
        at += width


def finish(cuts):
    parts = [x for cut in cuts for x in cut]
    rows, columns = parts[0].shape[0], sum(cut[0].shape[1] for cut in cuts)
    return call(
        finish_kernel,
        jax.ShapeDtypeStruct((rows, columns), jnp.bfloat16),
        parts,
        [FULL] * len(parts),
        "finish",
        moved=8 * columns * rows,
    )


def local(activations, norm_gain, query_weight, kv_weight, out_weight, kv_cache, lengths):
    wide_count = lax.axis_size("wide")
    narrow_count = lax.axis_size("narrow")
    me = jnp.stack([lax.axis_index("wide"), lax.axis_index("narrow")]).astype(jnp.int32)
    own_rows, head_dim = kv_cache.shape[0], kv_cache.shape[2] // 2
    rows, width = activations.shape
    queries = query_weight.shape[1]
    columns = out_weight.shape[1]
    tile = 256
    values = activations.astype(jnp.float32)
    stats = jnp.stack([jnp.sum(values, axis=1), jnp.sum(values * values, axis=1)])
    first_part, kv_part = fetch(
        [(query_weight, 0, queries // tile // 4 * tile), (kv_weight, None, None)], [stats, me], "fetch_query_weight"
    )
    kept, sent = project(
        me,
        sent_apart(stats, "wide"),
        activations,
        norm_gain,
        query_weight,
        kv_part,
        first_part,
        width * wide_count,
        wide_count,
        narrow_count,
        tile,
    )
    cut = columns // 3
    cuts = [(out_weight, k * cut, cut) for k in range(3)]
    d = 1
    while 2 * d < wide_count:
        kept, sent = fold(kept, swap(sent, "wide", d), [])
        d *= 2
    out_parts = [None] * 3
    out_parts[0], cache = fetch([cuts[0], (kv_cache, None, None)], [sent], "fetch_out_weight_0")
    split = call(
        functools.partial(split_kernel, queries, 1),
        [jax.ShapeDtypeStruct((own_rows, queries + 4 * head_dim), jnp.bfloat16)] * narrow_count,
        (me, kept, swap(sent, "wide", d), in_vmem(out_parts[0])),
        [SCALAR] + [FULL] * 3,
        "split",
        scratch=[pltpu.VMEM((narrow_count * PAD, queries + 2 * head_dim), jnp.float32)],
        moved=16 * kept.size,
    )
    [out_parts[1]] = fetch([cuts[1]], [split[0]], "fetch_out_weight_1")
    *context, out_parts[2] = attend(
        lengths, exchange(split, "narrow"), cache, cuts[2], head_dim, queries, [out_parts[1]]
    )
    returned = call(
        functools.partial(join_kernel, 0),
        jax.ShapeDtypeStruct((narrow_count * own_rows, queries), jnp.bfloat16),
        (me, *exchange(context, "narrow")),
        [SCALAR] + [FULL] * narrow_count,
        "join",
        scratch=[pltpu.VMEM((narrow_count * PAD, queries), jnp.float32)],
        moved=4 * narrow_count * own_rows * queries,
    )
    gathered = gather(returned, "wide")
    cut_sums, halved, last = [], [], []

    def exchange_cut(kept, sent, after):
        d = 1
        while 2 * d < narrow_count:
            kept, sent = halve(kept, swap(sent, "narrow", d), after)
            after = []
            d *= 2
        halved.append(kept)
        cut_sums.append((kept, swap(sent, "narrow", d)))

    for part in out_parts:
        kept, sent = output_part(me, gathered, part, narrow_count, halved[-1:])
        if last:
            exchange_cut(*last, [kept])
        last = (kept, sent)
    exchange_cut(*last, [])
    return finish(cut_sums)


def solution(mesh):
    return jax.shard_map(
        local,
        mesh=mesh,
        in_specs=(
            P("groups", "wide"),
            P("wide"),
            P("wide", "narrow"),
            P(("wide", "narrow"), None),
            P("narrow", "wide"),
            P(("groups", "wide", "narrow"), None, None),
            P(("groups", "wide", "narrow")),
        ),
        out_specs=P(("groups", "narrow"), "wide"),
        check_vma=False,
    )
```

```python
import functools
import math

import jax
import jax.numpy as jnp
from jax import lax
from jax.experimental import pallas as pl
from jax.experimental.pallas import tpu as pltpu
from jax.sharding import PartitionSpec as P

MIB = 1 << 20
FULL = pl.BlockSpec(memory_space=pltpu.VMEM)
ANY = pl.BlockSpec(memory_space=pl.ANY)
SCALAR = pl.BlockSpec(memory_space=pltpu.SMEM)
STEPS = 32700.0
TINY = 1e-37
LANES = 128
PAD = 8
PIECES = 4


def call(kernel, outs, ins, specs, name, scratch=(), limit=4, flops=0, moved=0):
    return pl.pallas_call(
        kernel,
        out_shape=outs,
        in_specs=specs,
        out_specs=jax.tree.map(lambda _: FULL, outs),
        scratch_shapes=list(scratch),
        compiler_params=pltpu.CompilerParams(vmem_limit_bytes=limit * MIB),
        cost_estimate=pl.CostEstimate(flops=flops, bytes_accessed=moved, transcendentals=0),
        name=name,
    )(*ins)


def held(shape, dtype):
    return pltpu.VMEM(shape, dtype)


def in_vmem(x):
    return pltpu.with_memory_space_constraint(x, pltpu.VMEM)


def in_hbm(x):
    return pltpu.with_memory_space_constraint(x, pltpu.HBM)


def swap(x, axis, distance):
    count = lax.axis_size(axis)
    return lax.ppermute(x, axis, [(i, i ^ distance) for i in range(count)])


def sent_apart(x, axis):
    count = lax.axis_size(axis)
    if count <= 4:
        return [x] + [swap(x, axis, d) for d in range(1, count)]
    d = 1
    while d < count:
        x = x + swap(x, axis, d)
        d *= 2
    return [x]


def exchange(blocks, axis):
    far_first = {d: swap(blocks[d], axis, d) for d in range(len(blocks) - 1, 0, -1)}
    return [blocks[0]] + [far_first[d] for d in range(1, len(blocks))]


def gather(x, axis):
    count = lax.axis_size(axis)
    blocks = {0: x}
    d = count // 2
    while d:
        blocks |= {k ^ d: swap(b, axis, d) for k, b in blocks.items()}
        d //= 2
    return [blocks[k] for k in range(count)]


def halving_order(count):
    bits = count.bit_length() - 1
    return [sum(((k >> b) & 1) << (bits - 1 - b) for b in range(bits)) for k in range(count)]


def fetches_of(starts, sources, shares, sems):
    fetches = []
    for k, start in enumerate(starts):
        source, share = sources[k], shares[k]
        if start is not None:
            source = source.at[:, pl.ds(start, share.shape[1])]
        pieces = PIECES if len(share.shape) > 2 or share.shape[0] % (16 * PIECES) == 0 else 1
        step = share.shape[0] // pieces
        for p in range(pieces):
            at = pl.ds(p * step, step)
            fetches.append(pltpu.make_async_copy(source.at[at], share.at[at], sems.at[k, p]))
    return fetches


def fetch_kernel(starts, *refs):
    count = len(starts)
    fetches = fetches_of(starts, refs[:count], refs[-count - 1 : -1], refs[-1])
    for fetch in fetches:
        fetch.start()
    for fetch in fetches:
        fetch.wait()


def fetch(items, after, name):
    shapes = [x.shape if start is None else (x.shape[0], width) for x, start, width in items]
    return call(
        functools.partial(fetch_kernel, [start for _, start, _ in items]),
        [held(shape, x.dtype) for shape, (x, _, _) in zip(shapes, items)],
        (*[in_hbm(x) for x, _, _ in items], *after),
        [ANY] * (len(items) + len(after)),
        name,
        scratch=[pltpu.SemaphoreType.DMA((len(items), PIECES))],
        moved=sum(2 * math.prod(shape) for shape in shapes),
    )


def project_kernel(many, width_all, count, narrow_count, tile, me_ref, *refs):
    stat_refs, refs = refs[:many], refs[many:]
    x_ref, gain_ref, w_ref, kv_ref, first_ref, kept_ref, sent_ref, normed, own, *groups, sems = refs
    rows, width = x_ref.shape
    half = rows // 2
    block = rows // count
    sub_width = width // narrow_count
    done = first_ref.shape[1]
    starts = [done + sum(ref.shape[1] for ref in groups[:g]) for g in range(len(groups))]
    fetches = [fetches_of([start], [w_ref], [ref], sems.at[pl.ds(g, 1)]) for g, (start, ref) in enumerate(zip(starts, groups))]
    for fetch in fetches:
        for piece in fetch:
            piece.start()
    me, narrow = me_ref[0], me_ref[1]
    stats = stat_refs[0][...]
    for ref in stat_refs[1:]:
        stats = stats + ref[...]
    row = lax.broadcasted_iota(jnp.int32, (rows, rows), 0)
    column = lax.broadcasted_iota(jnp.int32, (rows, rows), 1)
    sums = jnp.sum(jnp.where(row == column, stats[0:1, :], 0.0), axis=1, keepdims=True)
    squares = jnp.sum(jnp.where(row == column, stats[1:2, :], 0.0), axis=1, keepdims=True)
    center = sums / width_all
    spread = squares / width_all - center * center
    inverse = lax.rsqrt(spread + 1e-05)
    gain = gain_ref[...].reshape(1, width)
    order = halving_order(count)
    for j in range(count):
        pick = slice(j * block, (j + 1) * block)
        place = jnp.int32(0)
        for k, d in enumerate(order):
            place = jnp.where((me ^ d) == j, k, place)
        place = pl.multiple_of(place * block, 16)
        scaled = (x_ref[pick, :].astype(jnp.float32) - center[pick]) * inverse[pick] * gain
        normed[pl.ds(place, block), :] = scaled.astype(jnp.bfloat16)
    for j in range(narrow_count):
        @pl.when(narrow == j)
        def _(j=j):
            own[...] = normed[:, j * sub_width : (j + 1) * sub_width]

    def put(got, at):
        kept_ref[:, at] = got[:half, :]
        sent_ref[:, at] = got[half:, :]

    def products(source, start):
        got = jnp.dot(normed[...], source[...], preferred_element_type=jnp.float32)
        put(got, slice(start, start + source.shape[1]))

    put(jnp.dot(own[...], kv_ref[...], preferred_element_type=jnp.float32), slice(w_ref.shape[1], kept_ref.shape[1]))
    products(first_ref, 0)
    for start, fetch, ref in zip(starts, fetches, groups):
        for piece in fetch:
            piece.wait()
        products(ref, start)


def project(me, stats, x, gain, w, kv, first, width_all, count, narrow_count, tile):
    rows, width = x.shape
    queries = w.shape[1]
    tiles = (queries - first.shape[1]) // tile
    groups = [2] * (tiles // 2) + [1] * (tiles % 2)
    half = jax.ShapeDtypeStruct((rows // 2, queries + kv.shape[1]), jnp.float32)
    return call(
        functools.partial(project_kernel, len(stats), width_all, count, narrow_count, tile),
        (half, half),
        (me, *stats, x, gain, in_hbm(w), in_vmem(kv), in_vmem(first)),
        [SCALAR] + [FULL] * (len(stats) + 2) + [ANY] + [FULL] * 2,
        "project",
        scratch=[
            pltpu.VMEM((rows, width), jnp.bfloat16),
            pltpu.VMEM((rows, width // narrow_count), jnp.bfloat16),
            *[pltpu.VMEM((width, n * tile), jnp.bfloat16) for n in groups],
            pltpu.SemaphoreType.DMA((len(groups), PIECES)),
        ],
        limit=30,
        flops=2 * rows * width * queries,
        moved=2 * width * tiles * tile,
    )


def fold_kernel(guards, kept_ref, came_ref, *refs):
    still_ref, sent_ref = refs[guards:]
    half = still_ref.shape[0]
    still_ref[...] = kept_ref[:half, :] + came_ref[:half, :]
    sent_ref[...] = kept_ref[half:, :] + came_ref[half:, :]


def fold(kept, came, guards):
    half = jax.ShapeDtypeStruct((kept.shape[0] // 2, kept.shape[1]), jnp.float32)
    return call(
        functools.partial(fold_kernel, len(guards)),
        (half, half),
        (kept, came, *map(in_vmem, guards)),
        [FULL] * (2 + len(guards)),
        "fold",
        moved=16 * kept.size,
    )


def split_kernel(queries, guards, me_ref, kept_ref, came_ref, *refs):
    out_refs, slots = refs[guards:-1], refs[-1]
    count, rows = len(out_refs), out_refs[0].shape[0]
    narrow = me_ref[1]
    total = kept_ref[...] + came_ref[...]
    for j in range(count):
        slots[j * PAD : j * PAD + rows, :] = total[j * rows : (j + 1) * rows, :]
    for d, out_ref in enumerate(out_refs):
        mine = slots[pl.ds(pl.multiple_of((narrow ^ d) * PAD, PAD), rows), :]
        high = mine.astype(jnp.bfloat16)
        out_ref[:, : mine.shape[1]] = high
        out_ref[:, mine.shape[1] :] = (mine - high.astype(jnp.float32))[:, queries:].astype(jnp.bfloat16)


def attend_kernel(head_dim, count, guards, start, lengths_ref, *refs):
    came_refs, kv_ref, w_ref = refs[:count][::-1], refs[count], refs[count + 1]
    refs = refs[count + 2 + guards :]
    out_refs, share, (heads, contexts, sems) = refs[:count], refs[count], refs[count + 1 :]
    fetches = fetches_of([start], [w_ref], [share], sems)
    for fetch in fetches:
        fetch.start()
    rows, positions = kv_ref.shape[0], kv_ref.shape[1]
    queries = out_refs[0].shape[1]
    each = queries // head_dim
    total_heads = each * count
    slabs = head_dim // LANES
    scaling = 1.0 / math.sqrt(head_dim)
    for d, ref in enumerate(came_refs):
        for h in range(each):
            at = (d * each + h) * PAD
            for k in range(slabs):
                start = h * head_dim + k * LANES
                heads[k, at : at + rows, :] = ref[:, start : start + LANES].astype(jnp.float32)
    terms = came_refs[0][:, queries:].astype(jnp.float32)
    for ref in came_refs[1:]:
        terms = terms + ref[:, queries:].astype(jnp.float32)
    pair = 2 * head_dim
    fresh = terms[:, :pair] + terms[:, pair:]
    fresh = fresh.astype(jnp.bfloat16).astype(jnp.float32)
    place = lax.broadcasted_iota(jnp.int32, (total_heads, positions), 1)
    for r in range(rows):
        query = jnp.concatenate([heads[k, pl.ds(r, total_heads, stride=PAD), :] for k in range(slabs)], axis=1)
        scores = (
            lax.dot_general(
                query.astype(jnp.bfloat16),
                kv_ref[r, :, :head_dim],
                (((1,), (1,)), ((), ())),
                preferred_element_type=jnp.float32,
            )
            * scaling
        )
        own_score = jnp.sum(query * fresh[r : r + 1, :head_dim], axis=1, keepdims=True) * scaling
        valid = place < lengths_ref[r]
        top = jnp.maximum(jnp.max(jnp.where(valid, scores, -jnp.inf), axis=1, keepdims=True), own_score)
        weights = jnp.where(valid, jnp.exp(scores - top), 0.0)
        own_weight = jnp.exp(own_score - top)
        total = jnp.sum(weights, axis=1, keepdims=True) + own_weight
        numer = jnp.dot(weights.astype(jnp.bfloat16), kv_ref[r, :, head_dim:], preferred_element_type=jnp.float32)
        numer = numer + own_weight.astype(jnp.bfloat16).astype(jnp.float32) * fresh[r : r + 1, head_dim:]
        context = numer / total
        for k in range(slabs):
            contexts[k, pl.ds(r, total_heads, stride=PAD), :] = context[:, k * LANES : (k + 1) * LANES]
    for d, ref in enumerate(out_refs):
        for h in range(each):
            at = (d * each + h) * PAD
            for k in range(slabs):
                start = h * head_dim + k * LANES
                ref[:, start : start + LANES] = contexts[k, at : at + rows, :].astype(jnp.bfloat16)
    for fetch in fetches:
        fetch.wait()


def attend(lengths, came, kv, cut, head_dim, queries, guards):
    rows = kv.shape[0]
    count = len(came)
    all_heads = count * queries // head_dim
    scratch = pltpu.VMEM((head_dim // LANES, all_heads * PAD, LANES), jnp.float32)
    w, start, width = cut
    return call(
        functools.partial(attend_kernel, head_dim, count, len(guards), start),
        [jax.ShapeDtypeStruct((rows, queries), jnp.bfloat16)] * count + [held((w.shape[0], width), w.dtype)],
        (lengths, *came[::-1], in_vmem(kv), in_hbm(w), *map(in_vmem, guards)),
        [SCALAR] + [FULL] * (count + 1) + [ANY] + [FULL] * len(guards),
        "attend",
        scratch=[scratch, scratch, pltpu.SemaphoreType.DMA((1, PIECES))],
        limit=8,
        flops=4 * rows * count * queries * kv.shape[1],
    )


def join_kernel(guards, me_ref, *refs):
    count = len(refs) - guards - 2
    out_ref, joined = refs[-2:]
    rows = refs[0].shape[0]
    for d in range(count):
        at = pl.ds(pl.multiple_of((me_ref[1] ^ d) * PAD, PAD), rows)
        joined[at, :] = refs[count - 1 - d][...].astype(jnp.float32)
    came = [joined[j * PAD : j * PAD + rows, :] for j in range(count)]
    out_ref[...] = jnp.concatenate(came, axis=0).astype(jnp.bfloat16)


def code(x, ref):
    largest = jnp.maximum(jnp.max(jnp.abs(x), axis=1, keepdims=True), TINY)
    power = jnp.floor(jnp.log2(largest)) + 1.0
    steps = jnp.round(x * (STEPS * jnp.exp2(-power)))
    ref[:, : x.shape[1]] = steps.astype(jnp.int32).astype(jnp.int16)
    ref[:, x.shape[1] :] = jnp.broadcast_to(power, (x.shape[0], LANES)).astype(jnp.int32).astype(jnp.int16)


def decode(ref, width):
    power = ref[:, width:].astype(jnp.int32).astype(jnp.float32)[:, 0:1]
    return ref[:, :width].astype(jnp.int32).astype(jnp.float32) * (jnp.exp2(power) * (1.0 / STEPS))


def output_kernel(count, weights, narrow_count, me_ref, *refs):
    x_refs, w_refs, (sums_ref, sent_ref) = refs[:count], refs[count : count + weights], refs[-2:]
    block = x_refs[0].shape[0]
    ratio = count // narrow_count
    places = []
    for d in range(count):
        wide = me_ref[0] ^ d
        apart = (wide // ratio) ^ me_ref[1]
        place = jnp.int32(0)
        for k, distance in enumerate(halving_order(narrow_count)):
            place = jnp.where(apart == distance, k, place)
        places.append(pl.multiple_of((place * ratio + wide % ratio) * block, block))
    x = jnp.concatenate([ref[...] for ref in x_refs], axis=0)
    at = 0
    for w_ref in w_refs:
        width = w_ref.shape[1]
        got = jnp.dot(x, w_ref[...], preferred_element_type=jnp.float32)
        for d, place in enumerate(places):
            sums_ref[pl.ds(place, block), at : at + width] = got[d * block : (d + 1) * block, :]
        at += width
    code(sums_ref[sums_ref.shape[0] // 2 :, :], sent_ref)


def output_part(me, blocks, ws, narrow_count, after):
    count = len(blocks)
    block, depth = blocks[0].shape
    rows, columns = count * block, sum(w.shape[1] for w in ws)
    return call(
        functools.partial(output_kernel, count, len(ws), narrow_count),
        (
            jax.ShapeDtypeStruct((rows, columns), jnp.float32),
            jax.ShapeDtypeStruct((rows // 2, columns + LANES), jnp.int16),
        ),
        (me, *blocks, *map(in_vmem, ws), *after),
        [SCALAR] + [FULL] * (count + len(ws)) + [ANY] * len(after),
        "output_part",
        limit=8,
        flops=2 * rows * depth * columns,
        moved=2 * rows * depth,
    )


def halve_kernel(sums_ref, came_ref, *refs):
    still_ref, sent_ref = refs[-2:]
    half = still_ref.shape[0]
    total = sums_ref[: 2 * half, :] + decode(came_ref, sums_ref.shape[1])
    still_ref[...] = total[:half, :]
    code(total[half:, :], sent_ref)


def halve(sums, came, after):
    rows, columns = came.shape[0], sums.shape[1]
    return call(
        halve_kernel,
        (
            jax.ShapeDtypeStruct((rows // 2, columns), jnp.float32),
            jax.ShapeDtypeStruct((rows // 2, columns + LANES), jnp.int16),
        ),
        (sums, came, *after),
        [FULL, FULL] + [ANY] * len(after),
        "halve",
        moved=16 * rows * columns,
    )


def finish_kernel(starts, *refs):
    out_ref = refs[-1]
    for at, kept_ref, came_ref in zip(starts, refs[:-1:2], refs[1:-1:2]):
        width = kept_ref.shape[1]
        out_ref[:, at : at + width] = (kept_ref[...] + decode(came_ref, width)).astype(jnp.bfloat16)


def finish(starts, cuts):
    parts = [x for cut in cuts for x in cut]
    rows, columns = parts[0].shape[0], sum(cut[0].shape[1] for cut in cuts)
    return call(
        functools.partial(finish_kernel, starts),
        jax.ShapeDtypeStruct((rows, columns), jnp.bfloat16),
        parts,
        [FULL] * len(parts),
        "finish",
        moved=8 * columns * rows,
    )


def local(activations, norm_gain, query_weight, kv_weight, out_weight, kv_cache, lengths):
    wide_count = lax.axis_size("wide")
    narrow_count = lax.axis_size("narrow")
    me = jnp.stack([lax.axis_index("wide"), lax.axis_index("narrow")]).astype(jnp.int32)
    own_rows, head_dim = kv_cache.shape[0], kv_cache.shape[2] // 2
    rows, width = activations.shape
    queries = query_weight.shape[1]
    columns = out_weight.shape[1]
    tile = 256
    values = activations.astype(jnp.float32)
    stats = jnp.stack([jnp.sum(values, axis=1), jnp.sum(values * values, axis=1)])
    first_part, kv_part = fetch(
        [(query_weight, 0, queries // tile // 4 * tile), (kv_weight, None, None)], [stats, me], "fetch_query_weight"
    )
    kept, sent = project(
        me,
        sent_apart(stats, "wide"),
        activations,
        norm_gain,
        query_weight,
        kv_part,
        first_part,
        width * wide_count,
        wide_count,
        narrow_count,
        tile,
    )
    ends = [columns // LANES * k // 18 * LANES for k in (0, 6, 11, 13, 18)]
    cuts = [(out_weight, start, end - start) for start, end in zip(ends, ends[1:])]
    d = 1
    while 2 * d < wide_count:
        kept, sent = fold(kept, swap(sent, "wide", d), [])
        d *= 2
    out_parts = [None] * 4
    out_parts[0], cache = fetch([cuts[0], (kv_cache, None, None)], [sent], "fetch_out_weight_0")
    split = call(
        functools.partial(split_kernel, queries, 1),
        [jax.ShapeDtypeStruct((own_rows, queries + 4 * head_dim), jnp.bfloat16)] * narrow_count,
        (me, kept, swap(sent, "wide", d), in_vmem(out_parts[0])),
        [SCALAR] + [FULL] * 3,
        "split",
        scratch=[pltpu.VMEM((narrow_count * PAD, queries + 2 * head_dim), jnp.float32)],
        moved=16 * kept.size,
    )
    [out_parts[1]] = fetch([cuts[1]], [split[0]], "fetch_out_weight_1")
    *context, out_parts[2] = attend(
        lengths, exchange(split, "narrow"), cache, cuts[2], head_dim, queries, [out_parts[1]]
    )
    [out_parts[3]] = fetch([cuts[3]], [context[0]], "fetch_out_weight_3")
    returned = call(
        functools.partial(join_kernel, 1),
        jax.ShapeDtypeStruct((narrow_count * own_rows, queries), jnp.bfloat16),
        (me, *exchange(context, "narrow")[::-1], in_vmem(out_parts[3])),
        [SCALAR] + [FULL] * (narrow_count + 1),
        "join",
        scratch=[pltpu.VMEM((narrow_count * PAD, queries), jnp.float32)],
        moved=4 * narrow_count * own_rows * queries,
    )
    gathered = gather(returned, "wide")
    cut_sums, halved, last = [], [], []

    def exchange_cut(kept, sent, after):
        d = 1
        while 2 * d < narrow_count:
            kept, sent = halve(kept, swap(sent, "narrow", d), after)
            after = []
            d *= 2
        halved.append(kept)
        cut_sums.append((kept, swap(sent, "narrow", d)))

    for parts in (out_parts[:1], out_parts[2:], out_parts[1:2]):
        kept, sent = output_part(me, gathered, parts, narrow_count, halved[-1:])
        if last:
            exchange_cut(*last, [kept])
        last = (kept, sent)
    exchange_cut(*last, [])
    return finish([ends[0], ends[2], ends[1]], cut_sums)


def solution(mesh):
    return jax.shard_map(
        local,
        mesh=mesh,
        in_specs=(
            P("groups", "wide"),
            P("wide"),
            P("wide", "narrow"),
            P(("wide", "narrow"), None),
            P("narrow", "wide"),
            P(("groups", "wide", "narrow"), None, None),
            P(("groups", "wide", "narrow")),
        ),
        out_specs=P(("groups", "narrow"), "wide"),
        check_vma=False,
    )
```

```python
import functools
import math

import jax
import jax.numpy as jnp
from jax import lax
from jax.experimental import pallas as pl
from jax.experimental.pallas import tpu as pltpu
from jax.sharding import PartitionSpec as P

MIB = 1 << 20
FULL = pl.BlockSpec(memory_space=pltpu.VMEM)
ANY = pl.BlockSpec(memory_space=pl.ANY)
SCALAR = pl.BlockSpec(memory_space=pltpu.SMEM)
STEPS = 32700.0
TINY = 1e-37
LANES = 128
PAD = 8
PIECES = 4
BESIDE = 5 * 10**9


def call(kernel, outs, ins, specs, name, scratch=(), limit=4, flops=0, moved=0):
    return pl.pallas_call(
        kernel,
        out_shape=outs,
        in_specs=specs,
        out_specs=jax.tree.map(lambda _: FULL, outs),
        scratch_shapes=list(scratch),
        compiler_params=pltpu.CompilerParams(vmem_limit_bytes=limit * MIB),
        cost_estimate=pl.CostEstimate(flops=flops, bytes_accessed=moved, transcendentals=0),
        name=name,
    )(*ins)


def held(shape, dtype):
    return pltpu.VMEM(shape, dtype)


def in_vmem(x):
    return pltpu.with_memory_space_constraint(x, pltpu.VMEM)


def in_hbm(x):
    return pltpu.with_memory_space_constraint(x, pltpu.HBM)


def swap(x, axis, distance):
    count = lax.axis_size(axis)
    return lax.ppermute(x, axis, [(i, i ^ distance) for i in range(count)])


def sent_apart(x, axis):
    count = lax.axis_size(axis)
    if count <= 4:
        return [x] + [swap(x, axis, d) for d in range(1, count)]
    d = 1
    while d < count:
        x = x + swap(x, axis, d)
        d *= 2
    return [x]


def exchange(blocks, axis):
    far_first = {d: swap(blocks[d], axis, d) for d in range(len(blocks) - 1, 0, -1)}
    return [blocks[0]] + [far_first[d] for d in range(1, len(blocks))]


def gather(x, axis):
    count = lax.axis_size(axis)
    blocks = {0: x}
    d = count // 2
    while d:
        blocks |= {k ^ d: swap(b, axis, d) for k, b in blocks.items()}
        d //= 2
    return [blocks[k] for k in range(count)]


def halving_order(count):
    bits = count.bit_length() - 1
    return [sum(((k >> b) & 1) << (bits - 1 - b) for b in range(bits)) for k in range(count)]


def fetches_of(starts, sources, shares, sems):
    fetches = []
    for k, start in enumerate(starts):
        source, share = sources[k], shares[k]
        if start is not None:
            source = source.at[:, pl.ds(start, share.shape[1])]
        pieces = PIECES if len(share.shape) > 2 or share.shape[0] % (16 * PIECES) == 0 else 1
        step = share.shape[0] // pieces
        for p in range(pieces):
            at = pl.ds(p * step, step)
            fetches.append(pltpu.make_async_copy(source.at[at], share.at[at], sems.at[k, p]))
    return fetches


def fetch_kernel(starts, *refs):
    count = len(starts)
    fetches = fetches_of(starts, refs[:count], refs[-count - 1 : -1], refs[-1])
    for fetch in fetches:
        fetch.start()
    for fetch in fetches:
        fetch.wait()


def fetch(items, after, name):
    shapes = [x.shape if start is None else (x.shape[0], width) for x, start, width in items]
    return call(
        functools.partial(fetch_kernel, [start for _, start, _ in items]),
        [held(shape, x.dtype) for shape, (x, _, _) in zip(shapes, items)],
        (*[in_hbm(x) for x, _, _ in items], *after),
        [ANY] * (len(items) + len(after)),
        name,
        scratch=[pltpu.SemaphoreType.DMA((len(items), PIECES))],
        moved=sum(2 * math.prod(shape) for shape in shapes),
    )


def project_kernel(many, width_all, count, narrow_count, tile, me_ref, *refs):
    stat_refs, refs = refs[:many], refs[many:]
    x_ref, gain_ref, w_ref, kv_ref, first_ref, kept_ref, sent_ref, normed, own, *groups, sems = refs
    rows, width = x_ref.shape
    half = rows // 2
    block = rows // count
    sub_width = width // narrow_count
    done = first_ref.shape[1]
    starts = [done + sum(ref.shape[1] for ref in groups[:g]) for g in range(len(groups))]
    fetches = [fetches_of([start], [w_ref], [ref], sems.at[pl.ds(g, 1)]) for g, (start, ref) in enumerate(zip(starts, groups))]
    ahead = 2
    for fetch in fetches[:ahead]:
        for piece in fetch:
            piece.start()
    me, narrow = me_ref[0], me_ref[1]
    stats = stat_refs[0][...]
    for ref in stat_refs[1:]:
        stats = stats + ref[...]
    row = lax.broadcasted_iota(jnp.int32, (rows, rows), 0)
    column = lax.broadcasted_iota(jnp.int32, (rows, rows), 1)
    sums = jnp.sum(jnp.where(row == column, stats[0:1, :], 0.0), axis=1, keepdims=True)
    squares = jnp.sum(jnp.where(row == column, stats[1:2, :], 0.0), axis=1, keepdims=True)
    center = sums / width_all
    spread = squares / width_all - center * center
    inverse = lax.rsqrt(spread + 1e-05)
    gain = gain_ref[...].reshape(1, width)
    order = halving_order(count)
    for j in range(count):
        pick = slice(j * block, (j + 1) * block)
        place = jnp.int32(0)
        for k, d in enumerate(order):
            place = jnp.where((me ^ d) == j, k, place)
        place = pl.multiple_of(place * block, 16)
        scaled = (x_ref[pick, :].astype(jnp.float32) - center[pick]) * inverse[pick] * gain
        normed[pl.ds(place, block), :] = scaled.astype(jnp.bfloat16)
    for j in range(narrow_count):
        @pl.when(narrow == j)
        def _(j=j):
            own[...] = normed[:, j * sub_width : (j + 1) * sub_width]

    def put(got, at):
        kept_ref[:, at] = got[:half, :]
        sent_ref[:, at] = got[half:, :]

    def products(source, start):
        got = jnp.dot(normed[...], source[...], preferred_element_type=jnp.float32)
        put(got, slice(start, start + source.shape[1]))

    put(jnp.dot(own[...], kv_ref[...], preferred_element_type=jnp.float32), slice(w_ref.shape[1], kept_ref.shape[1]))
    products(first_ref, 0)
    for g, fetch in enumerate(fetches):
        for piece in fetch:
            piece.wait()
        for piece in fetches[g + ahead] if g + ahead < len(fetches) else ():
            piece.start()
        products(groups[g], starts[g])


def project(me, stats, x, gain, w, kv, first, width_all, count, narrow_count, tile):
    rows, width = x.shape
    queries = w.shape[1]
    tiles = (queries - first.shape[1]) // tile
    groups = [2] * (tiles // 2) + [1] * (tiles % 2)
    half = jax.ShapeDtypeStruct((rows // 2, queries + kv.shape[1]), jnp.float32)
    return call(
        functools.partial(project_kernel, len(stats), width_all, count, narrow_count, tile),
        (half, half),
        (me, *stats, x, gain, in_hbm(w), in_vmem(kv), in_vmem(first)),
        [SCALAR] + [FULL] * (len(stats) + 2) + [ANY] + [FULL] * 2,
        "project",
        scratch=[
            pltpu.VMEM((rows, width), jnp.bfloat16),
            pltpu.VMEM((rows, width // narrow_count), jnp.bfloat16),
            *[pltpu.VMEM((width, n * tile), jnp.bfloat16) for n in groups],
            pltpu.SemaphoreType.DMA((len(groups), PIECES)),
        ],
        limit=30,
        flops=2 * rows * width * queries,
        moved=2 * width * tiles * tile,
    )


def fold_kernel(kept_ref, came_ref, still_ref, sent_ref):
    half = still_ref.shape[0]
    still_ref[...] = kept_ref[:half, :] + came_ref[:half, :]
    sent_ref[...] = kept_ref[half:, :] + came_ref[half:, :]


def fold(kept, came):
    half = jax.ShapeDtypeStruct((kept.shape[0] // 2, kept.shape[1]), jnp.float32)
    return call(
        fold_kernel,
        (half, half),
        (kept, came),
        [FULL] * 2,
        "fold",
        flops=BESIDE,
    )


def split_kernel(queries, me_ref, kept_ref, came_ref, *refs):
    out_refs, slots = refs[:-1], refs[-1]
    count, rows = len(out_refs), out_refs[0].shape[0]
    narrow = me_ref[1]
    total = kept_ref[...] + came_ref[...]
    for j in range(count):
        slots[j * PAD : j * PAD + rows, :] = total[j * rows : (j + 1) * rows, :]
    for d, out_ref in enumerate(out_refs):
        mine = slots[pl.ds(pl.multiple_of((narrow ^ d) * PAD, PAD), rows), :]
        high = mine.astype(jnp.bfloat16)
        out_ref[:, : mine.shape[1]] = high
        out_ref[:, mine.shape[1] :] = (mine - high.astype(jnp.float32))[:, queries:].astype(jnp.bfloat16)


def attend_kernel(head_dim, count, lengths_ref, *refs):
    came_refs, kv_ref = refs[:count][::-1], refs[count]
    refs = refs[count + 1 :]
    out_refs, (heads, contexts) = refs[:count], refs[count:]
    rows, positions = kv_ref.shape[0], kv_ref.shape[1]
    queries = out_refs[0].shape[1]
    each = queries // head_dim
    total_heads = each * count
    slabs = head_dim // LANES
    scaling = 1.0 / math.sqrt(head_dim)
    for d, ref in enumerate(came_refs):
        for h in range(each):
            at = (d * each + h) * PAD
            for k in range(slabs):
                start = h * head_dim + k * LANES
                heads[k, at : at + rows, :] = ref[:, start : start + LANES].astype(jnp.float32)
    terms = came_refs[0][:, queries:].astype(jnp.float32)
    for ref in came_refs[1:]:
        terms = terms + ref[:, queries:].astype(jnp.float32)
    pair = 2 * head_dim
    fresh = terms[:, :pair] + terms[:, pair:]
    fresh = fresh.astype(jnp.bfloat16).astype(jnp.float32)
    place = lax.broadcasted_iota(jnp.int32, (total_heads, positions), 1)
    for r in range(rows):
        query = jnp.concatenate([heads[k, pl.ds(r, total_heads, stride=PAD), :] for k in range(slabs)], axis=1)
        scores = (
            lax.dot_general(
                query.astype(jnp.bfloat16),
                kv_ref[r, :, :head_dim],
                (((1,), (1,)), ((), ())),
                preferred_element_type=jnp.float32,
            )
            * scaling
        )
        own_score = jnp.sum(query * fresh[r : r + 1, :head_dim], axis=1, keepdims=True) * scaling
        valid = place < lengths_ref[r]
        top = jnp.maximum(jnp.max(jnp.where(valid, scores, -jnp.inf), axis=1, keepdims=True), own_score)
        weights = jnp.where(valid, jnp.exp(scores - top), 0.0)
        own_weight = jnp.exp(own_score - top)
        total = jnp.sum(weights, axis=1, keepdims=True) + own_weight
        numer = jnp.dot(weights.astype(jnp.bfloat16), kv_ref[r, :, head_dim:], preferred_element_type=jnp.float32)
        numer = numer + own_weight.astype(jnp.bfloat16).astype(jnp.float32) * fresh[r : r + 1, head_dim:]
        context = numer / total
        for k in range(slabs):
            contexts[k, pl.ds(r, total_heads, stride=PAD), :] = context[:, k * LANES : (k + 1) * LANES]
    for d, ref in enumerate(out_refs):
        for h in range(each):
            at = (d * each + h) * PAD
            for k in range(slabs):
                start = h * head_dim + k * LANES
                ref[:, start : start + LANES] = contexts[k, at : at + rows, :].astype(jnp.bfloat16)


def attend(lengths, came, kv, head_dim, queries):
    rows = kv.shape[0]
    count = len(came)
    all_heads = count * queries // head_dim
    scratch = pltpu.VMEM((head_dim // LANES, all_heads * PAD, LANES), jnp.float32)
    return call(
        functools.partial(attend_kernel, head_dim, count),
        [jax.ShapeDtypeStruct((rows, queries), jnp.bfloat16)] * count,
        (lengths, *came[::-1], in_vmem(kv)),
        [SCALAR] + [FULL] * (count + 1),
        "attend",
        scratch=[scratch, scratch],
        limit=8,
        flops=BESIDE,
    )


def join_kernel(me_ref, *refs):
    count = len(refs) - 2
    out_ref, joined = refs[-2:]
    rows = refs[0].shape[0]
    for d in range(count):
        at = pl.ds(pl.multiple_of((me_ref[1] ^ d) * PAD, PAD), rows)
        joined[at, :] = refs[count - 1 - d][...].astype(jnp.float32)
    came = [joined[j * PAD : j * PAD + rows, :] for j in range(count)]
    out_ref[...] = jnp.concatenate(came, axis=0).astype(jnp.bfloat16)


def code(x, ref):
    largest = jnp.maximum(jnp.max(jnp.abs(x), axis=1, keepdims=True), TINY)
    power = jnp.floor(jnp.log2(largest)) + 1.0
    steps = jnp.round(x * (STEPS * jnp.exp2(-power)))
    ref[:, : x.shape[1]] = steps.astype(jnp.int32).astype(jnp.int16)
    ref[:, x.shape[1] :] = jnp.broadcast_to(power, (x.shape[0], LANES)).astype(jnp.int32).astype(jnp.int16)


def decode(ref, width):
    power = ref[:, width:].astype(jnp.int32).astype(jnp.float32)[:, 0:1]
    return ref[:, :width].astype(jnp.int32).astype(jnp.float32) * (jnp.exp2(power) * (1.0 / STEPS))


def output_kernel(start, count, narrow_count, me_ref, *refs):
    x_refs, w_ref, (sums_ref, sent_ref) = refs[:count], refs[count], refs[-2:]
    block = x_refs[0].shape[0]
    ratio = count // narrow_count
    places = []
    for d in range(count):
        wide = me_ref[0] ^ d
        apart = (wide // ratio) ^ me_ref[1]
        place = jnp.int32(0)
        for k, distance in enumerate(halving_order(narrow_count)):
            place = jnp.where(apart == distance, k, place)
        places.append(pl.multiple_of((place * ratio + wide % ratio) * block, block))
    x = jnp.concatenate([ref[...] for ref in x_refs], axis=0)
    got = jnp.dot(x, w_ref[:, start : start + sums_ref.shape[1]], preferred_element_type=jnp.float32)
    for d, place in enumerate(places):
        sums_ref[pl.ds(place, block), :] = got[d * block : (d + 1) * block, :]
    code(sums_ref[sums_ref.shape[0] // 2 :, :], sent_ref)


def output_part(me, blocks, w, start, columns, narrow_count, after):
    count = len(blocks)
    block, depth = blocks[0].shape
    rows = count * block
    return call(
        functools.partial(output_kernel, start, count, narrow_count),
        (
            jax.ShapeDtypeStruct((rows, columns), jnp.float32),
            jax.ShapeDtypeStruct((rows // 2, columns + LANES), jnp.int16),
        ),
        (me, *blocks, in_vmem(w), *after),
        [SCALAR] + [FULL] * (count + 1) + [ANY] * len(after),
        "output_part",
        limit=8,
        flops=2 * rows * depth * columns,
        moved=2 * rows * depth,
    )


def halve_kernel(sums_ref, came_ref, *refs):
    still_ref, sent_ref = refs[-2:]
    half = still_ref.shape[0]
    total = sums_ref[: 2 * half, :] + decode(came_ref, sums_ref.shape[1])
    still_ref[...] = total[:half, :]
    code(total[half:, :], sent_ref)


def halve(sums, came, after):
    rows, columns = came.shape[0], sums.shape[1]
    return call(
        halve_kernel,
        (
            jax.ShapeDtypeStruct((rows // 2, columns), jnp.float32),
            jax.ShapeDtypeStruct((rows // 2, columns + LANES), jnp.int16),
        ),
        (sums, came, *after),
        [FULL, FULL] + [ANY] * len(after),
        "halve",
        moved=16 * rows * columns,
    )


def finish_kernel(starts, kinds, *refs):
    out_ref = refs[-1]
    k = 0
    for at, kind in zip(starts, kinds):
        width = refs[k].shape[1]
        done = refs[k][...]
        if kind == 2:
            done = (done + decode(refs[k + 1], width)).astype(jnp.bfloat16)
        out_ref[:, at : at + width] = done
        k += kind


def finish(starts, cuts):
    parts = [x for cut in cuts for x in cut]
    rows, columns = parts[0].shape[0], sum(cut[0].shape[1] for cut in cuts)
    return call(
        functools.partial(finish_kernel, starts, [len(cut) for cut in cuts]),
        jax.ShapeDtypeStruct((rows, columns), jnp.bfloat16),
        parts,
        [FULL] * len(parts),
        "finish",
        moved=8 * columns * rows,
    )


def local(activations, norm_gain, query_weight, kv_weight, out_weight, kv_cache, lengths):
    wide_count = lax.axis_size("wide")
    narrow_count = lax.axis_size("narrow")
    me = jnp.stack([lax.axis_index("wide"), lax.axis_index("narrow")]).astype(jnp.int32)
    own_rows, head_dim = kv_cache.shape[0], kv_cache.shape[2] // 2
    rows, width = activations.shape
    queries = query_weight.shape[1]
    columns = out_weight.shape[1]
    tile = 256
    values = activations.astype(jnp.float32)
    stats = jnp.stack([jnp.sum(values, axis=1), jnp.sum(values * values, axis=1)])
    first_part, kv_part = fetch(
        [(query_weight, 0, queries // tile // 4 * tile), (kv_weight, None, None)], [stats, me], "fetch_query_weight"
    )
    kept, sent = project(
        me,
        sent_apart(stats, "wide"),
        activations,
        norm_gain,
        query_weight,
        kv_part,
        first_part,
        width * wide_count,
        wide_count,
        narrow_count,
        tile,
    )
    d = 1
    while 2 * d < wide_count:
        kept, sent = fold(kept, swap(sent, "wide", d))
        d *= 2
    split = call(
        functools.partial(split_kernel, queries),
        [jax.ShapeDtypeStruct((own_rows, queries + 4 * head_dim), jnp.bfloat16)] * narrow_count,
        (me, kept, swap(sent, "wide", d)),
        [SCALAR] + [FULL] * 2,
        "split",
        scratch=[pltpu.VMEM((narrow_count * PAD, queries + 2 * head_dim), jnp.float32)],
        flops=BESIDE,
    )
    context = attend(lengths, exchange(split, "narrow"), kv_cache, head_dim, queries)
    returned = call(
        join_kernel,
        jax.ShapeDtypeStruct((narrow_count * own_rows, queries), jnp.bfloat16),
        (me, *exchange(context, "narrow")[::-1]),
        [SCALAR] + [FULL] * narrow_count,
        "join",
        scratch=[pltpu.VMEM((narrow_count * PAD, queries), jnp.float32)],
        flops=BESIDE,
    )
    gathered = gather(returned, "wide")
    ends = [columns // LANES * k // 18 * LANES for k in (0,7,15,18)]
    cut_sums, halved, last = [], [], []

    def exchange_cut(kept, sent, after):
        d = 1
        while 2 * d < narrow_count:
            kept, sent = halve(kept, swap(sent, "narrow", d), after)
            after = []
            d *= 2
        halved.append(kept)
        cut_sums.append((kept, swap(sent, "narrow", d)))

    for start, end in zip(ends, ends[1:]):
        kept, sent = output_part(me, gathered, out_weight, start, end - start, narrow_count, halved[-1:])
        if last:
            exchange_cut(*last, [kept])
        last = (kept, sent)
    early = finish([0], cut_sums[:1])
    exchange_cut(*last, [early])
    cut_sums[0] = (early,)
    return finish(ends[:-1], cut_sums)


def solution(mesh):
    return jax.shard_map(
        local,
        mesh=mesh,
        in_specs=(
            P("groups", "wide"),
            P("wide"),
            P("wide", "narrow"),
            P(("wide", "narrow"), None),
            P("narrow", "wide"),
            P(("groups", "wide", "narrow"), None, None),
            P(("groups", "wide", "narrow")),
        ),
        out_specs=P(("groups", "narrow"), "wide"),
        check_vma=False,
    )
```

```python
import functools
import math

import jax
import jax.numpy as jnp
from jax import lax
from jax.experimental import pallas as pl
from jax.experimental.pallas import tpu as pltpu
from jax.sharding import PartitionSpec as P

MIB = 1 << 20
FULL = pl.BlockSpec(memory_space=pltpu.VMEM)
ANY = pl.BlockSpec(memory_space=pl.ANY)
SCALAR = pl.BlockSpec(memory_space=pltpu.SMEM)
STEPS = 32700.0
TINY = 1e-37
LANES = 128
PAD = 8
BESIDE = 5 * 10**9


def call(kernel, outs, ins, specs, name, scratch=(), limit=4, flops=0, moved=0):
    return pl.pallas_call(
        kernel,
        out_shape=outs,
        in_specs=specs,
        out_specs=jax.tree.map(lambda _: FULL, outs),
        scratch_shapes=list(scratch),
        compiler_params=pltpu.CompilerParams(vmem_limit_bytes=limit * MIB),
        cost_estimate=pl.CostEstimate(flops=flops, bytes_accessed=moved, transcendentals=0),
        name=name,
    )(*ins)


def held(shape, dtype):
    return pltpu.VMEM(shape, dtype)


def in_vmem(x):
    return pltpu.with_memory_space_constraint(x, pltpu.VMEM)


def in_hbm(x):
    return pltpu.with_memory_space_constraint(x, pltpu.HBM)


def swap(x, axis, distance):
    count = lax.axis_size(axis)
    return lax.ppermute(x, axis, [(i, i ^ distance) for i in range(count)])


def sent_apart(x, axis):
    count = lax.axis_size(axis)
    if count <= 4:
        return [x] + [swap(x, axis, d) for d in range(1, count)]
    d = 1
    while d < count:
        x = x + swap(x, axis, d)
        d *= 2
    return [x]


def exchange(blocks, axis):
    far_first = {d: swap(blocks[d], axis, d) for d in range(len(blocks) - 1, 0, -1)}
    return [blocks[0]] + [far_first[d] for d in range(1, len(blocks))]


def gather(x, axis):
    count = lax.axis_size(axis)
    blocks = {0: x}
    d = count // 2
    while d:
        blocks |= {k ^ d: swap(b, axis, d) for k, b in blocks.items()}
        d //= 2
    return [blocks[k] for k in range(count)]


def halving_order(count):
    bits = count.bit_length() - 1
    return [sum(((k >> b) & 1) << (bits - 1 - b) for b in range(bits)) for k in range(count)]


def fetch_kernel(w_ref, kv_ref, *refs):
    share_ref, kv_share_ref, sems = refs[-3:]
    fetches = [
        pltpu.make_async_copy(w_ref.at[: share_ref.shape[0]], share_ref, sems.at[0]),
        pltpu.make_async_copy(kv_ref, kv_share_ref, sems.at[1]),
    ]
    for fetch in fetches:
        fetch.start()
    for fetch in fetches:
        fetch.wait()


def fetch(w, kv, rows, after):
    return call(
        fetch_kernel,
        [held((rows, w.shape[1]), w.dtype), held(kv.shape, kv.dtype)],
        (in_hbm(w), in_hbm(kv), *after),
        [ANY] * (2 + len(after)),
        "fetch_query_weight",
        scratch=[pltpu.SemaphoreType.DMA((2,))],
        moved=2 * (rows * w.shape[1] + kv.size),
    )


def row_block(rows):
    return LANES * max(1, rows // LANES // 6)


def project_kernel(many, width_all, count, narrow_count, me_ref, *refs):
    stat_refs, refs = refs[:many], refs[many:]
    x_ref, gain_ref, w_ref, kv_ref, first_ref, kept_ref, sent_ref, normed, own, *blocks, sems = refs
    rows, width = x_ref.shape
    half = rows // 2
    block = rows // count
    sub_width = width // narrow_count
    done = first_ref.shape[0]
    step = blocks[0].shape[0]
    fetches = [
        pltpu.make_async_copy(w_ref.at[done + g * step : done + (g + 1) * step], ref, sems.at[g])
        for g, ref in enumerate(blocks)
    ]
    ahead = 3
    for fetch in fetches[:ahead]:
        fetch.start()
    me, narrow = me_ref[0], me_ref[1]
    stats = stat_refs[0][...]
    for ref in stat_refs[1:]:
        stats = stats + ref[...]
    row = lax.broadcasted_iota(jnp.int32, (rows, rows), 0)
    column = lax.broadcasted_iota(jnp.int32, (rows, rows), 1)
    sums = jnp.sum(jnp.where(row == column, stats[0:1, :], 0.0), axis=1, keepdims=True)
    squares = jnp.sum(jnp.where(row == column, stats[1:2, :], 0.0), axis=1, keepdims=True)
    center = sums / width_all
    spread = squares / width_all - center * center
    inverse = lax.rsqrt(spread + 1e-05)
    gain = gain_ref[...].reshape(1, width)
    order = halving_order(count)
    for j in range(count):
        pick = slice(j * block, (j + 1) * block)
        place = jnp.int32(0)
        for k, d in enumerate(order):
            place = jnp.where((me ^ d) == j, k, place)
        place = pl.multiple_of(place * block, 16)
        scaled = (x_ref[pick, :].astype(jnp.float32) - center[pick]) * inverse[pick] * gain
        normed[pl.ds(place, block), :] = scaled.astype(jnp.bfloat16)
    for j in range(narrow_count):
        @pl.when(narrow == j)
        def _(j=j):
            own[...] = normed[:, j * sub_width : (j + 1) * sub_width]

    queries = w_ref.shape[1]

    def products(source, start):
        got = jnp.dot(normed[:, start : start + source.shape[0]], source[...], preferred_element_type=jnp.float32)
        if start:
            kept_ref[:, :queries] += got[:half, :]
            sent_ref[:, :queries] += got[half:, :]
        else:
            kept_ref[:, :queries] = got[:half, :]
            sent_ref[:, :queries] = got[half:, :]

    fresh = jnp.dot(own[...], kv_ref[...], preferred_element_type=jnp.float32)
    kept_ref[:, queries:] = fresh[:half, :]
    sent_ref[:, queries:] = fresh[half:, :]
    products(first_ref, 0)
    for g, fetch in enumerate(fetches):
        fetch.wait()
        if g + ahead < len(fetches):
            fetches[g + ahead].start()
        products(blocks[g], done + g * step)


def project(me, stats, x, gain, w, kv, first, width_all, count, narrow_count):
    rows, width = x.shape
    queries = w.shape[1]
    step = row_block(width)
    blocks = (width - first.shape[0]) // step
    half = jax.ShapeDtypeStruct((rows // 2, queries + kv.shape[1]), jnp.float32)
    return call(
        functools.partial(project_kernel, len(stats), width_all, count, narrow_count),
        (half, half),
        (me, *stats, x, gain, in_hbm(w), in_vmem(kv), in_vmem(first)),
        [SCALAR] + [FULL] * (len(stats) + 2) + [ANY] + [FULL] * 2,
        "project",
        scratch=[
            pltpu.VMEM((rows, width), jnp.bfloat16),
            pltpu.VMEM((rows, width // narrow_count), jnp.bfloat16),
            *[pltpu.VMEM((step, queries), jnp.bfloat16)] * blocks,
            pltpu.SemaphoreType.DMA((blocks,)),
        ],
        limit=32,
        flops=2 * rows * width * queries,
        moved=2 * blocks * step * queries,
    )


def fold_kernel(kept_ref, came_ref, still_ref, sent_ref):
    half = still_ref.shape[0]
    still_ref[...] = kept_ref[:half, :] + came_ref[:half, :]
    sent_ref[...] = kept_ref[half:, :] + came_ref[half:, :]


def fold(kept, came):
    half = jax.ShapeDtypeStruct((kept.shape[0] // 2, kept.shape[1]), jnp.float32)
    return call(
        fold_kernel,
        (half, half),
        (kept, came),
        [FULL] * 2,
        "fold",
        flops=BESIDE,
    )


def split_kernel(queries, me_ref, kept_ref, came_ref, *refs):
    out_refs, slots = refs[:-1], refs[-1]
    count, rows = len(out_refs), out_refs[0].shape[0]
    narrow = me_ref[1]
    total = kept_ref[...] + came_ref[...]
    for j in range(count):
        slots[j * PAD : j * PAD + rows, :] = total[j * rows : (j + 1) * rows, :]
    for d, out_ref in enumerate(out_refs):
        mine = slots[pl.ds(pl.multiple_of((narrow ^ d) * PAD, PAD), rows), :]
        high = mine.astype(jnp.bfloat16)
        out_ref[:, : mine.shape[1]] = high
        out_ref[:, mine.shape[1] :] = (mine - high.astype(jnp.float32))[:, queries:].astype(jnp.bfloat16)


def attend_kernel(head_dim, count, lengths_ref, *refs):
    came_refs, kv_ref = refs[:count][::-1], refs[count]
    refs = refs[count + 1 :]
    out_refs, (heads, contexts) = refs[:count], refs[count:]
    rows, positions = kv_ref.shape[0], kv_ref.shape[1]
    queries = out_refs[0].shape[1]
    each = queries // head_dim
    total_heads = each * count
    slabs = head_dim // LANES
    scaling = 1.0 / math.sqrt(head_dim)
    for d, ref in enumerate(came_refs):
        for h in range(each):
            at = (d * each + h) * PAD
            for k in range(slabs):
                start = h * head_dim + k * LANES
                heads[k, at : at + rows, :] = ref[:, start : start + LANES].astype(jnp.float32)
    terms = came_refs[0][:, queries:].astype(jnp.float32)
    for ref in came_refs[1:]:
        terms = terms + ref[:, queries:].astype(jnp.float32)
    pair = 2 * head_dim
    fresh = terms[:, :pair] + terms[:, pair:]
    fresh = fresh.astype(jnp.bfloat16).astype(jnp.float32)
    place = lax.broadcasted_iota(jnp.int32, (total_heads, positions), 1)
    for r in range(rows):
        query = jnp.concatenate([heads[k, pl.ds(r, total_heads, stride=PAD), :] for k in range(slabs)], axis=1)
        scores = (
            lax.dot_general(
                query.astype(jnp.bfloat16),
                kv_ref[r, :, :head_dim],
                (((1,), (1,)), ((), ())),
                preferred_element_type=jnp.float32,
            )
            * scaling
        )
        own_score = jnp.sum(query * fresh[r : r + 1, :head_dim], axis=1, keepdims=True) * scaling
        valid = place < lengths_ref[r]
        top = jnp.maximum(jnp.max(jnp.where(valid, scores, -jnp.inf), axis=1, keepdims=True), own_score)
        weights = jnp.where(valid, jnp.exp(scores - top), 0.0)
        own_weight = jnp.exp(own_score - top)
        total = jnp.sum(weights, axis=1, keepdims=True) + own_weight
        numer = jnp.dot(weights.astype(jnp.bfloat16), kv_ref[r, :, head_dim:], preferred_element_type=jnp.float32)
        numer = numer + own_weight.astype(jnp.bfloat16).astype(jnp.float32) * fresh[r : r + 1, head_dim:]
        context = numer / total
        for k in range(slabs):
            contexts[k, pl.ds(r, total_heads, stride=PAD), :] = context[:, k * LANES : (k + 1) * LANES]
    for d, ref in enumerate(out_refs):
        for h in range(each):
            at = (d * each + h) * PAD
            for k in range(slabs):
                start = h * head_dim + k * LANES
                ref[:, start : start + LANES] = contexts[k, at : at + rows, :].astype(jnp.bfloat16)


def attend(lengths, came, kv, head_dim, queries):
    rows = kv.shape[0]
    count = len(came)
    all_heads = count * queries // head_dim
    scratch = pltpu.VMEM((head_dim // LANES, all_heads * PAD, LANES), jnp.float32)
    return call(
        functools.partial(attend_kernel, head_dim, count),
        [jax.ShapeDtypeStruct((rows, queries), jnp.bfloat16)] * count,
        (lengths, *came[::-1], in_vmem(kv)),
        [SCALAR] + [FULL] * (count + 1),
        "attend",
        scratch=[scratch, scratch],
        limit=8,
        flops=BESIDE,
    )


def join_kernel(me_ref, *refs):
    count = len(refs) - 2
    out_ref, joined = refs[-2:]
    rows = refs[0].shape[0]
    for d in range(count):
        at = pl.ds(pl.multiple_of((me_ref[1] ^ d) * PAD, PAD), rows)
        joined[at, :] = refs[count - 1 - d][...].astype(jnp.float32)
    came = [joined[j * PAD : j * PAD + rows, :] for j in range(count)]
    out_ref[...] = jnp.concatenate(came, axis=0).astype(jnp.bfloat16)


def code(x, ref):
    largest = jnp.maximum(jnp.max(jnp.abs(x), axis=1, keepdims=True), TINY)
    power = jnp.floor(jnp.log2(largest)) + 1.0
    steps = jnp.round(x * (STEPS * jnp.exp2(-power)))
    ref[:, : x.shape[1]] = steps.astype(jnp.int32).astype(jnp.int16)
    ref[:, x.shape[1] :] = jnp.broadcast_to(power, (x.shape[0], LANES)).astype(jnp.int32).astype(jnp.int16)


def decode(ref, width):
    power = ref[:, width:].astype(jnp.int32).astype(jnp.float32)[:, 0:1]
    return ref[:, :width].astype(jnp.int32).astype(jnp.float32) * (jnp.exp2(power) * (1.0 / STEPS))


def output_kernel(start, count, narrow_count, me_ref, *refs):
    x_refs, w_ref, (sums_ref, sent_ref) = refs[:count], refs[count], refs[-2:]
    block = x_refs[0].shape[0]
    ratio = count // narrow_count
    places = []
    for d in range(count):
        wide = me_ref[0] ^ d
        apart = (wide // ratio) ^ me_ref[1]
        place = jnp.int32(0)
        for k, distance in enumerate(halving_order(narrow_count)):
            place = jnp.where(apart == distance, k, place)
        places.append(pl.multiple_of((place * ratio + wide % ratio) * block, block))
    x = jnp.concatenate([ref[...] for ref in x_refs], axis=0)
    got = jnp.dot(x, w_ref[:, start : start + sums_ref.shape[1]], preferred_element_type=jnp.float32)
    for d, place in enumerate(places):
        sums_ref[pl.ds(place, block), :] = got[d * block : (d + 1) * block, :]
    code(sums_ref[sums_ref.shape[0] // 2 :, :], sent_ref)


def output_part(me, blocks, w, start, columns, narrow_count, after):
    count = len(blocks)
    block, depth = blocks[0].shape
    rows = count * block
    return call(
        functools.partial(output_kernel, start, count, narrow_count),
        (
            jax.ShapeDtypeStruct((rows, columns), jnp.float32),
            jax.ShapeDtypeStruct((rows // 2, columns + LANES), jnp.int16),
        ),
        (me, *blocks, in_vmem(w), *after),
        [SCALAR] + [FULL] * (count + 1) + [ANY] * len(after),
        "output_part",
        limit=8,
        flops=2 * rows * depth * columns,
        moved=2 * rows * depth,
    )


def halve_kernel(sums_ref, came_ref, *refs):
    still_ref, sent_ref = refs[-2:]
    half = still_ref.shape[0]
    total = sums_ref[: 2 * half, :] + decode(came_ref, sums_ref.shape[1])
    still_ref[...] = total[:half, :]
    code(total[half:, :], sent_ref)


def halve(sums, came, after):
    rows, columns = came.shape[0], sums.shape[1]
    return call(
        halve_kernel,
        (
            jax.ShapeDtypeStruct((rows // 2, columns), jnp.float32),
            jax.ShapeDtypeStruct((rows // 2, columns + LANES), jnp.int16),
        ),
        (sums, came, *after),
        [FULL, FULL] + [ANY] * len(after),
        "halve",
        moved=16 * rows * columns,
    )


def finish_kernel(starts, kinds, *refs):
    out_ref = refs[-1]
    k = 0
    for at, kind in zip(starts, kinds):
        width = refs[k].shape[1]
        done = refs[k][...]
        if kind == 2:
            done = (done + decode(refs[k + 1], width)).astype(jnp.bfloat16)
        out_ref[:, at : at + width] = done
        k += kind


def finish(starts, cuts):
    parts = [x for cut in cuts for x in cut]
    rows, columns = parts[0].shape[0], sum(cut[0].shape[1] for cut in cuts)
    return call(
        functools.partial(finish_kernel, starts, [len(cut) for cut in cuts]),
        jax.ShapeDtypeStruct((rows, columns), jnp.bfloat16),
        parts,
        [FULL] * len(parts),
        "finish",
        moved=8 * columns * rows,
    )


def local(activations, norm_gain, query_weight, kv_weight, out_weight, kv_cache, lengths):
    wide_count = lax.axis_size("wide")
    narrow_count = lax.axis_size("narrow")
    me = jnp.stack([lax.axis_index("wide"), lax.axis_index("narrow")]).astype(jnp.int32)
    own_rows, head_dim = kv_cache.shape[0], kv_cache.shape[2] // 2
    rows, width = activations.shape
    queries = query_weight.shape[1]
    columns = out_weight.shape[1]
    values = activations.astype(jnp.float32)
    stats = jnp.stack([jnp.sum(values, axis=1), jnp.sum(values * values, axis=1)])
    step = row_block(width)
    first_part, kv_part = fetch(query_weight, kv_weight, width // step // 3 * step, [stats, me])
    kept, sent = project(
        me,
        sent_apart(stats, "wide"),
        activations,
        norm_gain,
        query_weight,
        kv_part,
        first_part,
        width * wide_count,
        wide_count,
        narrow_count,
    )
    d = 1
    while 2 * d < wide_count:
        kept, sent = fold(kept, swap(sent, "wide", d))
        d *= 2
    split = call(
        functools.partial(split_kernel, queries),
        [jax.ShapeDtypeStruct((own_rows, queries + 4 * head_dim), jnp.bfloat16)] * narrow_count,
        (me, kept, swap(sent, "wide", d)),
        [SCALAR] + [FULL] * 2,
        "split",
        scratch=[pltpu.VMEM((narrow_count * PAD, queries + 2 * head_dim), jnp.float32)],
        flops=BESIDE,
    )
    context = attend(lengths, exchange(split, "narrow"), kv_cache, head_dim, queries)
    returned = call(
        join_kernel,
        jax.ShapeDtypeStruct((narrow_count * own_rows, queries), jnp.bfloat16),
        (me, *exchange(context, "narrow")[::-1]),
        [SCALAR] + [FULL] * narrow_count,
        "join",
        scratch=[pltpu.VMEM((narrow_count * PAD, queries), jnp.float32)],
        flops=BESIDE,
    )
    gathered = gather(returned, "wide")
    ends = [columns // LANES * k // 18 * LANES for k in (0,7,15,18)]
    cut_sums, halved, last = [], [], []

    def exchange_cut(kept, sent, after):
        d = 1
        while 2 * d < narrow_count:
            kept, sent = halve(kept, swap(sent, "narrow", d), after)
            after = []
            d *= 2
        halved.append(kept)
        cut_sums.append((kept, swap(sent, "narrow", d)))

    for start, end in zip(ends, ends[1:]):
        kept, sent = output_part(me, gathered, out_weight, start, end - start, narrow_count, halved[-1:])
        if last:
            exchange_cut(*last, [kept])
        last = (kept, sent)
    early = finish([0], cut_sums[:1])
    exchange_cut(*last, [early])
    cut_sums[0] = (early,)
    return finish(ends[:-1], cut_sums)


def solution(mesh):
    return jax.shard_map(
        local,
        mesh=mesh,
        in_specs=(
            P("groups", "wide"),
            P("wide"),
            P("wide", "narrow"),
            P(("wide", "narrow"), None),
            P("narrow", "wide"),
            P(("groups", "wide", "narrow"), None, None),
            P(("groups", "wide", "narrow")),
        ),
        out_specs=P(("groups", "narrow"), "wide"),
        check_vma=False,
    )
```

```python
import functools
import math

import jax
import jax.numpy as jnp
from jax import lax
from jax.experimental import pallas as pl
from jax.experimental.pallas import tpu as pltpu
from jax.sharding import PartitionSpec as P

MIB = 1 << 20
FULL = pl.BlockSpec(memory_space=pltpu.VMEM)
ANY = pl.BlockSpec(memory_space=pl.ANY)
SCALAR = pl.BlockSpec(memory_space=pltpu.SMEM)
STEPS = 32700.0
TINY = 1e-37
LANES = 128
PAD = 8
PIECES = 4
BESIDE = 5 * 10**9


def call(kernel, outs, ins, specs, name, scratch=(), limit=4, flops=0, moved=0):
    return pl.pallas_call(
        kernel,
        out_shape=outs,
        in_specs=specs,
        out_specs=jax.tree.map(lambda _: FULL, outs),
        scratch_shapes=list(scratch),
        compiler_params=pltpu.CompilerParams(vmem_limit_bytes=limit * MIB),
        cost_estimate=pl.CostEstimate(flops=flops, bytes_accessed=moved, transcendentals=0),
        name=name,
    )(*ins)


def held(shape, dtype):
    return pltpu.VMEM(shape, dtype)


def in_vmem(x):
    return pltpu.with_memory_space_constraint(x, pltpu.VMEM)


def in_hbm(x):
    return pltpu.with_memory_space_constraint(x, pltpu.HBM)


def swap(x, axis, distance):
    count = lax.axis_size(axis)
    return lax.ppermute(x, axis, [(i, i ^ distance) for i in range(count)])


def sent_apart(x, axis):
    count = lax.axis_size(axis)
    if count <= 4:
        return [x] + [swap(x, axis, d) for d in range(1, count)]
    d = 1
    while d < count:
        x = x + swap(x, axis, d)
        d *= 2
    return [x]


def exchange(blocks, axis):
    far_first = {d: swap(blocks[d], axis, d) for d in range(len(blocks) - 1, 0, -1)}
    return [blocks[0]] + [far_first[d] for d in range(1, len(blocks))]


def gather(x, axis):
    count = lax.axis_size(axis)
    blocks = {0: x}
    d = count // 2
    while d:
        blocks |= {k ^ d: swap(b, axis, d) for k, b in blocks.items()}
        d //= 2
    return [blocks[k] for k in range(count)]


def halving_order(count):
    bits = count.bit_length() - 1
    return [sum(((k >> b) & 1) << (bits - 1 - b) for b in range(bits)) for k in range(count)]


def stats_kernel(me_ref, x_ref, w_ref, out_ref, share_ref, copied, sems):
    rows, width = x_ref.shape
    step = rows // PIECES
    pieces = [pl.ds(p * step, step) for p in range(PIECES)]
    copies = [pltpu.make_async_copy(x_ref.at[at], copied.at[at], sems.at[p]) for p, at in enumerate(pieces)]
    for copy in copies:
        copy.start()
    fetch = pltpu.make_async_copy(w_ref.at[: share_ref.shape[0]], share_ref, sems.at[PIECES])
    fetch.start()
    totals, squares = [], []
    for copy, at in zip(copies, pieces):
        copy.wait()
        total = jnp.zeros((step, LANES), jnp.float32)
        square = jnp.zeros((step, LANES), jnp.float32)
        for c in range(0, width, LANES):
            part = copied[at, c : c + LANES].astype(jnp.float32)
            total += part
            square += part * part
        totals.append(jnp.sum(total, axis=1, keepdims=True))
        squares.append(jnp.sum(square, axis=1, keepdims=True))
    row = lax.broadcasted_iota(jnp.int32, (rows, rows), 0)
    column = lax.broadcasted_iota(jnp.int32, (rows, rows), 1)
    for k, sums in enumerate((totals, squares)):
        sums = jnp.where(row == column, jnp.concatenate(sums, axis=0), 0.0)
        out_ref[k : k + 1, :] = jnp.sum(sums, axis=0, keepdims=True)
    fetch.wait()


def row_sums(me, x, w, share):
    return call(
        stats_kernel,
        (jax.ShapeDtypeStruct((2, x.shape[0]), jnp.float32), held((share, w.shape[1]), w.dtype)),
        (me, in_hbm(x), in_hbm(w)),
        [SCALAR, ANY, ANY],
        "row_sums",
        scratch=[pltpu.VMEM(x.shape, x.dtype), pltpu.SemaphoreType.DMA((PIECES + 1,))],
        moved=2 * share * w.shape[1],
    )


def row_block(rows):
    return LANES * max(1, rows // LANES // 6)


def project_kernel(many, width_all, count, narrow_count, me_ref, *refs):
    stat_refs, refs = refs[:many], refs[many:]
    x_ref, gain_ref, w_ref, kv_ref, first_ref, kept_ref, sent_ref, normed, own, *blocks, sems = refs
    rows, width = x_ref.shape
    half = rows // 2
    block = rows // count
    sub_width = width // narrow_count
    done = first_ref.shape[0]
    step = blocks[0].shape[0]
    fetches = [
        pltpu.make_async_copy(w_ref.at[done + g * step : done + (g + 1) * step], ref, sems.at[g])
        for g, ref in enumerate(blocks)
    ]
    ahead = 3
    for fetch in fetches[:ahead]:
        fetch.start()
    me, narrow = me_ref[0], me_ref[1]
    stats = stat_refs[0][...]
    for ref in stat_refs[1:]:
        stats = stats + ref[...]
    row = lax.broadcasted_iota(jnp.int32, (rows, rows), 0)
    column = lax.broadcasted_iota(jnp.int32, (rows, rows), 1)
    sums = jnp.sum(jnp.where(row == column, stats[0:1, :], 0.0), axis=1, keepdims=True)
    squares = jnp.sum(jnp.where(row == column, stats[1:2, :], 0.0), axis=1, keepdims=True)
    center = sums / width_all
    spread = squares / width_all - center * center
    inverse = lax.rsqrt(spread + 1e-05)
    gain = gain_ref[...].reshape(1, width)
    order = halving_order(count)
    for j in range(count):
        pick = slice(j * block, (j + 1) * block)
        place = jnp.int32(0)
        for k, d in enumerate(order):
            place = jnp.where((me ^ d) == j, k, place)
        place = pl.multiple_of(place * block, 16)
        scaled = (x_ref[pick, :].astype(jnp.float32) - center[pick]) * inverse[pick] * gain
        normed[pl.ds(place, block), :] = scaled.astype(jnp.bfloat16)
    for j in range(narrow_count):
        @pl.when(narrow == j)
        def _(j=j):
            own[...] = normed[:, j * sub_width : (j + 1) * sub_width]

    queries = w_ref.shape[1]

    def products(source, start):
        got = jnp.dot(normed[:, start : start + source.shape[0]], source[...], preferred_element_type=jnp.float32)
        if start:
            kept_ref[:, :queries] += got[:half, :]
            sent_ref[:, :queries] += got[half:, :]
        else:
            kept_ref[:, :queries] = got[:half, :]
            sent_ref[:, :queries] = got[half:, :]

    fresh = jnp.dot(own[...], kv_ref[...], preferred_element_type=jnp.float32)
    kept_ref[:, queries:] = fresh[:half, :]
    sent_ref[:, queries:] = fresh[half:, :]
    products(first_ref, 0)
    for g, fetch in enumerate(fetches):
        fetch.wait()
        if g + ahead < len(fetches):
            fetches[g + ahead].start()
        products(blocks[g], done + g * step)


def project(me, stats, x, gain, w, kv, first, width_all, count, narrow_count):
    rows, width = x.shape
    queries = w.shape[1]
    step = row_block(width)
    blocks = (width - first.shape[0]) // step
    half = jax.ShapeDtypeStruct((rows // 2, queries + kv.shape[1]), jnp.float32)
    return call(
        functools.partial(project_kernel, len(stats), width_all, count, narrow_count),
        (half, half),
        (me, *stats, x, gain, in_hbm(w), in_vmem(kv), in_vmem(first)),
        [SCALAR] + [FULL] * (len(stats) + 2) + [ANY] + [FULL] * 2,
        "project",
        scratch=[
            pltpu.VMEM((rows, width), jnp.bfloat16),
            pltpu.VMEM((rows, width // narrow_count), jnp.bfloat16),
            *[pltpu.VMEM((step, queries), jnp.bfloat16)] * blocks,
            pltpu.SemaphoreType.DMA((blocks,)),
        ],
        limit=32,
        flops=2 * rows * width * queries,
        moved=2 * blocks * step * queries,
    )


def fold_kernel(kept_ref, came_ref, still_ref, sent_ref):
    half = still_ref.shape[0]
    still_ref[...] = kept_ref[:half, :] + came_ref[:half, :]
    sent_ref[...] = kept_ref[half:, :] + came_ref[half:, :]


def fold(kept, came):
    half = jax.ShapeDtypeStruct((kept.shape[0] // 2, kept.shape[1]), jnp.float32)
    return call(
        fold_kernel,
        (half, half),
        (kept, came),
        [FULL] * 2,
        "fold",
        flops=BESIDE,
    )


def split_kernel(queries, me_ref, kept_ref, came_ref, *refs):
    out_refs, slots = refs[:-1], refs[-1]
    count, rows = len(out_refs), out_refs[0].shape[0]
    narrow = me_ref[1]
    total = kept_ref[...] + came_ref[...]
    for j in range(count):
        slots[j * PAD : j * PAD + rows, :] = total[j * rows : (j + 1) * rows, :]
    for d, out_ref in enumerate(out_refs):
        mine = slots[pl.ds(pl.multiple_of((narrow ^ d) * PAD, PAD), rows), :]
        high = mine.astype(jnp.bfloat16)
        out_ref[:, : mine.shape[1]] = high
        out_ref[:, mine.shape[1] :] = (mine - high.astype(jnp.float32))[:, queries:].astype(jnp.bfloat16)


def attend_kernel(head_dim, count, lengths_ref, *refs):
    came_refs, kv_ref = refs[:count][::-1], refs[count]
    refs = refs[count + 1 :]
    out_refs, (heads, contexts) = refs[:count], refs[count:]
    rows, positions = kv_ref.shape[0], kv_ref.shape[1]
    queries = out_refs[0].shape[1]
    each = queries // head_dim
    total_heads = each * count
    slabs = head_dim // LANES
    scaling = 1.0 / math.sqrt(head_dim)
    for d, ref in enumerate(came_refs):
        for h in range(each):
            at = (d * each + h) * PAD
            for k in range(slabs):
                start = h * head_dim + k * LANES
                heads[k, at : at + rows, :] = ref[:, start : start + LANES].astype(jnp.float32)
    terms = came_refs[0][:, queries:].astype(jnp.float32)
    for ref in came_refs[1:]:
        terms = terms + ref[:, queries:].astype(jnp.float32)
    pair = 2 * head_dim
    fresh = terms[:, :pair] + terms[:, pair:]
    fresh = fresh.astype(jnp.bfloat16).astype(jnp.float32)
    place = lax.broadcasted_iota(jnp.int32, (total_heads, positions), 1)
    for r in range(rows):
        query = jnp.concatenate([heads[k, pl.ds(r, total_heads, stride=PAD), :] for k in range(slabs)], axis=1)
        scores = (
            lax.dot_general(
                query.astype(jnp.bfloat16),
                kv_ref[r, :, :head_dim],
                (((1,), (1,)), ((), ())),
                preferred_element_type=jnp.float32,
            )
            * scaling
        )
        own_score = jnp.sum(query * fresh[r : r + 1, :head_dim], axis=1, keepdims=True) * scaling
        valid = place < lengths_ref[r]
        top = jnp.maximum(jnp.max(jnp.where(valid, scores, -jnp.inf), axis=1, keepdims=True), own_score)
        weights = jnp.where(valid, jnp.exp(scores - top), 0.0)
        own_weight = jnp.exp(own_score - top)
        total = jnp.sum(weights, axis=1, keepdims=True) + own_weight
        numer = jnp.dot(weights.astype(jnp.bfloat16), kv_ref[r, :, head_dim:], preferred_element_type=jnp.float32)
        numer = numer + own_weight.astype(jnp.bfloat16).astype(jnp.float32) * fresh[r : r + 1, head_dim:]
        context = numer / total
        for k in range(slabs):
            contexts[k, pl.ds(r, total_heads, stride=PAD), :] = context[:, k * LANES : (k + 1) * LANES]
    for d, ref in enumerate(out_refs):
        for h in range(each):
            at = (d * each + h) * PAD
            for k in range(slabs):
                start = h * head_dim + k * LANES
                ref[:, start : start + LANES] = contexts[k, at : at + rows, :].astype(jnp.bfloat16)


def attend(lengths, came, kv, head_dim, queries):
    rows = kv.shape[0]
    count = len(came)
    all_heads = count * queries // head_dim
    scratch = pltpu.VMEM((head_dim // LANES, all_heads * PAD, LANES), jnp.float32)
    return call(
        functools.partial(attend_kernel, head_dim, count),
        [jax.ShapeDtypeStruct((rows, queries), jnp.bfloat16)] * count,
        (lengths, *came[::-1], in_vmem(kv)),
        [SCALAR] + [FULL] * (count + 1),
        "attend",
        scratch=[scratch, scratch],
        limit=8,
        flops=BESIDE,
    )


def join_kernel(me_ref, *refs):
    count = len(refs) - 2
    out_ref, joined = refs[-2:]
    rows = refs[0].shape[0]
    for d in range(count):
        at = pl.ds(pl.multiple_of((me_ref[1] ^ d) * PAD, PAD), rows)
        joined[at, :] = refs[count - 1 - d][...].astype(jnp.float32)
    came = [joined[j * PAD : j * PAD + rows, :] for j in range(count)]
    out_ref[...] = jnp.concatenate(came, axis=0).astype(jnp.bfloat16)


def code(x, ref):
    largest = jnp.maximum(jnp.max(jnp.abs(x), axis=1, keepdims=True), TINY)
    power = jnp.floor(jnp.log2(largest)) + 1.0
    steps = jnp.round(x * (STEPS * jnp.exp2(-power)))
    ref[:, : x.shape[1]] = steps.astype(jnp.int32).astype(jnp.int16)
    ref[:, x.shape[1] :] = jnp.broadcast_to(power, (x.shape[0], LANES)).astype(jnp.int32).astype(jnp.int16)


def decode(ref, width):
    power = ref[:, width:].astype(jnp.int32).astype(jnp.float32)[:, 0:1]
    return ref[:, :width].astype(jnp.int32).astype(jnp.float32) * (jnp.exp2(power) * (1.0 / STEPS))


def output_kernel(start, count, narrow_count, me_ref, *refs):
    x_refs, w_ref, (sums_ref, sent_ref) = refs[:count], refs[count], refs[-2:]
    block = x_refs[0].shape[0]
    ratio = count // narrow_count
    places = []
    for d in range(count):
        wide = me_ref[0] ^ d
        apart = (wide // ratio) ^ me_ref[1]
        place = jnp.int32(0)
        for k, distance in enumerate(halving_order(narrow_count)):
            place = jnp.where(apart == distance, k, place)
        places.append(pl.multiple_of((place * ratio + wide % ratio) * block, block))
    x = jnp.concatenate([ref[...] for ref in x_refs], axis=0)
    got = jnp.dot(x, w_ref[:, start : start + sums_ref.shape[1]], preferred_element_type=jnp.float32)
    for d, place in enumerate(places):
        sums_ref[pl.ds(place, block), :] = got[d * block : (d + 1) * block, :]
    code(sums_ref[sums_ref.shape[0] // 2 :, :], sent_ref)


def output_part(me, blocks, w, start, columns, narrow_count, after):
    count = len(blocks)
    block, depth = blocks[0].shape
    rows = count * block
    return call(
        functools.partial(output_kernel, start, count, narrow_count),
        (
            jax.ShapeDtypeStruct((rows, columns), jnp.float32),
            jax.ShapeDtypeStruct((rows // 2, columns + LANES), jnp.int16),
        ),
        (me, *blocks, in_vmem(w), *after),
        [SCALAR] + [FULL] * (count + 1) + [ANY] * len(after),
        "output_part",
        limit=8,
        flops=2 * rows * depth * columns,
        moved=2 * rows * depth,
    )


def halve_kernel(sums_ref, came_ref, *refs):
    still_ref, sent_ref = refs[-2:]
    half = still_ref.shape[0]
    total = sums_ref[: 2 * half, :] + decode(came_ref, sums_ref.shape[1])
    still_ref[...] = total[:half, :]
    code(total[half:, :], sent_ref)


def halve(sums, came, after):
    rows, columns = came.shape[0], sums.shape[1]
    return call(
        halve_kernel,
        (
            jax.ShapeDtypeStruct((rows // 2, columns), jnp.float32),
            jax.ShapeDtypeStruct((rows // 2, columns + LANES), jnp.int16),
        ),
        (sums, came, *after),
        [FULL, FULL] + [ANY] * len(after),
        "halve",
        moved=16 * rows * columns,
    )


def finish_kernel(starts, kinds, *refs):
    out_ref = refs[-1]
    k = 0
    for at, kind in zip(starts, kinds):
        width = refs[k].shape[1]
        done = refs[k][...]
        if kind == 2:
            done = (done + decode(refs[k + 1], width)).astype(jnp.bfloat16)
        out_ref[:, at : at + width] = done
        k += kind


def finish(starts, cuts):
    parts = [x for cut in cuts for x in cut]
    rows, columns = parts[0].shape[0], sum(cut[0].shape[1] for cut in cuts)
    return call(
        functools.partial(finish_kernel, starts, [len(cut) for cut in cuts]),
        jax.ShapeDtypeStruct((rows, columns), jnp.bfloat16),
        parts,
        [FULL] * len(parts),
        "finish",
        moved=8 * columns * rows,
    )


def local(activations, norm_gain, query_weight, kv_weight, out_weight, kv_cache, lengths):
    wide_count = lax.axis_size("wide")
    narrow_count = lax.axis_size("narrow")
    me = jnp.stack([lax.axis_index("wide"), lax.axis_index("narrow")]).astype(jnp.int32)
    own_rows, head_dim = kv_cache.shape[0], kv_cache.shape[2] // 2
    rows, width = activations.shape
    queries = query_weight.shape[1]
    columns = out_weight.shape[1]
    step = row_block(width)
    stats, first_part = row_sums(me, activations, query_weight, width // step // 3 * step)
    kept, sent = project(
        me,
        sent_apart(stats, "wide"),
        activations,
        norm_gain,
        query_weight,
        kv_weight,
        first_part,
        width * wide_count,
        wide_count,
        narrow_count,
    )
    d = 1
    while 2 * d < wide_count:
        kept, sent = fold(kept, swap(sent, "wide", d))
        d *= 2
    split = call(
        functools.partial(split_kernel, queries),
        [jax.ShapeDtypeStruct((own_rows, queries + 4 * head_dim), jnp.bfloat16)] * narrow_count,
        (me, kept, swap(sent, "wide", d)),
        [SCALAR] + [FULL] * 2,
        "split",
        scratch=[pltpu.VMEM((narrow_count * PAD, queries + 2 * head_dim), jnp.float32)],
        flops=BESIDE,
    )
    context = attend(lengths, exchange(split, "narrow"), kv_cache, head_dim, queries)
    returned = call(
        join_kernel,
        jax.ShapeDtypeStruct((narrow_count * own_rows, queries), jnp.bfloat16),
        (me, *exchange(context, "narrow")[::-1]),
        [SCALAR] + [FULL] * narrow_count,
        "join",
        scratch=[pltpu.VMEM((narrow_count * PAD, queries), jnp.float32)],
        flops=BESIDE,
    )
    gathered = gather(returned, "wide")
    ends = [columns // LANES * k // 18 * LANES for k in (0,7,15,18)]
    cut_sums, halved, last = [], [], []

    def exchange_cut(kept, sent, after):
        d = 1
        while 2 * d < narrow_count:
            kept, sent = halve(kept, swap(sent, "narrow", d), after)
            after = []
            d *= 2
        halved.append(kept)
        cut_sums.append((kept, swap(sent, "narrow", d)))

    for start, end in zip(ends, ends[1:]):
        kept, sent = output_part(me, gathered, out_weight, start, end - start, narrow_count, halved[-1:])
        if last:
            exchange_cut(*last, [kept])
        last = (kept, sent)
    early = finish([0], cut_sums[:1])
    exchange_cut(*last, [early])
    cut_sums[0] = (early,)
    return finish(ends[:-1], cut_sums)


def solution(mesh):
    return jax.shard_map(
        local,
        mesh=mesh,
        in_specs=(
            P("groups", "wide"),
            P("wide"),
            P("wide", "narrow"),
            P(("wide", "narrow"), None),
            P("narrow", "wide"),
            P(("groups", "wide", "narrow"), None, None),
            P(("groups", "wide", "narrow")),
        ),
        out_specs=P(("groups", "narrow"), "wide"),
        check_vma=False,
    )
```

```python
import functools
import math

import jax
import jax.numpy as jnp
from jax import lax
from jax.experimental import pallas as pl
from jax.experimental.pallas import tpu as pltpu
from jax.sharding import PartitionSpec as P

MIB = 1 << 20
FULL = pl.BlockSpec(memory_space=pltpu.VMEM)
ANY = pl.BlockSpec(memory_space=pl.ANY)
SCALAR = pl.BlockSpec(memory_space=pltpu.SMEM)
STEPS = 32700.0
TINY = 1e-37
LANES = 128
PAD = 8
BESIDE = 5 * 10**9


def call(kernel, outs, ins, specs, name, scratch=(), limit=4, flops=0, moved=0):
    return pl.pallas_call(
        kernel,
        out_shape=outs,
        in_specs=specs,
        out_specs=jax.tree.map(lambda _: FULL, outs),
        scratch_shapes=list(scratch),
        compiler_params=pltpu.CompilerParams(vmem_limit_bytes=limit * MIB),
        cost_estimate=pl.CostEstimate(flops=flops, bytes_accessed=moved, transcendentals=0),
        name=name,
    )(*ins)


def held(shape, dtype):
    return pltpu.VMEM(shape, dtype)


def in_vmem(x):
    return pltpu.with_memory_space_constraint(x, pltpu.VMEM)


def in_hbm(x):
    return pltpu.with_memory_space_constraint(x, pltpu.HBM)


def swap(x, axis, distance):
    count = lax.axis_size(axis)
    return lax.ppermute(x, axis, [(i, i ^ distance) for i in range(count)])


def sent_apart(x, axis):
    count = lax.axis_size(axis)
    if count <= 4:
        return [x] + [swap(x, axis, d) for d in range(1, count)]
    d = 1
    while d < count:
        x = x + swap(x, axis, d)
        d *= 2
    return [x]


def exchange(blocks, axis):
    far_first = {d: swap(blocks[d], axis, d) for d in range(len(blocks) - 1, 0, -1)}
    return [blocks[0]] + [far_first[d] for d in range(1, len(blocks))]


def gather(x, axis):
    count = lax.axis_size(axis)
    blocks = {0: x}
    d = count // 2
    while d:
        blocks |= {k ^ d: swap(b, axis, d) for k, b in blocks.items()}
        d //= 2
    return [blocks[k] for k in range(count)]


def halving_order(count):
    bits = count.bit_length() - 1
    return [sum(((k >> b) & 1) << (bits - 1 - b) for b in range(bits)) for k in range(count)]


def fetch_kernel(w_ref, *refs):
    share_ref, sem = refs[-2:]
    fetch = pltpu.make_async_copy(w_ref.at[: share_ref.shape[0]], share_ref, sem)
    fetch.start()
    fetch.wait()


def fetch(w, rows, after):
    return call(
        fetch_kernel,
        held((rows, w.shape[1]), w.dtype),
        (in_hbm(w), *after),
        [ANY] * (1 + len(after)),
        "fetch_query_weight",
        scratch=[pltpu.SemaphoreType.DMA],
        moved=2 * rows * w.shape[1],
    )


def row_blocks(rows):
    tiles = rows // LANES
    step = max(1, tiles // 6)
    blocks = [step]
    while tiles - sum(blocks) > step:
        blocks.append(step)
    last = tiles - sum(blocks)
    blocks += [last - last // 3, last // 3] if last > 2 else [last]
    return [LANES * n for n in blocks]


def project_kernel(many, width_all, count, narrow_count, me_ref, *refs):
    stat_refs, refs = refs[:many], refs[many:]
    x_ref, gain_ref, w_ref, kv_ref, first_ref, kept_ref, sent_ref, normed, own, *blocks, sems = refs
    rows, width = x_ref.shape
    half = rows // 2
    block = rows // count
    sub_width = width // narrow_count
    sizes = [ref.shape[0] for ref in (first_ref, *blocks)]
    starts = [sum(sizes[:g]) for g in range(len(sizes))]
    fetches = [
        pltpu.make_async_copy(w_ref.at[start : start + size], ref, sems.at[g])
        for g, (start, size, ref) in enumerate(zip(starts[1:], sizes[1:], blocks))
    ]
    ahead = 3
    for fetch in fetches[:ahead]:
        fetch.start()
    me, narrow = me_ref[0], me_ref[1]
    stats = stat_refs[0][...]
    for ref in stat_refs[1:]:
        stats = stats + ref[...]
    row = lax.broadcasted_iota(jnp.int32, (rows, rows), 0)
    column = lax.broadcasted_iota(jnp.int32, (rows, rows), 1)
    sums = jnp.sum(jnp.where(row == column, stats[0:1, :], 0.0), axis=1, keepdims=True)
    squares = jnp.sum(jnp.where(row == column, stats[1:2, :], 0.0), axis=1, keepdims=True)
    center = sums / width_all
    spread = squares / width_all - center * center
    inverse = lax.rsqrt(spread + 1e-05)
    gain = gain_ref[...].reshape(1, width)
    order = halving_order(count)
    for j in range(count):
        pick = slice(j * block, (j + 1) * block)
        place = jnp.int32(0)
        for k, d in enumerate(order):
            place = jnp.where((me ^ d) == j, k, place)
        place = pl.multiple_of(place * block, 16)
        scaled = (x_ref[pick, :].astype(jnp.float32) - center[pick]) * inverse[pick] * gain
        normed[pl.ds(place, block), :] = scaled.astype(jnp.bfloat16)
    for j in range(narrow_count):
        @pl.when(narrow == j)
        def _(j=j):
            own[...] = normed[:, j * sub_width : (j + 1) * sub_width]

    queries = w_ref.shape[1]

    def products(source, start):
        got = jnp.dot(normed[:, start : start + source.shape[0]], source[...], preferred_element_type=jnp.float32)
        if start:
            kept_ref[:, :queries] += got[:half, :]
            sent_ref[:, :queries] += got[half:, :]
        else:
            kept_ref[:, :queries] = got[:half, :]
            sent_ref[:, :queries] = got[half:, :]

    fresh = jnp.dot(own[...], kv_ref[...], preferred_element_type=jnp.float32)
    kept_ref[:, queries:] = fresh[:half, :]
    sent_ref[:, queries:] = fresh[half:, :]
    products(first_ref, 0)
    for g, fetch in enumerate(fetches):
        fetch.wait()
        if g + ahead < len(fetches):
            fetches[g + ahead].start()
        products(blocks[g], starts[g + 1])


def project(me, stats, x, gain, w, kv, first, width_all, count, narrow_count):
    rows, width = x.shape
    queries = w.shape[1]
    blocks = row_blocks(width)[1:]
    half = jax.ShapeDtypeStruct((rows // 2, queries + kv.shape[1]), jnp.float32)
    return call(
        functools.partial(project_kernel, len(stats), width_all, count, narrow_count),
        (half, half),
        (me, *stats, x, gain, in_hbm(w), in_vmem(kv), in_vmem(first)),
        [SCALAR] + [FULL] * (len(stats) + 2) + [ANY] + [FULL] * 2,
        "project",
        scratch=[
            pltpu.VMEM((rows, width), jnp.bfloat16),
            pltpu.VMEM((rows, width // narrow_count), jnp.bfloat16),
            *[pltpu.VMEM((n, queries), jnp.bfloat16) for n in blocks],
            pltpu.SemaphoreType.DMA((len(blocks),)),
        ],
        limit=36,
        flops=2 * rows * width * queries,
        moved=2 * sum(blocks) * queries,
    )


def fold_kernel(kept_ref, came_ref, still_ref, sent_ref):
    half = still_ref.shape[0]
    still_ref[...] = kept_ref[:half, :] + came_ref[:half, :]
    sent_ref[...] = kept_ref[half:, :] + came_ref[half:, :]


def fold(kept, came):
    half = jax.ShapeDtypeStruct((kept.shape[0] // 2, kept.shape[1]), jnp.float32)
    return call(
        fold_kernel,
        (half, half),
        (kept, came),
        [FULL] * 2,
        "fold",
        flops=BESIDE,
    )


def split_kernel(queries, me_ref, kept_ref, came_ref, *refs):
    out_refs, slots = refs[:-1], refs[-1]
    count, rows = len(out_refs), out_refs[0].shape[0]
    narrow = me_ref[1]
    total = kept_ref[...] + came_ref[...]
    for j in range(count):
        slots[j * PAD : j * PAD + rows, :] = total[j * rows : (j + 1) * rows, :]
    for d, out_ref in enumerate(out_refs):
        mine = slots[pl.ds(pl.multiple_of((narrow ^ d) * PAD, PAD), rows), :]
        high = mine.astype(jnp.bfloat16)
        out_ref[:, : mine.shape[1]] = high
        out_ref[:, mine.shape[1] :] = (mine - high.astype(jnp.float32))[:, queries:].astype(jnp.bfloat16)


def attend_kernel(head_dim, count, lengths_ref, *refs):
    came_refs, kv_ref = refs[:count][::-1], refs[count]
    refs = refs[count + 1 :]
    out_refs, (heads, contexts) = refs[:count], refs[count:]
    rows, positions = kv_ref.shape[0], kv_ref.shape[1]
    queries = out_refs[0].shape[1]
    each = queries // head_dim
    total_heads = each * count
    slabs = head_dim // LANES
    scaling = 1.0 / math.sqrt(head_dim)
    for d, ref in enumerate(came_refs):
        for h in range(each):
            at = (d * each + h) * PAD
            for k in range(slabs):
                start = h * head_dim + k * LANES
                heads[k, at : at + rows, :] = ref[:, start : start + LANES].astype(jnp.float32)
    terms = came_refs[0][:, queries:].astype(jnp.float32)
    for ref in came_refs[1:]:
        terms = terms + ref[:, queries:].astype(jnp.float32)
    pair = 2 * head_dim
    fresh = terms[:, :pair] + terms[:, pair:]
    fresh = fresh.astype(jnp.bfloat16).astype(jnp.float32)
    place = lax.broadcasted_iota(jnp.int32, (total_heads, positions), 1)
    for r in range(rows):
        query = jnp.concatenate([heads[k, pl.ds(r, total_heads, stride=PAD), :] for k in range(slabs)], axis=1)
        scores = (
            lax.dot_general(
                query.astype(jnp.bfloat16),
                kv_ref[r, :, :head_dim],
                (((1,), (1,)), ((), ())),
                preferred_element_type=jnp.float32,
            )
            * scaling
        )
        own_score = jnp.sum(query * fresh[r : r + 1, :head_dim], axis=1, keepdims=True) * scaling
        valid = place < lengths_ref[r]
        top = jnp.maximum(jnp.max(jnp.where(valid, scores, -jnp.inf), axis=1, keepdims=True), own_score)
        weights = jnp.where(valid, jnp.exp(scores - top), 0.0)
        own_weight = jnp.exp(own_score - top)
        total = jnp.sum(weights, axis=1, keepdims=True) + own_weight
        numer = jnp.dot(weights.astype(jnp.bfloat16), kv_ref[r, :, head_dim:], preferred_element_type=jnp.float32)
        numer = numer + own_weight.astype(jnp.bfloat16).astype(jnp.float32) * fresh[r : r + 1, head_dim:]
        context = numer / total
        for k in range(slabs):
            contexts[k, pl.ds(r, total_heads, stride=PAD), :] = context[:, k * LANES : (k + 1) * LANES]
    for d, ref in enumerate(out_refs):
        for h in range(each):
            at = (d * each + h) * PAD
            for k in range(slabs):
                start = h * head_dim + k * LANES
                ref[:, start : start + LANES] = contexts[k, at : at + rows, :].astype(jnp.bfloat16)


def attend(lengths, came, kv, head_dim, queries):
    rows = kv.shape[0]
    count = len(came)
    all_heads = count * queries // head_dim
    scratch = pltpu.VMEM((head_dim // LANES, all_heads * PAD, LANES), jnp.float32)
    return call(
        functools.partial(attend_kernel, head_dim, count),
        [jax.ShapeDtypeStruct((rows, queries), jnp.bfloat16)] * count,
        (lengths, *came[::-1], in_vmem(kv)),
        [SCALAR] + [FULL] * (count + 1),
        "attend",
        scratch=[scratch, scratch],
        limit=8,
        flops=BESIDE,
    )


def join_kernel(me_ref, *refs):
    count = len(refs) - 2
    out_ref, joined = refs[-2:]
    rows = refs[0].shape[0]
    for d in range(count):
        at = pl.ds(pl.multiple_of((me_ref[1] ^ d) * PAD, PAD), rows)
        joined[at, :] = refs[count - 1 - d][...].astype(jnp.float32)
    came = [joined[j * PAD : j * PAD + rows, :] for j in range(count)]
    out_ref[...] = jnp.concatenate(came, axis=0).astype(jnp.bfloat16)


def code(x, ref):
    largest = jnp.maximum(jnp.max(jnp.abs(x), axis=1, keepdims=True), TINY)
    power = jnp.floor(jnp.log2(largest)) + 1.0
    steps = jnp.round(x * (STEPS * jnp.exp2(-power)))
    ref[:, : x.shape[1]] = steps.astype(jnp.int32).astype(jnp.int16)
    ref[:, x.shape[1] :] = jnp.broadcast_to(power, (x.shape[0], LANES)).astype(jnp.int32).astype(jnp.int16)


def decode(ref, width):
    power = ref[:, width:].astype(jnp.int32).astype(jnp.float32)[:, 0:1]
    return ref[:, :width].astype(jnp.int32).astype(jnp.float32) * (jnp.exp2(power) * (1.0 / STEPS))


def output_kernel(start, count, narrow_count, me_ref, *refs):
    x_refs, w_ref, (sums_ref, sent_ref) = refs[:count], refs[count], refs[-2:]
    block = x_refs[0].shape[0]
    ratio = count // narrow_count
    places = []
    for d in range(count):
        wide = me_ref[0] ^ d
        apart = (wide // ratio) ^ me_ref[1]
        place = jnp.int32(0)
        for k, distance in enumerate(halving_order(narrow_count)):
            place = jnp.where(apart == distance, k, place)
        places.append(pl.multiple_of((place * ratio + wide % ratio) * block, block))
    x = jnp.concatenate([ref[...] for ref in x_refs], axis=0)
    got = jnp.dot(x, w_ref[:, start : start + sums_ref.shape[1]], preferred_element_type=jnp.float32)
    for d, place in enumerate(places):
        sums_ref[pl.ds(place, block), :] = got[d * block : (d + 1) * block, :]
    code(sums_ref[sums_ref.shape[0] // 2 :, :], sent_ref)


def output_part(me, blocks, w, start, columns, narrow_count, after):
    count = len(blocks)
    block, depth = blocks[0].shape
    rows = count * block
    return call(
        functools.partial(output_kernel, start, count, narrow_count),
        (
            jax.ShapeDtypeStruct((rows, columns), jnp.float32),
            jax.ShapeDtypeStruct((rows // 2, columns + LANES), jnp.int16),
        ),
        (me, *blocks, in_vmem(w), *after),
        [SCALAR] + [FULL] * (count + 1) + [ANY] * len(after),
        "output_part",
        limit=8,
        flops=2 * rows * depth * columns,
        moved=2 * rows * depth,
    )


def halve_kernel(sums_ref, came_ref, *refs):
    still_ref, sent_ref = refs[-2:]
    half = still_ref.shape[0]
    total = sums_ref[: 2 * half, :] + decode(came_ref, sums_ref.shape[1])
    still_ref[...] = total[:half, :]
    code(total[half:, :], sent_ref)


def halve(sums, came, after):
    rows, columns = came.shape[0], sums.shape[1]
    return call(
        halve_kernel,
        (
            jax.ShapeDtypeStruct((rows // 2, columns), jnp.float32),
            jax.ShapeDtypeStruct((rows // 2, columns + LANES), jnp.int16),
        ),
        (sums, came, *after),
        [FULL, FULL] + [ANY] * len(after),
        "halve",
        moved=16 * rows * columns,
    )


def finish_kernel(starts, kinds, *refs):
    out_ref = refs[-1]
    k = 0
    for at, kind in zip(starts, kinds):
        width = refs[k].shape[1]
        done = refs[k][...]
        if kind == 2:
            done = (done + decode(refs[k + 1], width)).astype(jnp.bfloat16)
        out_ref[:, at : at + width] = done
        k += kind


def finish(starts, cuts):
    parts = [x for cut in cuts for x in cut]
    rows, columns = parts[0].shape[0], sum(cut[0].shape[1] for cut in cuts)
    return call(
        functools.partial(finish_kernel, starts, [len(cut) for cut in cuts]),
        jax.ShapeDtypeStruct((rows, columns), jnp.bfloat16),
        parts,
        [FULL] * len(parts),
        "finish",
        moved=8 * columns * rows,
    )


def local(activations, norm_gain, query_weight, kv_weight, out_weight, kv_cache, lengths):
    wide_count = lax.axis_size("wide")
    narrow_count = lax.axis_size("narrow")
    me = jnp.stack([lax.axis_index("wide"), lax.axis_index("narrow")]).astype(jnp.int32)
    own_rows, head_dim = kv_cache.shape[0], kv_cache.shape[2] // 2
    rows, width = activations.shape
    queries = query_weight.shape[1]
    columns = out_weight.shape[1]
    values = activations.astype(jnp.float32)
    stats = jnp.stack([jnp.sum(values, axis=1), jnp.sum(values * values, axis=1)])
    first_part = fetch(query_weight, row_blocks(width)[0], [stats, me])
    kept, sent = project(
        me,
        sent_apart(stats, "wide"),
        activations,
        norm_gain,
        query_weight,
        kv_weight,
        first_part,
        width * wide_count,
        wide_count,
        narrow_count,
    )
    d = 1
    while 2 * d < wide_count:
        kept, sent = fold(kept, swap(sent, "wide", d))
        d *= 2
    split = call(
        functools.partial(split_kernel, queries),
        [jax.ShapeDtypeStruct((own_rows, queries + 4 * head_dim), jnp.bfloat16)] * narrow_count,
        (me, kept, swap(sent, "wide", d)),
        [SCALAR] + [FULL] * 2,
        "split",
        scratch=[pltpu.VMEM((narrow_count * PAD, queries + 2 * head_dim), jnp.float32)],
        flops=BESIDE,
    )
    context = attend(lengths, exchange(split, "narrow"), kv_cache, head_dim, queries)
    returned = call(
        join_kernel,
        jax.ShapeDtypeStruct((narrow_count * own_rows, queries), jnp.bfloat16),
        (me, *exchange(context, "narrow")[::-1]),
        [SCALAR] + [FULL] * narrow_count,
        "join",
        scratch=[pltpu.VMEM((narrow_count * PAD, queries), jnp.float32)],
        flops=BESIDE,
    )
    gathered = gather(returned, "wide")
    ends = [columns // LANES * k // 18 * LANES for k in (0,7,15,18)]
    cut_sums, halved, last = [], [], []

    def exchange_cut(kept, sent, after):
        d = 1
        while 2 * d < narrow_count:
            kept, sent = halve(kept, swap(sent, "narrow", d), after)
            after = []
            d *= 2
        halved.append(kept)
        cut_sums.append((kept, swap(sent, "narrow", d)))

    for start, end in zip(ends, ends[1:]):
        kept, sent = output_part(me, gathered, out_weight, start, end - start, narrow_count, halved[-1:])
        if last:
            exchange_cut(*last, [kept])
        last = (kept, sent)
    early = finish([0], cut_sums[:1])
    exchange_cut(*last, [early])
    cut_sums[0] = (early,)
    return finish(ends[:-1], cut_sums)


def solution(mesh):
    return jax.shard_map(
        local,
        mesh=mesh,
        in_specs=(
            P("groups", "wide"),
            P("wide"),
            P("wide", "narrow"),
            P(("wide", "narrow"), None),
            P("narrow", "wide"),
            P(("groups", "wide", "narrow"), None, None),
            P(("groups", "wide", "narrow")),
        ),
        out_specs=P(("groups", "narrow"), "wide"),
        check_vma=False,
    )
```

```python
import functools
import math

import jax
import jax.numpy as jnp
from jax import lax
from jax.experimental import pallas as pl
from jax.experimental.pallas import tpu as pltpu
from jax.sharding import PartitionSpec as P

MIB = 1 << 20
FULL = pl.BlockSpec(memory_space=pltpu.VMEM)
ANY = pl.BlockSpec(memory_space=pl.ANY)
SCALAR = pl.BlockSpec(memory_space=pltpu.SMEM)
STEPS = 32700.0
TINY = 1e-37
LANES = 128
PAD = 8
BESIDE = 5 * 10**9


def call(kernel, outs, ins, specs, name, scratch=(), limit=4, flops=0, moved=0):
    return pl.pallas_call(
        kernel,
        out_shape=outs,
        in_specs=specs,
        out_specs=jax.tree.map(lambda _: FULL, outs),
        scratch_shapes=list(scratch),
        compiler_params=pltpu.CompilerParams(vmem_limit_bytes=limit * MIB),
        cost_estimate=pl.CostEstimate(flops=flops, bytes_accessed=moved, transcendentals=0),
        name=name,
    )(*ins)


def held(shape, dtype):
    return pltpu.VMEM(shape, dtype)


def in_vmem(x):
    return pltpu.with_memory_space_constraint(x, pltpu.VMEM)


def in_hbm(x):
    return pltpu.with_memory_space_constraint(x, pltpu.HBM)


def swap(x, axis, distance):
    count = lax.axis_size(axis)
    return lax.ppermute(x, axis, [(i, i ^ distance) for i in range(count)])


def sent_apart(x, axis):
    count = lax.axis_size(axis)
    if count <= 4:
        return [x] + [swap(x, axis, d) for d in range(1, count)]
    d = 1
    while d < count:
        x = x + swap(x, axis, d)
        d *= 2
    return [x]


def exchange(blocks, axis):
    far_first = {d: swap(blocks[d], axis, d) for d in range(len(blocks) - 1, 0, -1)}
    return [blocks[0]] + [far_first[d] for d in range(1, len(blocks))]


def gather(x, axis):
    count = lax.axis_size(axis)
    blocks = {0: x}
    d = count // 2
    while d:
        blocks |= {k ^ d: swap(b, axis, d) for k, b in blocks.items()}
        d //= 2
    return [blocks[k] for k in range(count)]


def halving_order(count):
    bits = count.bit_length() - 1
    return [sum(((k >> b) & 1) << (bits - 1 - b) for b in range(bits)) for k in range(count)]


def fetch_kernel(w_ref, *refs):
    share_ref, sem = refs[-2:]
    fetch = pltpu.make_async_copy(w_ref.at[: share_ref.shape[0]], share_ref, sem)
    fetch.start()
    fetch.wait()


def fetch(w, rows, after):
    return call(
        fetch_kernel,
        held((rows, w.shape[1]), w.dtype),
        (in_hbm(w), *after),
        [ANY] * (1 + len(after)),
        "fetch_query_weight",
        scratch=[pltpu.SemaphoreType.DMA],
        moved=2 * rows * w.shape[1],
    )


def row_blocks(rows):
    tiles = rows // LANES
    step = max(1, tiles // 6)
    blocks = [step]
    while tiles - sum(blocks) > step:
        blocks.append(step)
    last = tiles - sum(blocks)
    blocks += [last - last // 3, last // 3] if last > 2 else [last]
    return [LANES * n for n in blocks]


def project_kernel(many, width_all, count, narrow_count, me_ref, *refs):
    stat_refs, refs = refs[:many], refs[many:]
    x_ref, gain_ref, w_ref, kv_ref, first_ref, kept_ref, sent_ref, normed, own, *blocks, sems = refs
    rows, width = x_ref.shape
    half = rows // 2
    block = rows // count
    sub_width = width // narrow_count
    sizes = [ref.shape[0] for ref in (first_ref, *blocks)]
    starts = [sum(sizes[:g]) for g in range(len(sizes))]
    fetches = [
        pltpu.make_async_copy(w_ref.at[start : start + size], ref, sems.at[g])
        for g, (start, size, ref) in enumerate(zip(starts[1:], sizes[1:], blocks))
    ]
    ahead = 3
    for fetch in fetches[:ahead]:
        fetch.start()
    me, narrow = me_ref[0], me_ref[1]
    stats = stat_refs[0][...]
    for ref in stat_refs[1:]:
        stats = stats + ref[...]
    row = lax.broadcasted_iota(jnp.int32, (rows, rows), 0)
    column = lax.broadcasted_iota(jnp.int32, (rows, rows), 1)
    sums = jnp.sum(jnp.where(row == column, stats[0:1, :], 0.0), axis=1, keepdims=True)
    squares = jnp.sum(jnp.where(row == column, stats[1:2, :], 0.0), axis=1, keepdims=True)
    center = sums / width_all
    spread = squares / width_all - center * center
    inverse = lax.rsqrt(spread + 1e-05)
    gain = gain_ref[...].reshape(1, width)
    order = halving_order(count)
    for j in range(count):
        pick = slice(j * block, (j + 1) * block)
        place = jnp.int32(0)
        for k, d in enumerate(order):
            place = jnp.where((me ^ d) == j, k, place)
        place = pl.multiple_of(place * block, 16)
        scaled = (x_ref[pick, :].astype(jnp.float32) - center[pick]) * inverse[pick] * gain
        normed[pl.ds(place, block), :] = scaled.astype(jnp.bfloat16)
    for j in range(narrow_count):
        @pl.when(narrow == j)
        def _(j=j):
            own[...] = normed[:, j * sub_width : (j + 1) * sub_width]

    queries = w_ref.shape[1]

    def products(source, start):
        got = jnp.dot(normed[:, start : start + source.shape[0]], source[...], preferred_element_type=jnp.float32)
        if start:
            kept_ref[:, :queries] += got[:half, :]
            sent_ref[:, :queries] += got[half:, :]
        else:
            kept_ref[:, :queries] = got[:half, :]
            sent_ref[:, :queries] = got[half:, :]

    fresh = jnp.dot(own[...], kv_ref[...], preferred_element_type=jnp.float32)
    kept_ref[:, queries:] = fresh[:half, :]
    sent_ref[:, queries:] = fresh[half:, :]
    products(first_ref, 0)
    for g, fetch in enumerate(fetches):
        fetch.wait()
        if g + ahead < len(fetches):
            fetches[g + ahead].start()
        products(blocks[g], starts[g + 1])


def project(me, stats, x, gain, w, kv, first, width_all, count, narrow_count):
    rows, width = x.shape
    queries = w.shape[1]
    blocks = row_blocks(width)[1:]
    half = jax.ShapeDtypeStruct((rows // 2, queries + kv.shape[1]), jnp.float32)
    return call(
        functools.partial(project_kernel, len(stats), width_all, count, narrow_count),
        (half, half),
        (me, *stats, x, gain, in_hbm(w), in_vmem(kv), in_vmem(first)),
        [SCALAR] + [FULL] * (len(stats) + 2) + [ANY] + [FULL] * 2,
        "project",
        scratch=[
            pltpu.VMEM((rows, width), jnp.bfloat16),
            pltpu.VMEM((rows, width // narrow_count), jnp.bfloat16),
            *[pltpu.VMEM((n, queries), jnp.bfloat16) for n in blocks],
            pltpu.SemaphoreType.DMA((len(blocks),)),
        ],
        limit=36,
        flops=2 * rows * width * queries,
        moved=2 * sum(blocks) * queries,
    )


def fold_kernel(kept_ref, came_ref, still_ref, sent_ref):
    half = still_ref.shape[0]
    still_ref[...] = kept_ref[:half, :] + came_ref[:half, :]
    sent_ref[...] = kept_ref[half:, :] + came_ref[half:, :]


def fold(kept, came):
    half = jax.ShapeDtypeStruct((kept.shape[0] // 2, kept.shape[1]), jnp.float32)
    return call(
        fold_kernel,
        (half, half),
        (kept, came),
        [FULL] * 2,
        "fold",
        flops=BESIDE,
    )


def split_kernel(queries, me_ref, kept_ref, came_ref, *refs):
    out_refs, slots = refs[:-1], refs[-1]
    count = len(out_refs)
    total = kept_ref[...] + came_ref[...]
    rows, columns = total.shape[0] // count, total.shape[1]
    half = slots.shape[1]
    fresh = total[:, queries:]
    low = fresh - fresh.astype(jnp.bfloat16).astype(jnp.float32)
    for j in range(count):
        mine = slice(j * rows, (j + 1) * rows)
        slots[j * PAD : j * PAD + rows, :] = total[mine, :half]
        slots[j * PAD + rows : (j + 1) * PAD, : columns - half] = total[mine, half:]
        slots[j * PAD + rows : (j + 1) * PAD, columns - half :] = low[mine, :]
    for d, out_ref in enumerate(out_refs):
        out_ref[...] = slots[pl.ds(pl.multiple_of((me_ref[1] ^ d) * PAD, PAD), PAD), :].astype(jnp.bfloat16)


def attend_kernel(head_dim, count, lengths_ref, *refs):
    came_refs, kv_ref = refs[:count][::-1], refs[count]
    out_refs, (heads, contexts) = refs[count + 1 : 2 * count + 1], refs[2 * count + 1 :]
    rows, positions = kv_ref.shape[0], kv_ref.shape[1]
    half = came_refs[0].shape[1]
    queries = 2 * out_refs[0].shape[1]
    each = queries // head_dim
    slabs = head_dim // LANES
    group = each // 2
    half_heads = count * group
    scaling = 1.0 / math.sqrt(head_dim)
    terms = 0.0
    for d, ref in enumerate(came_refs):
        for c in range(0, half, LANES):
            both = ref[:, c : c + LANES].astype(jnp.float32)
            for column, part in ((c, both[:rows, :]), (half + c, both[rows:, :])):
                if column < queries:
                    h = column // head_dim
                    at = ((h // group) * half_heads + d * group + h % group) * PAD
                    heads[column % head_dim // LANES, at : at + rows, :] = part
        terms = terms + ref[:, queries - half :].astype(jnp.float32)[rows:, :]
    pair = 2 * head_dim
    fresh = terms[:, :pair] + terms[:, pair:]
    fresh = fresh.astype(jnp.bfloat16).astype(jnp.float32)
    place = lax.broadcasted_iota(jnp.int32, (2 * half_heads, positions), 1)
    for r in range(rows):
        query = jnp.concatenate([heads[k, pl.ds(r, 2 * half_heads, stride=PAD), :] for k in range(slabs)], axis=1)
        scores = (
            lax.dot_general(
                query.astype(jnp.bfloat16),
                kv_ref[r, :, :head_dim],
                (((1,), (1,)), ((), ())),
                preferred_element_type=jnp.float32,
            )
            * scaling
        )
        own_score = jnp.sum(query * fresh[r : r + 1, :head_dim], axis=1, keepdims=True) * scaling
        valid = place < lengths_ref[r]
        top = jnp.maximum(jnp.max(jnp.where(valid, scores, -jnp.inf), axis=1, keepdims=True), own_score)
        weights = jnp.where(valid, jnp.exp(scores - top), 0.0)
        own_weight = jnp.exp(own_score - top)
        total = jnp.sum(weights, axis=1, keepdims=True) + own_weight
        numer = jnp.dot(weights.astype(jnp.bfloat16), kv_ref[r, :, head_dim:], preferred_element_type=jnp.float32)
        numer = numer + own_weight.astype(jnp.bfloat16).astype(jnp.float32) * fresh[r : r + 1, head_dim:]
        context = numer / total
        for k in range(slabs):
            for side in range(2):
                contexts[k, pl.ds(side * rows + r, half_heads, stride=PAD), :] = context[
                    side * half_heads : (side + 1) * half_heads, k * LANES : (k + 1) * LANES
                ]
    for d, ref in enumerate(out_refs):
        for h in range(group):
            at = (d * group + h) * PAD
            for k in range(slabs):
                start = h * head_dim + k * LANES
                ref[:, start : start + LANES] = contexts[k, at : at + PAD, :].astype(jnp.bfloat16)


def attend(lengths, came, kv, head_dim, queries):
    count = len(came)
    all_heads = count * queries // head_dim
    slabs = head_dim // LANES
    return call(
        functools.partial(attend_kernel, head_dim, count),
        [jax.ShapeDtypeStruct((PAD, queries // 2), jnp.bfloat16)] * count,
        (lengths, *came[::-1], in_vmem(kv)),
        [SCALAR] + [FULL] * (count + 1),
        "attend",
        scratch=[
            pltpu.VMEM((slabs, all_heads * PAD, LANES), jnp.float32),
            pltpu.VMEM((slabs, all_heads // 2 * PAD, LANES), jnp.float32),
        ],
        limit=8,
        flops=BESIDE,
    )


def join_kernel(me_ref, *refs):
    count = len(refs) - 2
    out_ref, joined = refs[-2:]
    half = joined.shape[1]
    rows = out_ref.shape[0] // count
    for d in range(count):
        at = pl.ds(pl.multiple_of((me_ref[1] ^ d) * PAD, PAD), PAD)
        joined[at, :] = refs[count - 1 - d][...].astype(jnp.float32)
    for side in range(2):
        came = [joined[j * PAD + side * rows : j * PAD + (side + 1) * rows, :] for j in range(count)]
        out_ref[:, side * half : (side + 1) * half] = jnp.concatenate(came, axis=0).astype(jnp.bfloat16)


def code(x, ref):
    largest = jnp.maximum(jnp.max(jnp.abs(x), axis=1, keepdims=True), TINY)
    power = jnp.floor(jnp.log2(largest)) + 1.0
    steps = jnp.round(x * (STEPS * jnp.exp2(-power)))
    ref[:, : x.shape[1]] = steps.astype(jnp.int32).astype(jnp.int16)
    ref[:, x.shape[1] :] = jnp.broadcast_to(power, (x.shape[0], LANES)).astype(jnp.int32).astype(jnp.int16)


def decode(ref, width):
    power = ref[:, width:].astype(jnp.int32).astype(jnp.float32)[:, 0:1]
    return ref[:, :width].astype(jnp.int32).astype(jnp.float32) * (jnp.exp2(power) * (1.0 / STEPS))


def output_kernel(start, count, narrow_count, me_ref, *refs):
    x_refs, w_ref, (sums_ref, sent_ref) = refs[:count], refs[count], refs[-2:]
    block = x_refs[0].shape[0]
    ratio = count // narrow_count
    places = []
    for d in range(count):
        wide = me_ref[0] ^ d
        apart = (wide // ratio) ^ me_ref[1]
        place = jnp.int32(0)
        for k, distance in enumerate(halving_order(narrow_count)):
            place = jnp.where(apart == distance, k, place)
        places.append(pl.multiple_of((place * ratio + wide % ratio) * block, block))
    x = jnp.concatenate([ref[...] for ref in x_refs], axis=0)
    got = jnp.dot(x, w_ref[:, start : start + sums_ref.shape[1]], preferred_element_type=jnp.float32)
    for d, place in enumerate(places):
        sums_ref[pl.ds(place, block), :] = got[d * block : (d + 1) * block, :]
    code(sums_ref[sums_ref.shape[0] // 2 :, :], sent_ref)


def output_part(me, blocks, w, start, columns, narrow_count, after):
    count = len(blocks)
    block, depth = blocks[0].shape
    rows = count * block
    return call(
        functools.partial(output_kernel, start, count, narrow_count),
        (
            jax.ShapeDtypeStruct((rows, columns), jnp.float32),
            jax.ShapeDtypeStruct((rows // 2, columns + LANES), jnp.int16),
        ),
        (me, *blocks, in_vmem(w), *after),
        [SCALAR] + [FULL] * (count + 1) + [ANY] * len(after),
        "output_part",
        limit=8,
        flops=2 * rows * depth * columns,
        moved=2 * rows * depth,
    )


def halve_kernel(sums_ref, came_ref, *refs):
    still_ref, sent_ref = refs[-2:]
    half = still_ref.shape[0]
    total = sums_ref[: 2 * half, :] + decode(came_ref, sums_ref.shape[1])
    still_ref[...] = total[:half, :]
    code(total[half:, :], sent_ref)


def halve(sums, came, after):
    rows, columns = came.shape[0], sums.shape[1]
    return call(
        halve_kernel,
        (
            jax.ShapeDtypeStruct((rows // 2, columns), jnp.float32),
            jax.ShapeDtypeStruct((rows // 2, columns + LANES), jnp.int16),
        ),
        (sums, came, *after),
        [FULL, FULL] + [ANY] * len(after),
        "halve",
        moved=16 * rows * columns,
    )


def finish_kernel(start, kept_ref, came_ref, *refs):
    out_ref, done, sem = refs[-3:]
    width = kept_ref.shape[1]
    done[...] = (kept_ref[...] + decode(came_ref, width)).astype(jnp.bfloat16)
    copy = pltpu.make_async_copy(done, out_ref.at[:, start : start + width], sem)
    copy.start()
    copy.wait()


def finish(kept, came, start, columns, result):
    rows, width = kept.shape
    return pl.pallas_call(
        functools.partial(finish_kernel, start),
        out_shape=pltpu.HBM((rows, columns), jnp.bfloat16),
        in_specs=[FULL, FULL] + [ANY] * (result is not None),
        out_specs=ANY,
        scratch_shapes=[pltpu.VMEM((rows, width), jnp.bfloat16), pltpu.SemaphoreType.DMA],
        input_output_aliases={} if result is None else {2: 0},
        compiler_params=pltpu.CompilerParams(vmem_limit_bytes=4 * MIB),
        cost_estimate=pl.CostEstimate(flops=0, bytes_accessed=8 * rows * width, transcendentals=0),
        name="finish",
    )(kept, came, *([] if result is None else [in_hbm(result)]))


def local(activations, norm_gain, query_weight, kv_weight, out_weight, kv_cache, lengths):
    wide_count = lax.axis_size("wide")
    narrow_count = lax.axis_size("narrow")
    me = jnp.stack([lax.axis_index("wide"), lax.axis_index("narrow")]).astype(jnp.int32)
    own_rows, head_dim = kv_cache.shape[0], kv_cache.shape[2] // 2
    assert PAD == 2 * own_rows
    rows, width = activations.shape
    queries = query_weight.shape[1]
    columns = out_weight.shape[1]
    values = activations.astype(jnp.float32)
    stats = jnp.stack([jnp.sum(values, axis=1), jnp.sum(values * values, axis=1)])
    first_part = fetch(query_weight, row_blocks(width)[0], [stats, me])
    kept, sent = project(
        me,
        sent_apart(stats, "wide"),
        activations,
        norm_gain,
        query_weight,
        kv_weight,
        first_part,
        width * wide_count,
        wide_count,
        narrow_count,
    )
    d = 1
    while 2 * d < wide_count:
        kept, sent = fold(kept, swap(sent, "wide", d))
        d *= 2
    split = call(
        functools.partial(split_kernel, queries),
        [jax.ShapeDtypeStruct((PAD, queries // 2 + 2 * head_dim), jnp.bfloat16)] * narrow_count,
        (me, kept, swap(sent, "wide", d)),
        [SCALAR] + [FULL] * 2,
        "split",
        scratch=[pltpu.VMEM((narrow_count * PAD, queries // 2 + 2 * head_dim), jnp.float32)],
        flops=BESIDE,
    )
    context = attend(lengths, exchange(split, "narrow"), kv_cache, head_dim, queries)
    returned = call(
        join_kernel,
        jax.ShapeDtypeStruct((narrow_count * own_rows, queries), jnp.bfloat16),
        (me, *exchange(context, "narrow")[::-1]),
        [SCALAR] + [FULL] * narrow_count,
        "join",
        scratch=[pltpu.VMEM((narrow_count * PAD, queries // 2), jnp.float32)],
        flops=BESIDE,
    )
    gathered = gather(returned, "wide")
    ends = [columns // LANES * k // 18 * LANES for k in (0,7,15,18)]
    cut_sums, halved, last = [], [], []

    def exchange_cut(kept, sent, after):
        d = 1
        while 2 * d < narrow_count:
            kept, sent = halve(kept, swap(sent, "narrow", d), after)
            after = []
            d *= 2
        halved.append(kept)
        cut_sums.append((kept, swap(sent, "narrow", d)))

    for start, end in zip(ends, ends[1:]):
        kept, sent = output_part(me, gathered, out_weight, start, end - start, narrow_count, halved[-1:])
        if last:
            exchange_cut(*last, [kept])
        last = (kept, sent)
    result = finish(*cut_sums[0], ends[0], columns, None)
    exchange_cut(*last, [in_hbm(result)])
    for cut, start in zip(cut_sums[1:], ends[1:]):
        result = finish(*cut, start, columns, result)
    return result


def solution(mesh):
    return jax.shard_map(
        local,
        mesh=mesh,
        in_specs=(
            P("groups", "wide"),
            P("wide"),
            P("wide", "narrow"),
            P(("wide", "narrow"), None),
            P("narrow", "wide"),
            P(("groups", "wide", "narrow"), None, None),
            P(("groups", "wide", "narrow")),
        ),
        out_specs=P(("groups", "narrow"), "wide"),
        check_vma=False,
    )
```

```python
import functools
import math

import jax
import jax.numpy as jnp
from jax import lax
from jax.experimental import pallas as pl
from jax.experimental.pallas import tpu as pltpu
from jax.sharding import PartitionSpec as P

MIB = 1 << 20
FULL = pl.BlockSpec(memory_space=pltpu.VMEM)
ANY = pl.BlockSpec(memory_space=pl.ANY)
STEPS = 32700.0
TINY = 1e-37
LANES = 128
PAD = 8
BESIDE = 5 * 10**9


def call(kernel, outs, ins, specs, name, scratch=(), limit=4, flops=0, moved=0):
    return pl.pallas_call(
        kernel,
        out_shape=outs,
        in_specs=specs,
        out_specs=jax.tree.map(lambda _: FULL, outs),
        scratch_shapes=list(scratch),
        compiler_params=pltpu.CompilerParams(vmem_limit_bytes=limit * MIB),
        cost_estimate=pl.CostEstimate(flops=flops, bytes_accessed=moved, transcendentals=0),
        name=name,
    )(*ins)


def held(shape, dtype):
    return pltpu.VMEM(shape, dtype)


def in_vmem(x):
    return pltpu.with_memory_space_constraint(x, pltpu.VMEM)


def in_hbm(x):
    return pltpu.with_memory_space_constraint(x, pltpu.HBM)


def swap(x, axis, distance):
    count = lax.axis_size(axis)
    return lax.ppermute(x, axis, [(i, i ^ distance) for i in range(count)])


def sent_apart(x, axis):
    count = lax.axis_size(axis)
    if count <= 4:
        return [x] + [swap(x, axis, d) for d in range(1, count)]
    d = 1
    while d < count:
        x = x + swap(x, axis, d)
        d *= 2
    return [x]


def exchange(blocks, axis):
    far_first = {d: swap(blocks[d], axis, d) for d in range(len(blocks) - 1, 0, -1)}
    return [blocks[0]] + [far_first[d] for d in range(1, len(blocks))]


def gather(x, axis):
    count = lax.axis_size(axis)
    blocks = {0: x}
    d = count // 2
    while d:
        blocks |= {k ^ d: swap(b, axis, d) for k, b in blocks.items()}
        d //= 2
    return [blocks[k] for k in range(count)]


def halving_order(count):
    bits = count.bit_length() - 1
    return [sum(((k >> b) & 1) << (bits - 1 - b) for b in range(bits)) for k in range(count)]


def fetch_kernel(w_ref, *refs):
    share_ref, sem = refs[-2:]
    fetch = pltpu.make_async_copy(w_ref.at[: share_ref.shape[0]], share_ref, sem)
    fetch.start()
    fetch.wait()


def fetch(w, rows, after):
    return call(
        fetch_kernel,
        held((rows, w.shape[1]), w.dtype),
        (in_hbm(w), *after),
        [ANY] * (1 + len(after)),
        "fetch_query_weight",
        scratch=[pltpu.SemaphoreType.DMA],
        moved=2 * rows * w.shape[1],
    )


def row_blocks(rows):
    tiles = rows // LANES
    step = max(1, tiles // 6)
    blocks = [step]
    while tiles - sum(blocks) > step:
        blocks.append(step)
    last = tiles - sum(blocks)
    blocks += [last - last // 3, last // 3] if last > 2 else [last]
    return [LANES * n for n in blocks]


def project_kernel(many, width_all, count, narrow_count, *refs):
    stat_refs, refs = refs[:many], refs[many:]
    x_ref, gain_ref, w_ref, kv_ref, first_ref, kept_ref, sent_ref, normed, own, *blocks, sems = refs
    rows, width = x_ref.shape
    half = rows // 2
    block = rows // count
    sub_width = width // narrow_count
    sizes = [ref.shape[0] for ref in (first_ref, *blocks)]
    starts = [sum(sizes[:g]) for g in range(len(sizes))]
    fetches = [
        pltpu.make_async_copy(w_ref.at[start : start + size], ref, sems.at[g])
        for g, (start, size, ref) in enumerate(zip(starts[1:], sizes[1:], blocks))
    ]
    ahead = 3
    for fetch in fetches[:ahead]:
        fetch.start()
    me, narrow = lax.axis_index("wide"), lax.axis_index("narrow")
    stats = stat_refs[0][...]
    for ref in stat_refs[1:]:
        stats = stats + ref[...]
    row = lax.broadcasted_iota(jnp.int32, (rows, rows), 0)
    column = lax.broadcasted_iota(jnp.int32, (rows, rows), 1)
    sums = jnp.sum(jnp.where(row == column, stats[0:1, :], 0.0), axis=1, keepdims=True)
    squares = jnp.sum(jnp.where(row == column, stats[1:2, :], 0.0), axis=1, keepdims=True)
    center = sums / width_all
    spread = squares / width_all - center * center
    inverse = lax.rsqrt(spread + 1e-05)
    gain = gain_ref[...].reshape(1, width)
    order = halving_order(count)
    for j in range(count):
        pick = slice(j * block, (j + 1) * block)
        place = jnp.int32(0)
        for k, d in enumerate(order):
            place = jnp.where((me ^ d) == j, k, place)
        place = pl.multiple_of(place * block, 16)
        scaled = (x_ref[pick, :].astype(jnp.float32) - center[pick]) * inverse[pick] * gain
        normed[pl.ds(place, block), :] = scaled.astype(jnp.bfloat16)
    for j in range(narrow_count):
        @pl.when(narrow == j)
        def _(j=j):
            own[...] = normed[:, j * sub_width : (j + 1) * sub_width]

    queries = w_ref.shape[1]

    def products(source, start):
        got = jnp.dot(normed[:, start : start + source.shape[0]], source[...], preferred_element_type=jnp.float32)
        if start:
            kept_ref[:, :queries] += got[:half, :]
            sent_ref[:, :queries] += got[half:, :]
        else:
            kept_ref[:, :queries] = got[:half, :]
            sent_ref[:, :queries] = got[half:, :]

    fresh = jnp.dot(own[...], kv_ref[...], preferred_element_type=jnp.float32)
    kept_ref[:, queries:] = fresh[:half, :]
    sent_ref[:, queries:] = fresh[half:, :]
    products(first_ref, 0)
    for g, fetch in enumerate(fetches):
        fetch.wait()
        if g + ahead < len(fetches):
            fetches[g + ahead].start()
        products(blocks[g], starts[g + 1])


def project(stats, x, gain, w, kv, first, width_all, count, narrow_count):
    rows, width = x.shape
    queries = w.shape[1]
    blocks = row_blocks(width)[1:]
    half = jax.ShapeDtypeStruct((rows // 2, queries + kv.shape[1]), jnp.float32)
    return call(
        functools.partial(project_kernel, len(stats), width_all, count, narrow_count),
        (half, half),
        (*stats, x, gain, in_hbm(w), in_vmem(kv), in_vmem(first)),
        [FULL] * (len(stats) + 2) + [ANY] + [FULL] * 2,
        "project",
        scratch=[
            pltpu.VMEM((rows, width), jnp.bfloat16),
            pltpu.VMEM((rows, width // narrow_count), jnp.bfloat16),
            *[pltpu.VMEM((n, queries), jnp.bfloat16) for n in blocks],
            pltpu.SemaphoreType.DMA((len(blocks),)),
        ],
        limit=36,
        flops=2 * rows * width * queries,
        moved=2 * sum(blocks) * queries,
    )


def fold_kernel(kept_ref, came_ref, still_ref, sent_ref):
    half = still_ref.shape[0]
    still_ref[...] = kept_ref[:half, :] + came_ref[:half, :]
    sent_ref[...] = kept_ref[half:, :] + came_ref[half:, :]


def fold(kept, came):
    half = jax.ShapeDtypeStruct((kept.shape[0] // 2, kept.shape[1]), jnp.float32)
    return call(
        fold_kernel,
        (half, half),
        (kept, came),
        [FULL] * 2,
        "fold",
        flops=BESIDE,
    )


def split_kernel(queries, kept_ref, came_ref, *refs):
    out_refs, slots = refs[:-1], refs[-1]
    count = len(out_refs)
    narrow = lax.axis_index("narrow")
    total = kept_ref[...] + came_ref[...]
    rows, columns = total.shape[0] // count, total.shape[1]
    half = slots.shape[1]
    fresh = total[:, queries:]
    low = fresh - fresh.astype(jnp.bfloat16).astype(jnp.float32)
    for j in range(count):
        mine = slice(j * rows, (j + 1) * rows)
        slots[j * PAD : j * PAD + rows, :] = total[mine, :half]
        slots[j * PAD + rows : (j + 1) * PAD, : columns - half] = total[mine, half:]
        slots[j * PAD + rows : (j + 1) * PAD, columns - half :] = low[mine, :]
    for d, out_ref in enumerate(out_refs):
        out_ref[...] = slots[pl.ds(pl.multiple_of((narrow ^ d) * PAD, PAD), PAD), :].astype(jnp.bfloat16)


def attend_kernel(head_dim, count, lengths_ref, *refs):
    came_refs, kv_ref = refs[:count][::-1], refs[count]
    out_refs, (heads, contexts) = refs[count + 1 : 2 * count + 1], refs[2 * count + 1 :]
    rows, positions = kv_ref.shape[0], kv_ref.shape[1]
    half = came_refs[0].shape[1]
    queries = 2 * out_refs[0].shape[1]
    each = queries // head_dim
    slabs = head_dim // LANES
    group = each // 2
    half_heads = count * group
    scaling = 1.0 / math.sqrt(head_dim)
    terms = 0.0
    for d, ref in enumerate(came_refs):
        for c in range(0, half, LANES):
            both = ref[:, c : c + LANES].astype(jnp.float32)
            for column, part in ((c, both[:rows, :]), (half + c, both[rows:, :])):
                if column < queries:
                    h = column // head_dim
                    at = ((h // group) * half_heads + d * group + h % group) * PAD
                    heads[column % head_dim // LANES, at : at + rows, :] = part
        terms = terms + ref[:, queries - half :].astype(jnp.float32)[rows:, :]
    pair = 2 * head_dim
    fresh = terms[:, :pair] + terms[:, pair:]
    fresh = fresh.astype(jnp.bfloat16).astype(jnp.float32)
    place = lax.broadcasted_iota(jnp.int32, (2 * half_heads, positions), 1)
    for r in range(rows):
        query = jnp.concatenate([heads[k, pl.ds(r, 2 * half_heads, stride=PAD), :] for k in range(slabs)], axis=1)
        scores = (
            lax.dot_general(
                query.astype(jnp.bfloat16),
                kv_ref[r, :, :head_dim],
                (((1,), (1,)), ((), ())),
                preferred_element_type=jnp.float32,
            )
            * scaling
        )
        own_score = jnp.sum(query * fresh[r : r + 1, :head_dim], axis=1, keepdims=True) * scaling
        valid = place < lengths_ref[:, r : r + 1]
        top = jnp.maximum(jnp.max(jnp.where(valid, scores, -jnp.inf), axis=1, keepdims=True), own_score)
        weights = jnp.where(valid, jnp.exp(scores - top), 0.0)
        own_weight = jnp.exp(own_score - top)
        total = jnp.sum(weights, axis=1, keepdims=True) + own_weight
        numer = jnp.dot(weights.astype(jnp.bfloat16), kv_ref[r, :, head_dim:], preferred_element_type=jnp.float32)
        numer = numer + own_weight.astype(jnp.bfloat16).astype(jnp.float32) * fresh[r : r + 1, head_dim:]
        context = numer / total
        for k in range(slabs):
            for side in range(2):
                contexts[k, pl.ds(side * rows + r, half_heads, stride=PAD), :] = context[
                    side * half_heads : (side + 1) * half_heads, k * LANES : (k + 1) * LANES
                ]
    for d, ref in enumerate(out_refs):
        for h in range(group):
            at = (d * group + h) * PAD
            for k in range(slabs):
                start = h * head_dim + k * LANES
                ref[:, start : start + LANES] = contexts[k, at : at + PAD, :].astype(jnp.bfloat16)


def attend(lengths, came, kv, head_dim, queries):
    count = len(came)
    all_heads = count * queries // head_dim
    slabs = head_dim // LANES
    return call(
        functools.partial(attend_kernel, head_dim, count),
        [jax.ShapeDtypeStruct((PAD, queries // 2), jnp.bfloat16)] * count,
        (lengths, *came[::-1], in_vmem(kv)),
        [FULL] * (count + 2),
        "attend",
        scratch=[
            pltpu.VMEM((slabs, all_heads * PAD, LANES), jnp.float32),
            pltpu.VMEM((slabs, all_heads // 2 * PAD, LANES), jnp.float32),
        ],
        limit=8,
        flops=BESIDE,
    )


def join_kernel(*refs):
    count = len(refs) - 2
    out_ref, joined = refs[-2:]
    half = joined.shape[1]
    rows = out_ref.shape[0] // count
    for d in range(count):
        at = pl.ds(pl.multiple_of((lax.axis_index("narrow") ^ d) * PAD, PAD), PAD)
        joined[at, :] = refs[count - 1 - d][...].astype(jnp.float32)
    for side in range(2):
        came = [joined[j * PAD + side * rows : j * PAD + (side + 1) * rows, :] for j in range(count)]
        out_ref[:, side * half : (side + 1) * half] = jnp.concatenate(came, axis=0).astype(jnp.bfloat16)


def code(x, ref):
    largest = jnp.maximum(jnp.max(jnp.abs(x), axis=1, keepdims=True), TINY)
    power = jnp.floor(jnp.log2(largest)) + 1.0
    steps = jnp.round(x * (STEPS * jnp.exp2(-power)))
    ref[:, : x.shape[1]] = steps.astype(jnp.int32).astype(jnp.int16)
    ref[:, x.shape[1] :] = jnp.broadcast_to(power, (x.shape[0], LANES)).astype(jnp.int32).astype(jnp.int16)


def decode(ref, width):
    power = ref[:, width:].astype(jnp.int32).astype(jnp.float32)[:, 0:1]
    return ref[:, :width].astype(jnp.int32).astype(jnp.float32) * (jnp.exp2(power) * (1.0 / STEPS))


def output_kernel(start, count, narrow_count, *refs):
    x_refs, w_ref, (sums_ref, sent_ref) = refs[:count], refs[count], refs[-2:]
    block = x_refs[0].shape[0]
    ratio = count // narrow_count
    places = []
    for d in range(count):
        wide = lax.axis_index("wide") ^ d
        apart = (wide // ratio) ^ lax.axis_index("narrow")
        place = jnp.int32(0)
        for k, distance in enumerate(halving_order(narrow_count)):
            place = jnp.where(apart == distance, k, place)
        places.append(pl.multiple_of((place * ratio + wide % ratio) * block, block))
    x = jnp.concatenate([ref[...] for ref in x_refs], axis=0)
    got = jnp.dot(x, w_ref[:, start : start + sums_ref.shape[1]], preferred_element_type=jnp.float32)
    for d, place in enumerate(places):
        sums_ref[pl.ds(place, block), :] = got[d * block : (d + 1) * block, :]
    code(sums_ref[sums_ref.shape[0] // 2 :, :], sent_ref)


def output_part(blocks, w, start, columns, narrow_count, after):
    count = len(blocks)
    block, depth = blocks[0].shape
    rows = count * block
    return call(
        functools.partial(output_kernel, start, count, narrow_count),
        (
            jax.ShapeDtypeStruct((rows, columns), jnp.float32),
            jax.ShapeDtypeStruct((rows // 2, columns + LANES), jnp.int16),
        ),
        (*blocks, in_vmem(w), *after),
        [FULL] * (count + 1) + [ANY] * len(after),
        "output_part",
        limit=8,
        flops=2 * rows * depth * columns,
        moved=2 * rows * depth,
    )


def halve_kernel(sums_ref, came_ref, *refs):
    still_ref, sent_ref = refs[-2:]
    half = still_ref.shape[0]
    total = sums_ref[: 2 * half, :] + decode(came_ref, sums_ref.shape[1])
    still_ref[...] = total[:half, :]
    code(total[half:, :], sent_ref)


def halve(sums, came, after):
    rows, columns = came.shape[0], sums.shape[1]
    return call(
        halve_kernel,
        (
            jax.ShapeDtypeStruct((rows // 2, columns), jnp.float32),
            jax.ShapeDtypeStruct((rows // 2, columns + LANES), jnp.int16),
        ),
        (sums, came, *after),
        [FULL, FULL] + [ANY] * len(after),
        "halve",
        moved=16 * rows * columns,
    )


def finish_kernel(start, kept_ref, came_ref, *refs):
    out_ref, done, sem = refs[-3:]
    width = kept_ref.shape[1]
    done[...] = (kept_ref[...] + decode(came_ref, width)).astype(jnp.bfloat16)
    copy = pltpu.make_async_copy(done, out_ref.at[:, start : start + width], sem)
    copy.start()
    copy.wait()


def finish(kept, came, start, columns, result):
    rows, width = kept.shape
    return pl.pallas_call(
        functools.partial(finish_kernel, start),
        out_shape=pltpu.HBM((rows, columns), jnp.bfloat16),
        in_specs=[FULL, FULL] + [ANY] * (result is not None),
        out_specs=ANY,
        scratch_shapes=[pltpu.VMEM((rows, width), jnp.bfloat16), pltpu.SemaphoreType.DMA],
        input_output_aliases={} if result is None else {2: 0},
        compiler_params=pltpu.CompilerParams(vmem_limit_bytes=4 * MIB),
        cost_estimate=pl.CostEstimate(flops=0, bytes_accessed=8 * rows * width, transcendentals=0),
        name="finish",
    )(kept, came, *([] if result is None else [in_hbm(result)]))


def local(activations, norm_gain, query_weight, kv_weight, out_weight, kv_cache, lengths):
    wide_count = lax.axis_size("wide")
    narrow_count = lax.axis_size("narrow")
    own_rows, head_dim = kv_cache.shape[0], kv_cache.shape[2] // 2
    assert PAD == 2 * own_rows
    rows, width = activations.shape
    queries = query_weight.shape[1]
    columns = out_weight.shape[1]
    values = activations.astype(jnp.float32)
    stats = jnp.stack([jnp.sum(values, axis=1), jnp.sum(values * values, axis=1)])
    first_part = fetch(query_weight, row_blocks(width)[0], [stats])
    kept, sent = project(
        sent_apart(stats, "wide"),
        activations,
        norm_gain,
        query_weight,
        kv_weight,
        first_part,
        width * wide_count,
        wide_count,
        narrow_count,
    )
    d = 1
    while 2 * d < wide_count:
        kept, sent = fold(kept, swap(sent, "wide", d))
        d *= 2
    split = call(
        functools.partial(split_kernel, queries),
        [jax.ShapeDtypeStruct((PAD, queries // 2 + 2 * head_dim), jnp.bfloat16)] * narrow_count,
        (kept, swap(sent, "wide", d)),
        [FULL] * 2,
        "split",
        scratch=[pltpu.VMEM((narrow_count * PAD, queries // 2 + 2 * head_dim), jnp.float32)],
        flops=BESIDE,
    )
    context = attend(lengths[None], exchange(split, "narrow"), kv_cache, head_dim, queries)
    returned = call(
        join_kernel,
        jax.ShapeDtypeStruct((narrow_count * own_rows, queries), jnp.bfloat16),
        exchange(context, "narrow")[::-1],
        [FULL] * narrow_count,
        "join",
        scratch=[pltpu.VMEM((narrow_count * PAD, queries // 2), jnp.float32)],
        flops=BESIDE,
    )
    gathered = gather(returned, "wide")
    ends = [columns // LANES * k // 18 * LANES for k in (0,7,15,18)]
    cut_sums, halved, last = [], [], []

    def exchange_cut(kept, sent, after):
        d = 1
        while 2 * d < narrow_count:
            kept, sent = halve(kept, swap(sent, "narrow", d), after)
            after = []
            d *= 2
        halved.append(kept)
        cut_sums.append((kept, swap(sent, "narrow", d)))

    for start, end in zip(ends, ends[1:]):
        kept, sent = output_part(gathered, out_weight, start, end - start, narrow_count, halved[-1:])
        if last:
            exchange_cut(*last, [kept])
        last = (kept, sent)
    result = finish(*cut_sums[0], ends[0], columns, None)
    exchange_cut(*last, [in_hbm(result)])
    for cut, start in zip(cut_sums[1:], ends[1:]):
        result = finish(*cut, start, columns, result)
    return result


def solution(mesh):
    return jax.shard_map(
        local,
        mesh=mesh,
        in_specs=(
            P("groups", "wide"),
            P("wide"),
            P("wide", "narrow"),
            P(("wide", "narrow"), None),
            P("narrow", "wide"),
            P(("groups", "wide", "narrow"), None, None),
            P(("groups", "wide", "narrow")),
        ),
        out_specs=P(("groups", "narrow"), "wide"),
        check_vma=False,
    )
```

```python
import functools
import math

import jax
import jax.numpy as jnp
from jax import lax
from jax.experimental import pallas as pl
from jax.experimental.pallas import tpu as pltpu
from jax.sharding import PartitionSpec as P

MIB = 1 << 20
FULL = pl.BlockSpec(memory_space=pltpu.VMEM)
ANY = pl.BlockSpec(memory_space=pl.ANY)
STEPS = 32700.0
TINY = 1e-37
LANES = 128
PAD = 8
BESIDE = 5 * 10**9


def call(kernel, outs, ins, specs, name, scratch=(), limit=4, flops=0, moved=0):
    return pl.pallas_call(
        kernel,
        out_shape=outs,
        in_specs=specs,
        out_specs=jax.tree.map(lambda _: FULL, outs),
        scratch_shapes=list(scratch),
        compiler_params=pltpu.CompilerParams(vmem_limit_bytes=limit * MIB),
        cost_estimate=pl.CostEstimate(flops=flops, bytes_accessed=moved, transcendentals=0),
        name=name,
    )(*ins)


def held(shape, dtype):
    return pltpu.VMEM(shape, dtype)


def in_vmem(x):
    return pltpu.with_memory_space_constraint(x, pltpu.VMEM)


def in_hbm(x):
    return pltpu.with_memory_space_constraint(x, pltpu.HBM)


def swap(x, axis, distance):
    count = lax.axis_size(axis)
    return lax.ppermute(x, axis, [(i, i ^ distance) for i in range(count)])


def sent_apart(x, axis):
    count = lax.axis_size(axis)
    if count <= 4:
        return [x] + [swap(x, axis, d) for d in range(1, count)]
    d = 1
    while d < count:
        x = x + swap(x, axis, d)
        d *= 2
    return [x]


def exchange(blocks, axis):
    far_first = {d: swap(blocks[d], axis, d) for d in range(len(blocks) - 1, 0, -1)}
    return [blocks[0]] + [far_first[d] for d in range(1, len(blocks))]


def gather(x, axis):
    count = lax.axis_size(axis)
    blocks = {0: x}
    d = count // 2
    while d:
        blocks |= {k ^ d: swap(b, axis, d) for k, b in blocks.items()}
        d //= 2
    return [blocks[k] for k in range(count)]


def halving_order(count):
    bits = count.bit_length() - 1
    return [sum(((k >> b) & 1) << (bits - 1 - b) for b in range(bits)) for k in range(count)]


def fetch_kernel(w_ref, *refs):
    share_ref, sem = refs[-2:]
    fetch = pltpu.make_async_copy(w_ref.at[: share_ref.shape[0]], share_ref, sem)
    fetch.start()
    fetch.wait()


def fetch(w, rows, after):
    return call(
        fetch_kernel,
        held((rows, w.shape[1]), w.dtype),
        (in_hbm(w), *after),
        [ANY] * (1 + len(after)),
        "fetch_query_weight",
        scratch=[pltpu.SemaphoreType.DMA],
        moved=2 * rows * w.shape[1],
    )


def row_blocks(rows):
    tiles = rows // LANES
    step = max(1, tiles // 6)
    blocks = [step]
    while tiles - sum(blocks) > step:
        blocks.append(step)
    last = tiles - sum(blocks)
    blocks += [last - last // 3, last // 3] if last > 2 else [last]
    return [LANES * n for n in blocks]


def project_kernel(many, width_all, count, narrow_count, *refs):
    stat_refs, refs = refs[:many], refs[many:]
    x_ref, gain_ref, w_ref, kv_ref, first_ref, kept_ref, sent_ref, normed, own, *blocks, sems = refs
    rows, width = x_ref.shape
    half = rows // 2
    block = rows // count
    sub_width = width // narrow_count
    sizes = [ref.shape[0] for ref in (first_ref, *blocks)]
    starts = [sum(sizes[:g]) for g in range(len(sizes))]
    fetches = [
        pltpu.make_async_copy(w_ref.at[start : start + size], ref, sems.at[g])
        for g, (start, size, ref) in enumerate(zip(starts[1:], sizes[1:], blocks))
    ]
    ahead = 3
    for fetch in fetches[:ahead]:
        fetch.start()
    me, narrow = lax.axis_index("wide"), lax.axis_index("narrow")
    stats = stat_refs[0][...]
    for ref in stat_refs[1:]:
        stats = stats + ref[...]
    row = lax.broadcasted_iota(jnp.int32, (rows, rows), 0)
    column = lax.broadcasted_iota(jnp.int32, (rows, rows), 1)
    sums = jnp.sum(jnp.where(row == column, stats[0:1, :], 0.0), axis=1, keepdims=True)
    squares = jnp.sum(jnp.where(row == column, stats[1:2, :], 0.0), axis=1, keepdims=True)
    center = sums / width_all
    spread = squares / width_all - center * center
    inverse = lax.rsqrt(spread + 1e-05)
    gain = gain_ref[...].reshape(1, width)
    order = halving_order(count)
    for j in range(count):
        pick = slice(j * block, (j + 1) * block)
        place = jnp.int32(0)
        for k, d in enumerate(order):
            place = jnp.where((me ^ d) == j, k, place)
        place = pl.multiple_of(place * block, 16)
        scaled = (x_ref[pick, :].astype(jnp.float32) - center[pick]) * inverse[pick] * gain
        normed[pl.ds(place, block), :] = scaled.astype(jnp.bfloat16)
    for j in range(narrow_count):
        @pl.when(narrow == j)
        def _(j=j):
            own[...] = normed[:, j * sub_width : (j + 1) * sub_width]

    queries = w_ref.shape[1]

    def products(source, start):
        got = jnp.dot(normed[:, start : start + source.shape[0]], source[...], preferred_element_type=jnp.float32)
        if start:
            kept_ref[:, :queries] += got[:half, :]
            sent_ref[:, :queries] += got[half:, :]
        else:
            kept_ref[:, :queries] = got[:half, :]
            sent_ref[:, :queries] = got[half:, :]

    fresh = jnp.dot(own[...], kv_ref[...], preferred_element_type=jnp.float32)
    kept_ref[:, queries:] = fresh[:half, :]
    sent_ref[:, queries:] = fresh[half:, :]
    products(first_ref, 0)
    for g, fetch in enumerate(fetches):
        fetch.wait()
        if g + ahead < len(fetches):
            fetches[g + ahead].start()
        products(blocks[g], starts[g + 1])


def project(stats, x, gain, w, kv, first, width_all, count, narrow_count):
    rows, width = x.shape
    queries = w.shape[1]
    blocks = row_blocks(width)[1:]
    half = jax.ShapeDtypeStruct((rows // 2, queries + kv.shape[1]), jnp.float32)
    return call(
        functools.partial(project_kernel, len(stats), width_all, count, narrow_count),
        (half, half),
        (*stats, x, gain, in_hbm(w), in_vmem(kv), in_vmem(first)),
        [FULL] * (len(stats) + 2) + [ANY] + [FULL] * 2,
        "project",
        scratch=[
            pltpu.VMEM((rows, width), jnp.bfloat16),
            pltpu.VMEM((rows, width // narrow_count), jnp.bfloat16),
            *[pltpu.VMEM((n, queries), jnp.bfloat16) for n in blocks],
            pltpu.SemaphoreType.DMA((len(blocks),)),
        ],
        limit=36,
        flops=2 * rows * width * queries,
        moved=2 * sum(blocks) * queries,
    )


def fold_kernel(kept_ref, came_ref, still_ref, sent_ref):
    half = still_ref.shape[0]
    still_ref[...] = kept_ref[:half, :] + came_ref[:half, :]
    sent_ref[...] = kept_ref[half:, :] + came_ref[half:, :]


def fold(kept, came):
    half = jax.ShapeDtypeStruct((kept.shape[0] // 2, kept.shape[1]), jnp.float32)
    return call(
        fold_kernel,
        (half, half),
        (kept, came),
        [FULL] * 2,
        "fold",
        flops=BESIDE,
    )


def split_kernel(queries, kept_ref, came_ref, *refs):
    out_refs, slots = refs[:-1], refs[-1]
    count = len(out_refs)
    narrow = lax.axis_index("narrow")
    total = kept_ref[...] + came_ref[...]
    rows, columns = total.shape[0] // count, total.shape[1]
    half = slots.shape[1]
    fresh = total[:, queries:]
    low = fresh - fresh.astype(jnp.bfloat16).astype(jnp.float32)
    for j in range(count):
        mine = slice(j * rows, (j + 1) * rows)
        slots[j * PAD : j * PAD + rows, :] = total[mine, :half]
        slots[j * PAD + rows : (j + 1) * PAD, : columns - half] = total[mine, half:]
        slots[j * PAD + rows : (j + 1) * PAD, columns - half :] = low[mine, :]
    for d, out_ref in enumerate(out_refs):
        out_ref[...] = slots[pl.ds(pl.multiple_of((narrow ^ d) * PAD, PAD), PAD), :].astype(jnp.bfloat16)


def attend_kernel(head_dim, count, lengths_ref, *refs):
    came_refs, kv_ref = refs[:count][::-1], refs[count]
    out_refs, (heads, contexts) = refs[count + 1 : 2 * count + 1], refs[2 * count + 1 :]
    rows, positions = kv_ref.shape[0], kv_ref.shape[1]
    half = came_refs[0].shape[1]
    queries = 2 * out_refs[0].shape[1]
    each = queries // head_dim
    slabs = head_dim // LANES
    group = each // 2
    half_heads = count * group
    scaling = 1.0 / math.sqrt(head_dim)
    terms = 0.0
    for d, ref in enumerate(came_refs):
        for c in range(0, half, LANES):
            both = ref[:, c : c + LANES].astype(jnp.float32)
            for column, part in ((c, both[:rows, :]), (half + c, both[rows:, :])):
                if column < queries:
                    h = column // head_dim
                    at = ((h // group) * half_heads + d * group + h % group) * PAD
                    heads[column % head_dim // LANES, at : at + rows, :] = part
        terms = terms + ref[:, queries - half :].astype(jnp.float32)[rows:, :]
    pair = 2 * head_dim
    fresh = terms[:, :pair] + terms[:, pair:]
    fresh = fresh.astype(jnp.bfloat16).astype(jnp.float32)
    place = lax.broadcasted_iota(jnp.int32, (2 * half_heads, positions), 1)
    for r in range(rows):
        query = jnp.concatenate([heads[k, pl.ds(r, 2 * half_heads, stride=PAD), :] for k in range(slabs)], axis=1)
        scores = (
            lax.dot_general(
                query.astype(jnp.bfloat16),
                kv_ref[r, :, :head_dim],
                (((1,), (1,)), ((), ())),
                preferred_element_type=jnp.float32,
            )
            * scaling
        )
        own_score = jnp.sum(query * fresh[r : r + 1, :head_dim], axis=1, keepdims=True) * scaling
        valid = place < lengths_ref[:, r : r + 1]
        top = jnp.maximum(jnp.max(jnp.where(valid, scores, -jnp.inf), axis=1, keepdims=True), own_score)
        weights = jnp.where(valid, jnp.exp(scores - top), 0.0)
        own_weight = jnp.exp(own_score - top)
        total = jnp.sum(weights, axis=1, keepdims=True) + own_weight
        numer = jnp.dot(weights.astype(jnp.bfloat16), kv_ref[r, :, head_dim:], preferred_element_type=jnp.float32)
        numer = numer + own_weight.astype(jnp.bfloat16).astype(jnp.float32) * fresh[r : r + 1, head_dim:]
        context = numer / total
        for k in range(slabs):
            for side in range(2):
                contexts[k, pl.ds(side * rows + r, half_heads, stride=PAD), :] = context[
                    side * half_heads : (side + 1) * half_heads, k * LANES : (k + 1) * LANES
                ]
    for d, ref in enumerate(out_refs):
        for h in range(group):
            at = (d * group + h) * PAD
            for k in range(slabs):
                start = h * head_dim + k * LANES
                ref[:, start : start + LANES] = contexts[k, at : at + PAD, :].astype(jnp.bfloat16)


def attend(lengths, came, kv, head_dim, queries):
    count = len(came)
    all_heads = count * queries // head_dim
    slabs = head_dim // LANES
    return call(
        functools.partial(attend_kernel, head_dim, count),
        [jax.ShapeDtypeStruct((PAD, queries // 2), jnp.bfloat16)] * count,
        (lengths, *came[::-1], in_vmem(kv)),
        [FULL] * (count + 2),
        "attend",
        scratch=[
            pltpu.VMEM((slabs, all_heads * PAD, LANES), jnp.float32),
            pltpu.VMEM((slabs, all_heads // 2 * PAD, LANES), jnp.float32),
        ],
        limit=8,
        flops=BESIDE,
    )


def join_kernel(*refs):
    count = len(refs) - 2
    out_ref, joined = refs[-2:]
    half = joined.shape[1]
    rows = out_ref.shape[0] // count
    for d in range(count):
        at = pl.ds(pl.multiple_of((lax.axis_index("narrow") ^ d) * PAD, PAD), PAD)
        joined[at, :] = refs[count - 1 - d][...].astype(jnp.float32)
    for side in range(2):
        came = [joined[j * PAD + side * rows : j * PAD + (side + 1) * rows, :] for j in range(count)]
        out_ref[:, side * half : (side + 1) * half] = jnp.concatenate(came, axis=0).astype(jnp.bfloat16)


def code(x, ref):
    largest = jnp.maximum(jnp.max(jnp.abs(x), axis=1, keepdims=True), TINY)
    power = jnp.floor(jnp.log2(largest)) + 1.0
    steps = jnp.round(x * (STEPS * jnp.exp2(-power)))
    ref[:, : x.shape[1]] = steps.astype(jnp.int32).astype(jnp.int16)
    ref[:, x.shape[1] :] = jnp.broadcast_to(power, (x.shape[0], LANES)).astype(jnp.int32).astype(jnp.int16)


def decode(ref, width):
    power = ref[:, width:].astype(jnp.int32).astype(jnp.float32)[:, 0:1]
    return ref[:, :width].astype(jnp.int32).astype(jnp.float32) * (jnp.exp2(power) * (1.0 / STEPS))


def output_kernel(start, count, narrow_count, *refs):
    x_refs, w_ref, (sums_ref, sent_ref) = refs[:count], refs[count], refs[-2:]
    block = x_refs[0].shape[0]
    ratio = count // narrow_count
    places = []
    for d in range(count):
        wide = lax.axis_index("wide") ^ d
        apart = (wide // ratio) ^ lax.axis_index("narrow")
        place = jnp.int32(0)
        for k, distance in enumerate(halving_order(narrow_count)):
            place = jnp.where(apart == distance, k, place)
        places.append(pl.multiple_of((place * ratio + wide % ratio) * block, block))
    x = jnp.concatenate([ref[...] for ref in x_refs], axis=0)
    got = jnp.dot(x, w_ref[:, start : start + sums_ref.shape[1]], preferred_element_type=jnp.float32)
    for d, place in enumerate(places):
        sums_ref[pl.ds(place, block), :] = got[d * block : (d + 1) * block, :]
    code(sums_ref[sums_ref.shape[0] // 2 :, :], sent_ref)


def output_part(blocks, w, start, columns, narrow_count, after):
    count = len(blocks)
    block, depth = blocks[0].shape
    rows = count * block
    return call(
        functools.partial(output_kernel, start, count, narrow_count),
        (
            jax.ShapeDtypeStruct((rows, columns), jnp.float32),
            jax.ShapeDtypeStruct((rows // 2, columns + LANES), jnp.int16),
        ),
        (*blocks, in_vmem(w), *after),
        [FULL] * (count + 1) + [ANY] * len(after),
        "output_part",
        limit=8,
        flops=2 * rows * depth * columns,
        moved=2 * rows * depth,
    )


def halve_kernel(sums_ref, came_ref, *refs):
    still_ref, sent_ref = refs[-2:]
    half = still_ref.shape[0]
    total = sums_ref[: 2 * half, :] + decode(came_ref, sums_ref.shape[1])
    still_ref[...] = total[:half, :]
    code(total[half:, :], sent_ref)


def halve(sums, came, after):
    rows, columns = came.shape[0], sums.shape[1]
    return call(
        halve_kernel,
        (
            jax.ShapeDtypeStruct((rows // 2, columns), jnp.float32),
            jax.ShapeDtypeStruct((rows // 2, columns + LANES), jnp.int16),
        ),
        (sums, came, *after),
        [FULL, FULL] + [ANY] * len(after),
        "halve",
        moved=16 * rows * columns,
    )


def finish_kernel(starts, kinds, *refs):
    out_ref = refs[-1]
    k = 0
    for at, kind in zip(starts, kinds):
        width = refs[k].shape[1]
        done = refs[k][...]
        if kind == 2:
            done = (done + decode(refs[k + 1], width)).astype(jnp.bfloat16)
        out_ref[:, at : at + width] = done
        k += kind


def finish(starts, cuts):
    parts = [x for cut in cuts for x in cut]
    rows, columns = parts[0].shape[0], sum(cut[0].shape[1] for cut in cuts)
    return call(
        functools.partial(finish_kernel, starts, [len(cut) for cut in cuts]),
        jax.ShapeDtypeStruct((rows, columns), jnp.bfloat16),
        parts,
        [FULL] * len(parts),
        "finish",
        moved=8 * columns * rows,
    )


def local(activations, norm_gain, query_weight, kv_weight, out_weight, kv_cache, lengths):
    wide_count = lax.axis_size("wide")
    narrow_count = lax.axis_size("narrow")
    own_rows, head_dim = kv_cache.shape[0], kv_cache.shape[2] // 2
    assert PAD == 2 * own_rows
    rows, width = activations.shape
    queries = query_weight.shape[1]
    columns = out_weight.shape[1]
    values = activations.astype(jnp.float32)
    stats = jnp.stack([jnp.sum(values, axis=1), jnp.sum(values * values, axis=1)])
    first_part = fetch(query_weight, row_blocks(width)[0], [stats])
    kept, sent = project(
        sent_apart(stats, "wide"),
        activations,
        norm_gain,
        query_weight,
        kv_weight,
        first_part,
        width * wide_count,
        wide_count,
        narrow_count,
    )
    d = 1
    while 2 * d < wide_count:
        kept, sent = fold(kept, swap(sent, "wide", d))
        d *= 2
    split = call(
        functools.partial(split_kernel, queries),
        [jax.ShapeDtypeStruct((PAD, queries // 2 + 2 * head_dim), jnp.bfloat16)] * narrow_count,
        (kept, swap(sent, "wide", d)),
        [FULL] * 2,
        "split",
        scratch=[pltpu.VMEM((narrow_count * PAD, queries // 2 + 2 * head_dim), jnp.float32)],
        flops=BESIDE,
    )
    context = attend(lengths[None], exchange(split, "narrow"), kv_cache, head_dim, queries)
    returned = call(
        join_kernel,
        jax.ShapeDtypeStruct((narrow_count * own_rows, queries), jnp.bfloat16),
        exchange(context, "narrow")[::-1],
        [FULL] * narrow_count,
        "join",
        scratch=[pltpu.VMEM((narrow_count * PAD, queries // 2), jnp.float32)],
        flops=BESIDE,
    )
    gathered = gather(returned, "wide")
    ends = [columns // LANES * k // 18 * LANES for k in (0, 8, 16, 18)]
    cut_sums, halved, last = [], [], []

    def exchange_cut(kept, sent, after):
        d = 1
        while 2 * d < narrow_count:
            kept, sent = halve(kept, swap(sent, "narrow", d), after)
            after = []
            d *= 2
        halved.append(kept)
        cut_sums.append((kept, swap(sent, "narrow", d)))

    for start, end in zip(ends, ends[1:]):
        kept, sent = output_part(gathered, out_weight, start, end - start, narrow_count, halved[-1:])
        if last:
            exchange_cut(*last, [kept])
        last = (kept, sent)
    early = finish([0], cut_sums[:1])
    exchange_cut(*last, [early])
    cut_sums[0] = (early,)
    return finish(ends[:-1], cut_sums)


def solution(mesh):
    return jax.shard_map(
        local,
        mesh=mesh,
        in_specs=(
            P("groups", "wide"),
            P("wide"),
            P("wide", "narrow"),
            P(("wide", "narrow"), None),
            P("narrow", "wide"),
            P(("groups", "wide", "narrow"), None, None),
            P(("groups", "wide", "narrow")),
        ),
        out_specs=P(("groups", "narrow"), "wide"),
        check_vma=False,
    )
```

```python
import functools
import math

import jax
import jax.numpy as jnp
from jax import lax
from jax.experimental import pallas as pl
from jax.experimental.pallas import tpu as pltpu
from jax.sharding import PartitionSpec as P

MIB = 1 << 20
FULL = pl.BlockSpec(memory_space=pltpu.VMEM)
ANY = pl.BlockSpec(memory_space=pl.ANY)
STEPS = 32700.0
TINY = 1e-37
LANES = 128
PAD = 8
BESIDE = 5 * 10**9


def call(kernel, outs, ins, specs, name, scratch=(), limit=4, flops=0, moved=0):
    return pl.pallas_call(
        kernel,
        out_shape=outs,
        in_specs=specs,
        out_specs=jax.tree.map(lambda _: FULL, outs),
        scratch_shapes=list(scratch),
        compiler_params=pltpu.CompilerParams(vmem_limit_bytes=limit * MIB),
        cost_estimate=pl.CostEstimate(flops=flops, bytes_accessed=moved, transcendentals=0),
        name=name,
    )(*ins)


def held(shape, dtype):
    return pltpu.VMEM(shape, dtype)


def in_vmem(x):
    return pltpu.with_memory_space_constraint(x, pltpu.VMEM)


def in_hbm(x):
    return pltpu.with_memory_space_constraint(x, pltpu.HBM)


def swap(x, axis, distance):
    count = lax.axis_size(axis)
    return lax.ppermute(x, axis, [(i, i ^ distance) for i in range(count)])


def sent_apart(x, axis):
    count = lax.axis_size(axis)
    if count <= 4:
        return [x] + [swap(x, axis, d) for d in range(1, count)]
    d = 1
    while d < count:
        x = x + swap(x, axis, d)
        d *= 2
    return [x]


def exchange(blocks, axis):
    far_first = {d: swap(blocks[d], axis, d) for d in range(len(blocks) - 1, 0, -1)}
    return [blocks[0]] + [far_first[d] for d in range(1, len(blocks))]


def gather(x, axis):
    count = lax.axis_size(axis)
    blocks = {0: x}
    d = count // 2
    while d:
        blocks |= {k ^ d: swap(b, axis, d) for k, b in blocks.items()}
        d //= 2
    return [blocks[k] for k in range(count)]


def halving_order(count):
    bits = count.bit_length() - 1
    return [sum(((k >> b) & 1) << (bits - 1 - b) for b in range(bits)) for k in range(count)]


def fetch_kernel(w_ref, *refs):
    share_ref, sem = refs[-2:]
    fetch = pltpu.make_async_copy(w_ref.at[: share_ref.shape[0]], share_ref, sem)
    fetch.start()
    fetch.wait()


def fetch(w, rows, after):
    return call(
        fetch_kernel,
        held((rows, w.shape[1]), w.dtype),
        (in_hbm(w), *after),
        [ANY] * (1 + len(after)),
        "fetch_query_weight",
        scratch=[pltpu.SemaphoreType.DMA],
        moved=2 * rows * w.shape[1],
    )


def row_blocks(rows):
    tiles = rows // LANES
    step = max(1, tiles // 6)
    blocks = [step]
    while tiles - sum(blocks) > step:
        blocks.append(step)
    last = tiles - sum(blocks)
    blocks += [last - last // 3, last // 3] if last > 2 else [last]
    return [LANES * n for n in blocks]


def project_kernel(many, width_all, count, narrow_count, *refs):
    stat_refs, refs = refs[:many], refs[many:]
    x_ref, gain_ref, w_ref, kv_ref, first_ref, kept_ref, sent_ref, normed, own, *blocks, sems = refs
    rows, width = x_ref.shape
    half = rows // 2
    block = rows // count
    sub_width = width // narrow_count
    sizes = [ref.shape[0] for ref in (first_ref, *blocks)]
    starts = [sum(sizes[:g]) for g in range(len(sizes))]
    fetches = [
        pltpu.make_async_copy(w_ref.at[start : start + size], ref, sems.at[g])
        for g, (start, size, ref) in enumerate(zip(starts[1:], sizes[1:], blocks))
    ]
    ahead = 3
    for fetch in fetches[:ahead]:
        fetch.start()
    me, narrow = lax.axis_index("wide"), lax.axis_index("narrow")
    stats = stat_refs[0][...]
    for ref in stat_refs[1:]:
        stats = stats + ref[...]
    row = lax.broadcasted_iota(jnp.int32, (rows, rows), 0)
    column = lax.broadcasted_iota(jnp.int32, (rows, rows), 1)
    sums = jnp.sum(jnp.where(row == column, stats[0:1, :], 0.0), axis=1, keepdims=True)
    squares = jnp.sum(jnp.where(row == column, stats[1:2, :], 0.0), axis=1, keepdims=True)
    center = sums / width_all
    spread = squares / width_all - center * center
    inverse = lax.rsqrt(spread + 1e-05)
    gain = gain_ref[...].reshape(1, width)
    order = halving_order(count)
    for j in range(count):
        pick = slice(j * block, (j + 1) * block)
        place = jnp.int32(0)
        for k, d in enumerate(order):
            place = jnp.where((me ^ d) == j, k, place)
        place = pl.multiple_of(place * block, 16)
        scaled = (x_ref[pick, :].astype(jnp.float32) - center[pick]) * inverse[pick] * gain
        normed[pl.ds(place, block), :] = scaled.astype(jnp.bfloat16)
    for j in range(narrow_count):
        @pl.when(narrow == j)
        def _(j=j):
            own[...] = normed[:, j * sub_width : (j + 1) * sub_width]

    queries = w_ref.shape[1]

    def products(source, start):
        got = jnp.dot(normed[:, start : start + source.shape[0]], source[...], preferred_element_type=jnp.float32)
        if start:
            kept_ref[:, :queries] += got[:half, :]
            sent_ref[:, :queries] += got[half:, :]
        else:
            kept_ref[:, :queries] = got[:half, :]
            sent_ref[:, :queries] = got[half:, :]

    fresh = jnp.dot(own[...], kv_ref[...], preferred_element_type=jnp.float32)
    kept_ref[:, queries:] = fresh[:half, :]
    sent_ref[:, queries:] = fresh[half:, :]
    products(first_ref, 0)
    for g, fetch in enumerate(fetches):
        fetch.wait()
        if g + ahead < len(fetches):
            fetches[g + ahead].start()
        products(blocks[g], starts[g + 1])


def project(stats, x, gain, w, kv, first, width_all, count, narrow_count):
    rows, width = x.shape
    queries = w.shape[1]
    blocks = row_blocks(width)[1:]
    half = jax.ShapeDtypeStruct((rows // 2, queries + kv.shape[1]), jnp.float32)
    return call(
        functools.partial(project_kernel, len(stats), width_all, count, narrow_count),
        (half, half),
        (*stats, x, gain, in_hbm(w), in_vmem(kv), in_vmem(first)),
        [FULL] * (len(stats) + 2) + [ANY] + [FULL] * 2,
        "project",
        scratch=[
            pltpu.VMEM((rows, width), jnp.bfloat16),
            pltpu.VMEM((rows, width // narrow_count), jnp.bfloat16),
            *[pltpu.VMEM((n, queries), jnp.bfloat16) for n in blocks],
            pltpu.SemaphoreType.DMA((len(blocks),)),
        ],
        limit=36,
        flops=2 * rows * width * queries,
        moved=2 * sum(blocks) * queries,
    )


def fold_kernel(kept_ref, came_ref, still_ref, sent_ref):
    half = still_ref.shape[0]
    still_ref[...] = kept_ref[:half, :] + came_ref[:half, :]
    sent_ref[...] = kept_ref[half:, :] + came_ref[half:, :]


def fold(kept, came):
    half = jax.ShapeDtypeStruct((kept.shape[0] // 2, kept.shape[1]), jnp.float32)
    return call(
        fold_kernel,
        (half, half),
        (kept, came),
        [FULL] * 2,
        "fold",
        flops=BESIDE,
    )


def split_kernel(queries, kept_ref, came_ref, *refs):
    out_refs, slots = refs[:-1], refs[-1]
    count = len(out_refs)
    narrow = lax.axis_index("narrow")
    total = kept_ref[...] + came_ref[...]
    rows, columns = total.shape[0] // count, total.shape[1]
    half = slots.shape[1]
    fresh = total[:, queries:]
    low = fresh - fresh.astype(jnp.bfloat16).astype(jnp.float32)
    for j in range(count):
        mine = slice(j * rows, (j + 1) * rows)
        slots[j * PAD : j * PAD + rows, :] = total[mine, :half]
        slots[j * PAD + rows : (j + 1) * PAD, : columns - half] = total[mine, half:]
        slots[j * PAD + rows : (j + 1) * PAD, columns - half :] = low[mine, :]
    for d, out_ref in enumerate(out_refs):
        out_ref[...] = slots[pl.ds(pl.multiple_of((narrow ^ d) * PAD, PAD), PAD), :].astype(jnp.bfloat16)


def attend_kernel(head_dim, count, lengths_ref, *refs):
    came_refs, kv_ref = refs[:count][::-1], refs[count]
    out_refs, (heads, contexts) = refs[count + 1 : 2 * count + 1], refs[2 * count + 1 :]
    rows, positions = kv_ref.shape[0], kv_ref.shape[1]
    half = came_refs[0].shape[1]
    queries = 2 * out_refs[0].shape[1]
    each = queries // head_dim
    slabs = head_dim // LANES
    group = each // 2
    half_heads = count * group
    scaling = 1.0 / math.sqrt(head_dim)
    terms = 0.0
    for d, ref in enumerate(came_refs):
        for c in range(0, half, LANES):
            both = ref[:, c : c + LANES].astype(jnp.float32)
            for column, part in ((c, both[:rows, :]), (half + c, both[rows:, :])):
                if column < queries:
                    h = column // head_dim
                    at = ((h // group) * half_heads + d * group + h % group) * PAD
                    heads[column % head_dim // LANES, at : at + rows, :] = part
        terms = terms + ref[:, queries - half :].astype(jnp.float32)[rows:, :]
    pair = 2 * head_dim
    fresh = terms[:, :pair] + terms[:, pair:]
    fresh = fresh.astype(jnp.bfloat16).astype(jnp.float32)
    place = lax.broadcasted_iota(jnp.int32, (2 * half_heads, positions), 1)
    for r in range(rows):
        query = jnp.concatenate([heads[k, pl.ds(r, 2 * half_heads, stride=PAD), :] for k in range(slabs)], axis=1)
        scores = (
            lax.dot_general(
                query.astype(jnp.bfloat16),
                kv_ref[r, :, :head_dim],
                (((1,), (1,)), ((), ())),
                preferred_element_type=jnp.float32,
            )
            * scaling
        )
        own_score = jnp.sum(query * fresh[r : r + 1, :head_dim], axis=1, keepdims=True) * scaling
        valid = place < lengths_ref[:, r : r + 1]
        top = jnp.maximum(jnp.max(jnp.where(valid, scores, -jnp.inf), axis=1, keepdims=True), own_score)
        weights = jnp.where(valid, jnp.exp(scores - top), 0.0)
        own_weight = jnp.exp(own_score - top)
        total = jnp.sum(weights, axis=1, keepdims=True) + own_weight
        numer = jnp.dot(weights.astype(jnp.bfloat16), kv_ref[r, :, head_dim:], preferred_element_type=jnp.float32)
        numer = numer + own_weight.astype(jnp.bfloat16).astype(jnp.float32) * fresh[r : r + 1, head_dim:]
        context = numer / total
        for k in range(slabs):
            for side in range(2):
                contexts[k, pl.ds(side * rows + r, half_heads, stride=PAD), :] = context[
                    side * half_heads : (side + 1) * half_heads, k * LANES : (k + 1) * LANES
                ]
    for d, ref in enumerate(out_refs):
        for h in range(group):
            at = (d * group + h) * PAD
            for k in range(slabs):
                start = h * head_dim + k * LANES
                ref[:, start : start + LANES] = contexts[k, at : at + PAD, :].astype(jnp.bfloat16)


def attend(lengths, came, kv, head_dim, queries):
    count = len(came)
    all_heads = count * queries // head_dim
    slabs = head_dim // LANES
    return call(
        functools.partial(attend_kernel, head_dim, count),
        [jax.ShapeDtypeStruct((PAD, queries // 2), jnp.bfloat16)] * count,
        (lengths, *came[::-1], in_vmem(kv)),
        [FULL] * (count + 2),
        "attend",
        scratch=[
            pltpu.VMEM((slabs, all_heads * PAD, LANES), jnp.float32),
            pltpu.VMEM((slabs, all_heads // 2 * PAD, LANES), jnp.float32),
        ],
        limit=8,
        flops=BESIDE,
    )


def join_kernel(*refs):
    count = len(refs) - 2
    out_ref, joined = refs[-2:]
    half = joined.shape[1]
    rows = out_ref.shape[0] // count
    for d in range(count):
        at = pl.ds(pl.multiple_of((lax.axis_index("narrow") ^ d) * PAD, PAD), PAD)
        joined[at, :] = refs[count - 1 - d][...].astype(jnp.float32)
    for side in range(2):
        came = [joined[j * PAD + side * rows : j * PAD + (side + 1) * rows, :] for j in range(count)]
        out_ref[:, side * half : (side + 1) * half] = jnp.concatenate(came, axis=0).astype(jnp.bfloat16)


def code(x, ref):
    largest = jnp.maximum(jnp.max(jnp.abs(x), axis=1, keepdims=True), TINY)
    power = jnp.floor(jnp.log2(largest)) + 1.0
    steps = jnp.round(x * (STEPS * jnp.exp2(-power)))
    ref[:, : x.shape[1]] = steps.astype(jnp.int32).astype(jnp.int16)
    ref[:, x.shape[1] :] = jnp.broadcast_to(power, (x.shape[0], LANES)).astype(jnp.int32).astype(jnp.int16)


def decode(ref, width):
    power = ref[:, width:].astype(jnp.int32).astype(jnp.float32)[:, 0:1]
    return ref[:, :width].astype(jnp.int32).astype(jnp.float32) * (jnp.exp2(power) * (1.0 / STEPS))


def output_kernel(start, count, narrow_count, *refs):
    x_refs, w_ref, (sums_ref, sent_ref) = refs[:count], refs[count], refs[-2:]
    block = x_refs[0].shape[0]
    ratio = count // narrow_count
    places = []
    for d in range(count):
        wide = lax.axis_index("wide") ^ d
        apart = (wide // ratio) ^ lax.axis_index("narrow")
        place = jnp.int32(0)
        for k, distance in enumerate(halving_order(narrow_count)):
            place = jnp.where(apart == distance, k, place)
        places.append(pl.multiple_of((place * ratio + wide % ratio) * block, block))
    x = jnp.concatenate([ref[...] for ref in x_refs], axis=0)
    got = jnp.dot(x, w_ref[:, start : start + sums_ref.shape[1]], preferred_element_type=jnp.float32)
    for d, place in enumerate(places):
        sums_ref[pl.ds(place, block), :] = got[d * block : (d + 1) * block, :]
    code(sums_ref[sums_ref.shape[0] // 2 :, :], sent_ref)


def output_part(blocks, w, start, columns, narrow_count, after):
    count = len(blocks)
    block, depth = blocks[0].shape
    rows = count * block
    return call(
        functools.partial(output_kernel, start, count, narrow_count),
        (
            jax.ShapeDtypeStruct((rows, columns), jnp.float32),
            jax.ShapeDtypeStruct((rows // 2, columns + LANES), jnp.int16),
        ),
        (*blocks, in_vmem(w), *after),
        [FULL] * (count + 1) + [ANY] * len(after),
        "output_part",
        limit=8,
        flops=2 * rows * depth * columns,
        moved=2 * rows * depth,
    )


def halve_kernel(sums_ref, came_ref, *refs):
    still_ref, sent_ref = refs[-2:]
    half = still_ref.shape[0]
    total = sums_ref[: 2 * half, :] + decode(came_ref, sums_ref.shape[1])
    still_ref[...] = total[:half, :]
    code(total[half:, :], sent_ref)


def halve(sums, came, after):
    rows, columns = came.shape[0], sums.shape[1]
    return call(
        halve_kernel,
        (
            jax.ShapeDtypeStruct((rows // 2, columns), jnp.float32),
            jax.ShapeDtypeStruct((rows // 2, columns + LANES), jnp.int16),
        ),
        (sums, came, *after),
        [FULL, FULL] + [ANY] * len(after),
        "halve",
        moved=16 * rows * columns,
    )


def finish_kernel(starts, kinds, *refs):
    out_ref = refs[-1]
    k = 0
    for at, kind in zip(starts, kinds):
        width = refs[k].shape[1]
        done = refs[k][...]
        if kind == 2:
            done = (done + decode(refs[k + 1], width)).astype(jnp.bfloat16)
        out_ref[:, at : at + width] = done
        k += kind


def finish(starts, cuts):
    parts = [x for cut in cuts for x in cut]
    rows, columns = parts[0].shape[0], sum(cut[0].shape[1] for cut in cuts)
    return call(
        functools.partial(finish_kernel, starts, [len(cut) for cut in cuts]),
        jax.ShapeDtypeStruct((rows, columns), jnp.bfloat16),
        parts,
        [FULL] * len(parts),
        "finish",
        moved=8 * columns * rows,
    )


def local(activations, norm_gain, query_weight, kv_weight, out_weight, kv_cache, lengths):
    wide_count = lax.axis_size("wide")
    narrow_count = lax.axis_size("narrow")
    own_rows, head_dim = kv_cache.shape[0], kv_cache.shape[2] // 2
    assert PAD == 2 * own_rows
    rows, width = activations.shape
    queries = query_weight.shape[1]
    columns = out_weight.shape[1]
    values = activations.astype(jnp.float32)
    stats = jnp.stack([jnp.sum(values, axis=1), jnp.sum(values * values, axis=1)])
    first_part = fetch(query_weight, row_blocks(width)[0], [stats])
    kept, sent = project(
        sent_apart(stats, "wide"),
        activations,
        norm_gain,
        query_weight,
        kv_weight,
        first_part,
        width * wide_count,
        wide_count,
        narrow_count,
    )
    d = 1
    while 2 * d < wide_count:
        kept, sent = fold(kept, swap(sent, "wide", d))
        d *= 2
    split = call(
        functools.partial(split_kernel, queries),
        [jax.ShapeDtypeStruct((PAD, queries // 2 + 2 * head_dim), jnp.bfloat16)] * narrow_count,
        (kept, swap(sent, "wide", d)),
        [FULL] * 2,
        "split",
        scratch=[pltpu.VMEM((narrow_count * PAD, queries // 2 + 2 * head_dim), jnp.float32)],
        flops=BESIDE,
    )
    context = attend(lengths[None], exchange(split, "narrow"), kv_cache, head_dim, queries)
    returned = call(
        join_kernel,
        jax.ShapeDtypeStruct((narrow_count * own_rows, queries), jnp.bfloat16),
        exchange(context, "narrow")[::-1],
        [FULL] * narrow_count,
        "join",
        scratch=[pltpu.VMEM((narrow_count * PAD, queries // 2), jnp.float32)],
        flops=BESIDE,
    )
    gathered = gather(returned, "wide")
    ends = [columns // LANES * k // 18 * LANES for k in (0, 8, 15, 18)]
    cut_sums, halved, last = [], [], []

    def exchange_cut(kept, sent, after):
        d = 1
        while 2 * d < narrow_count:
            kept, sent = halve(kept, swap(sent, "narrow", d), after)
            after = []
            d *= 2
        halved.append(kept)
        cut_sums.append((kept, swap(sent, "narrow", d)))

    for start, end in zip(ends, ends[1:]):
        kept, sent = output_part(gathered, out_weight, start, end - start, narrow_count, halved[-1:])
        if last:
            exchange_cut(*last, [kept])
        last = (kept, sent)
    early = finish([0], cut_sums[:1])
    exchange_cut(*last, [early])
    cut_sums[0] = (early,)
    return finish(ends[:-1], cut_sums)


def solution(mesh):
    return jax.shard_map(
        local,
        mesh=mesh,
        in_specs=(
            P("groups", "wide"),
            P("wide"),
            P("wide", "narrow"),
            P(("wide", "narrow"), None),
            P("narrow", "wide"),
            P(("groups", "wide", "narrow"), None, None),
            P(("groups", "wide", "narrow")),
        ),
        out_specs=P(("groups", "narrow"), "wide"),
        check_vma=False,
    )
```

```python
import functools
import math

import jax
import jax.numpy as jnp
from jax import lax
from jax.experimental import pallas as pl
from jax.experimental.pallas import tpu as pltpu
from jax.sharding import PartitionSpec as P

MIB = 1 << 20
FULL = pl.BlockSpec(memory_space=pltpu.VMEM)
ANY = pl.BlockSpec(memory_space=pl.ANY)
STEPS = 32700.0
TINY = 1e-37
LANES = 128
PAD = 8
BESIDE = 5 * 10**9


def call(kernel, outs, ins, specs, name, scratch=(), limit=4, flops=0, moved=0):
    return pl.pallas_call(
        kernel,
        out_shape=outs,
        in_specs=specs,
        out_specs=jax.tree.map(lambda _: FULL, outs),
        scratch_shapes=list(scratch),
        compiler_params=pltpu.CompilerParams(vmem_limit_bytes=limit * MIB),
        cost_estimate=pl.CostEstimate(flops=flops, bytes_accessed=moved, transcendentals=0),
        name=name,
    )(*ins)


def held(shape, dtype):
    return pltpu.VMEM(shape, dtype)


def in_vmem(x):
    return pltpu.with_memory_space_constraint(x, pltpu.VMEM)


def in_hbm(x):
    return pltpu.with_memory_space_constraint(x, pltpu.HBM)


def swap(x, axis, distance):
    count = lax.axis_size(axis)
    return lax.ppermute(x, axis, [(i, i ^ distance) for i in range(count)])


def sent_apart(x, axis):
    count = lax.axis_size(axis)
    if count <= 4:
        return [x] + [swap(x, axis, d) for d in range(1, count)]
    d = 1
    while d < count:
        x = x + swap(x, axis, d)
        d *= 2
    return [x]


def exchange(blocks, axis):
    far_first = {d: swap(blocks[d], axis, d) for d in range(len(blocks) - 1, 0, -1)}
    return [blocks[0]] + [far_first[d] for d in range(1, len(blocks))]


def gather(x, axis):
    count = lax.axis_size(axis)
    blocks = {0: x}
    d = count // 2
    while d:
        blocks |= {k ^ d: swap(b, axis, d) for k, b in blocks.items()}
        d //= 2
    return [blocks[k] for k in range(count)]


def halving_order(count):
    bits = count.bit_length() - 1
    return [sum(((k >> b) & 1) << (bits - 1 - b) for b in range(bits)) for k in range(count)]


def fetch_kernel(w_ref, *refs):
    share_ref, sem = refs[-2:]
    fetch = pltpu.make_async_copy(w_ref.at[: share_ref.shape[0]], share_ref, sem)
    fetch.start()
    fetch.wait()


def fetch(w, rows, after):
    return call(
        fetch_kernel,
        held((rows, w.shape[1]), w.dtype),
        (in_hbm(w), *after),
        [ANY] * (1 + len(after)),
        "fetch_query_weight",
        scratch=[pltpu.SemaphoreType.DMA],
        moved=2 * rows * w.shape[1],
    )


def row_blocks(rows):
    tiles = rows // LANES
    step = max(1, tiles // 6)
    blocks = [step]
    while tiles - sum(blocks) > step:
        blocks.append(step)
    last = tiles - sum(blocks)
    blocks += [last - last // 3, last // 3] if last > 2 else [last]
    return [LANES * n for n in blocks]


def project_kernel(many, width_all, count, narrow_count, *refs):
    stat_refs, refs = refs[:many], refs[many:]
    x_ref, gain_ref, w_ref, kv_ref, first_ref, kept_ref, sent_ref, normed, own, *blocks, sems = refs
    rows, width = x_ref.shape
    half = rows // 2
    block = rows // count
    sub_width = width // narrow_count
    sizes = [ref.shape[0] for ref in (first_ref, *blocks)]
    starts = [sum(sizes[:g]) for g in range(len(sizes))]
    fetches = [
        pltpu.make_async_copy(w_ref.at[start : start + size], ref, sems.at[g])
        for g, (start, size, ref) in enumerate(zip(starts[1:], sizes[1:], blocks))
    ]
    ahead = 3
    for fetch in fetches[:ahead]:
        fetch.start()
    me, narrow = lax.axis_index("wide"), lax.axis_index("narrow")
    stats = stat_refs[0][...]
    for ref in stat_refs[1:]:
        stats = stats + ref[...]
    row = lax.broadcasted_iota(jnp.int32, (rows, rows), 0)
    column = lax.broadcasted_iota(jnp.int32, (rows, rows), 1)
    sums = jnp.sum(jnp.where(row == column, stats[0:1, :], 0.0), axis=1, keepdims=True)
    squares = jnp.sum(jnp.where(row == column, stats[1:2, :], 0.0), axis=1, keepdims=True)
    center = sums / width_all
    spread = squares / width_all - center * center
    inverse = lax.rsqrt(spread + 1e-05)
    gain = gain_ref[...].reshape(1, width)
    order = halving_order(count)
    for j in range(count):
        pick = slice(j * block, (j + 1) * block)
        place = jnp.int32(0)
        for k, d in enumerate(order):
            place = jnp.where((me ^ d) == j, k, place)
        place = pl.multiple_of(place * block, 16)
        scaled = (x_ref[pick, :].astype(jnp.float32) - center[pick]) * inverse[pick] * gain
        normed[pl.ds(place, block), :] = scaled.astype(jnp.bfloat16)
    for j in range(narrow_count):
        @pl.when(narrow == j)
        def _(j=j):
            own[...] = normed[:, j * sub_width : (j + 1) * sub_width]

    queries = w_ref.shape[1]

    def products(source, start):
        got = jnp.dot(normed[:, start : start + source.shape[0]], source[...], preferred_element_type=jnp.float32)
        if start:
            kept_ref[:, :queries] += got[:half, :]
            sent_ref[:, :queries] += got[half:, :]
        else:
            kept_ref[:, :queries] = got[:half, :]
            sent_ref[:, :queries] = got[half:, :]

    fresh = jnp.dot(own[...], kv_ref[...], preferred_element_type=jnp.float32)
    kept_ref[:, queries:] = fresh[:half, :]
    sent_ref[:, queries:] = fresh[half:, :]
    products(first_ref, 0)
    for g, fetch in enumerate(fetches):
        fetch.wait()
        if g + ahead < len(fetches):
            fetches[g + ahead].start()
        products(blocks[g], starts[g + 1])


def project(stats, x, gain, w, kv, first, width_all, count, narrow_count):
    rows, width = x.shape
    queries = w.shape[1]
    blocks = row_blocks(width)[1:]
    half = jax.ShapeDtypeStruct((rows // 2, queries + kv.shape[1]), jnp.float32)
    return call(
        functools.partial(project_kernel, len(stats), width_all, count, narrow_count),
        (half, half),
        (*stats, x, gain, in_hbm(w), in_vmem(kv), in_vmem(first)),
        [FULL] * (len(stats) + 2) + [ANY] + [FULL] * 2,
        "project",
        scratch=[
            pltpu.VMEM((rows, width), jnp.bfloat16),
            pltpu.VMEM((rows, width // narrow_count), jnp.bfloat16),
            *[pltpu.VMEM((n, queries), jnp.bfloat16) for n in blocks],
            pltpu.SemaphoreType.DMA((len(blocks),)),
        ],
        limit=36,
        flops=2 * rows * width * queries,
        moved=2 * sum(blocks) * queries,
    )


def fold_kernel(kept_ref, came_ref, still_ref, sent_ref):
    half = still_ref.shape[0]
    still_ref[...] = kept_ref[:half, :] + came_ref[:half, :]
    sent_ref[...] = kept_ref[half:, :] + came_ref[half:, :]


def fold(kept, came):
    half = jax.ShapeDtypeStruct((kept.shape[0] // 2, kept.shape[1]), jnp.float32)
    return call(
        fold_kernel,
        (half, half),
        (kept, came),
        [FULL] * 2,
        "fold",
        flops=BESIDE,
    )


def split_kernel(queries, kept_ref, came_ref, *refs):
    out_refs, slots = refs[:-1], refs[-1]
    count = len(out_refs)
    narrow = lax.axis_index("narrow")
    total = kept_ref[...] + came_ref[...]
    rows, columns = total.shape[0] // count, total.shape[1]
    half = slots.shape[1]
    fresh = total[:, queries:]
    low = fresh - fresh.astype(jnp.bfloat16).astype(jnp.float32)
    for j in range(count):
        mine = slice(j * rows, (j + 1) * rows)
        slots[j * PAD : j * PAD + rows, :] = total[mine, :half]
        slots[j * PAD + rows : (j + 1) * PAD, : columns - half] = total[mine, half:]
        slots[j * PAD + rows : (j + 1) * PAD, columns - half :] = low[mine, :]
    for d, out_ref in enumerate(out_refs):
        out_ref[...] = slots[pl.ds(pl.multiple_of((narrow ^ d) * PAD, PAD), PAD), :].astype(jnp.bfloat16)


def attend_kernel(head_dim, count, lengths_ref, *refs):
    came_refs, kv_ref = refs[:count][::-1], refs[count]
    out_refs, (heads, contexts) = refs[count + 1 : 2 * count + 1], refs[2 * count + 1 :]
    rows, positions = kv_ref.shape[0], kv_ref.shape[1]
    half = came_refs[0].shape[1]
    queries = 2 * out_refs[0].shape[1]
    each = queries // head_dim
    slabs = head_dim // LANES
    group = each // 2
    half_heads = count * group
    scaling = 1.0 / math.sqrt(head_dim)
    terms = 0.0
    for d, ref in enumerate(came_refs):
        for c in range(0, half, LANES):
            both = ref[:, c : c + LANES].astype(jnp.float32)
            for column, part in ((c, both[:rows, :]), (half + c, both[rows:, :])):
                if column < queries:
                    h = column // head_dim
                    at = ((h // group) * half_heads + d * group + h % group) * PAD
                    heads[column % head_dim // LANES, at : at + rows, :] = part
        terms = terms + ref[:, queries - half :].astype(jnp.float32)[rows:, :]
    pair = 2 * head_dim
    fresh = terms[:, :pair] + terms[:, pair:]
    fresh = fresh.astype(jnp.bfloat16).astype(jnp.float32)
    place = lax.broadcasted_iota(jnp.int32, (2 * half_heads, positions), 1)
    for r in range(rows):
        query = jnp.concatenate([heads[k, pl.ds(r, 2 * half_heads, stride=PAD), :] for k in range(slabs)], axis=1)
        scores = (
            lax.dot_general(
                query.astype(jnp.bfloat16),
                kv_ref[r, :, :head_dim],
                (((1,), (1,)), ((), ())),
                preferred_element_type=jnp.float32,
            )
            * scaling
        )
        own_score = jnp.sum(query * fresh[r : r + 1, :head_dim], axis=1, keepdims=True) * scaling
        valid = place < lengths_ref[:, r : r + 1]
        top = jnp.maximum(jnp.max(jnp.where(valid, scores, -jnp.inf), axis=1, keepdims=True), own_score)
        weights = jnp.where(valid, jnp.exp(scores - top), 0.0)
        own_weight = jnp.exp(own_score - top)
        total = jnp.sum(weights, axis=1, keepdims=True) + own_weight
        numer = jnp.dot(weights.astype(jnp.bfloat16), kv_ref[r, :, head_dim:], preferred_element_type=jnp.float32)
        numer = numer + own_weight.astype(jnp.bfloat16).astype(jnp.float32) * fresh[r : r + 1, head_dim:]
        context = numer / total
        for k in range(slabs):
            for side in range(2):
                contexts[k, pl.ds(side * rows + r, half_heads, stride=PAD), :] = context[
                    side * half_heads : (side + 1) * half_heads, k * LANES : (k + 1) * LANES
                ]
    for d, ref in enumerate(out_refs):
        for h in range(group):
            at = (d * group + h) * PAD
            for k in range(slabs):
                start = h * head_dim + k * LANES
                ref[:, start : start + LANES] = contexts[k, at : at + PAD, :].astype(jnp.bfloat16)


def attend(lengths, came, kv, head_dim, queries):
    count = len(came)
    all_heads = count * queries // head_dim
    slabs = head_dim // LANES
    return call(
        functools.partial(attend_kernel, head_dim, count),
        [jax.ShapeDtypeStruct((PAD, queries // 2), jnp.bfloat16)] * count,
        (lengths, *came[::-1], in_vmem(kv)),
        [FULL] * (count + 2),
        "attend",
        scratch=[
            pltpu.VMEM((slabs, all_heads * PAD, LANES), jnp.float32),
            pltpu.VMEM((slabs, all_heads // 2 * PAD, LANES), jnp.float32),
        ],
        limit=8,
        flops=BESIDE,
    )


def join_kernel(*refs):
    count = len(refs) - 2
    out_ref, joined = refs[-2:]
    half = joined.shape[1]
    rows = out_ref.shape[0] // count
    for d in range(count):
        at = pl.ds(pl.multiple_of((lax.axis_index("narrow") ^ d) * PAD, PAD), PAD)
        joined[at, :] = refs[count - 1 - d][...].astype(jnp.float32)
    for side in range(2):
        came = [joined[j * PAD + side * rows : j * PAD + (side + 1) * rows, :] for j in range(count)]
        out_ref[:, side * half : (side + 1) * half] = jnp.concatenate(came, axis=0).astype(jnp.bfloat16)


def code(x, ref):
    largest = jnp.maximum(jnp.max(jnp.abs(x), axis=1, keepdims=True), TINY)
    power = jnp.floor(jnp.log2(largest)) + 1.0
    steps = jnp.round(x * (STEPS * jnp.exp2(-power)))
    ref[:, : x.shape[1]] = steps.astype(jnp.int32).astype(jnp.int16)
    ref[:, x.shape[1] :] = jnp.broadcast_to(power, (x.shape[0], LANES)).astype(jnp.int32).astype(jnp.int16)


def decode(ref, width):
    power = ref[:, width:].astype(jnp.int32).astype(jnp.float32)[:, 0:1]
    return ref[:, :width].astype(jnp.int32).astype(jnp.float32) * (jnp.exp2(power) * (1.0 / STEPS))


def output_kernel(start, count, narrow_count, *refs):
    x_refs, w_ref, (sums_ref, sent_ref) = refs[:count], refs[count], refs[-2:]
    block = x_refs[0].shape[0]
    ratio = count // narrow_count
    places = []
    for d in range(count):
        wide = lax.axis_index("wide") ^ d
        apart = (wide // ratio) ^ lax.axis_index("narrow")
        place = jnp.int32(0)
        for k, distance in enumerate(halving_order(narrow_count)):
            place = jnp.where(apart == distance, k, place)
        places.append(pl.multiple_of((place * ratio + wide % ratio) * block, block))
    x = jnp.concatenate([ref[...] for ref in x_refs], axis=0)
    got = jnp.dot(x, w_ref[:, start : start + sums_ref.shape[1]], preferred_element_type=jnp.float32)
    for d, place in enumerate(places):
        sums_ref[pl.ds(place, block), :] = got[d * block : (d + 1) * block, :]
    code(sums_ref[sums_ref.shape[0] // 2 :, :], sent_ref)


def output_part(blocks, w, start, columns, narrow_count, after):
    count = len(blocks)
    block, depth = blocks[0].shape
    rows = count * block
    return call(
        functools.partial(output_kernel, start, count, narrow_count),
        (
            jax.ShapeDtypeStruct((rows, columns), jnp.float32),
            jax.ShapeDtypeStruct((rows // 2, columns + LANES), jnp.int16),
        ),
        (*blocks, in_vmem(w), *after),
        [FULL] * (count + 1) + [ANY] * len(after),
        "output_part",
        limit=8,
        flops=2 * rows * depth * columns,
        moved=2 * rows * depth,
    )


def halve_kernel(sums_ref, came_ref, *refs):
    still_ref, sent_ref = refs[-2:]
    half = still_ref.shape[0]
    total = sums_ref[: 2 * half, :] + decode(came_ref, sums_ref.shape[1])
    still_ref[...] = total[:half, :]
    code(total[half:, :], sent_ref)


def halve(sums, came, after):
    rows, columns = came.shape[0], sums.shape[1]
    return call(
        halve_kernel,
        (
            jax.ShapeDtypeStruct((rows // 2, columns), jnp.float32),
            jax.ShapeDtypeStruct((rows // 2, columns + LANES), jnp.int16),
        ),
        (sums, came, *after),
        [FULL, FULL] + [ANY] * len(after),
        "halve",
        moved=16 * rows * columns,
    )


def finish_kernel(starts, kinds, *refs):
    out_ref = refs[-1]
    k = 0
    for at, kind in zip(starts, kinds):
        width = refs[k].shape[1]
        done = refs[k][...]
        if kind == 2:
            done = (done + decode(refs[k + 1], width)).astype(jnp.bfloat16)
        out_ref[:, at : at + width] = done
        k += kind


def finish(starts, cuts):
    parts = [x for cut in cuts for x in cut]
    rows, columns = parts[0].shape[0], sum(cut[0].shape[1] for cut in cuts)
    return call(
        functools.partial(finish_kernel, starts, [len(cut) for cut in cuts]),
        jax.ShapeDtypeStruct((rows, columns), jnp.bfloat16),
        parts,
        [FULL] * len(parts),
        "finish",
        moved=8 * columns * rows,
    )


def local(activations, norm_gain, query_weight, kv_weight, out_weight, kv_cache, lengths):
    wide_count = lax.axis_size("wide")
    narrow_count = lax.axis_size("narrow")
    own_rows, head_dim = kv_cache.shape[0], kv_cache.shape[2] // 2
    assert PAD == 2 * own_rows
    rows, width = activations.shape
    queries = query_weight.shape[1]
    columns = out_weight.shape[1]
    values = activations.astype(jnp.float32)
    stats = jnp.stack([jnp.sum(values, axis=1), jnp.sum(values * values, axis=1)])
    first_part = fetch(query_weight, row_blocks(width)[0], [stats])
    kept, sent = project(
        sent_apart(stats, "wide"),
        activations,
        norm_gain,
        query_weight,
        kv_weight,
        first_part,
        width * wide_count,
        wide_count,
        narrow_count,
    )
    d = 1
    while 2 * d < wide_count:
        kept, sent = fold(kept, swap(sent, "wide", d))
        d *= 2
    split = call(
        functools.partial(split_kernel, queries),
        [jax.ShapeDtypeStruct((PAD, queries // 2 + 2 * head_dim), jnp.bfloat16)] * narrow_count,
        (kept, swap(sent, "wide", d)),
        [FULL] * 2,
        "split",
        scratch=[pltpu.VMEM((narrow_count * PAD, queries // 2 + 2 * head_dim), jnp.float32)],
        flops=BESIDE,
    )
    context = attend(lengths[None], exchange(split, "narrow"), kv_cache, head_dim, queries)
    returned = call(
        join_kernel,
        jax.ShapeDtypeStruct((narrow_count * own_rows, queries), jnp.bfloat16),
        exchange(context, "narrow")[::-1],
        [FULL] * narrow_count,
        "join",
        scratch=[pltpu.VMEM((narrow_count * PAD, queries // 2), jnp.float32)],
        flops=BESIDE,
    )
    gathered = gather(returned, "wide")
    ends = [columns // LANES * k // 18 * LANES for k in (0, 7, 15, 18)]
    cut_sums, halved, last = [], [], []

    def exchange_cut(kept, sent, after):
        d = 1
        while 2 * d < narrow_count:
            kept, sent = halve(kept, swap(sent, "narrow", d), after)
            after = []
            d *= 2
        halved.append(kept)
        cut_sums.append((kept, swap(sent, "narrow", d)))

    for start, end in zip(ends, ends[1:]):
        kept, sent = output_part(gathered, out_weight, start, end - start, narrow_count, halved[-1:])
        if last:
            exchange_cut(*last, [kept])
        last = (kept, sent)
    early = finish([0], cut_sums[:1])
    exchange_cut(*last, [early])
    cut_sums[0] = (early,)
    return finish(ends[:-1], cut_sums)


def solution(mesh):
    return jax.shard_map(
        local,
        mesh=mesh,
        in_specs=(
            P("groups", "wide"),
            P("wide"),
            P("wide", "narrow"),
            P(("wide", "narrow"), None),
            P("narrow", "wide"),
            P(("groups", "wide", "narrow"), None, None),
            P(("groups", "wide", "narrow")),
        ),
        out_specs=P(("groups", "narrow"), "wide"),
        check_vma=False,
    )
```

```python
import functools
import math

import jax
import jax.numpy as jnp
from jax import lax
from jax.experimental import pallas as pl
from jax.experimental.pallas import tpu as pltpu
from jax.sharding import PartitionSpec as P

MIB = 1 << 20
FULL = pl.BlockSpec(memory_space=pltpu.VMEM)
ANY = pl.BlockSpec(memory_space=pl.ANY)
STEPS = 32700.0
TINY = 1e-37
LANES = 128
PAD = 8
BESIDE = 5 * 10**9


def call(kernel, outs, ins, specs, name, scratch=(), limit=4, flops=0, moved=0):
    return pl.pallas_call(
        kernel,
        out_shape=outs,
        in_specs=specs,
        out_specs=jax.tree.map(lambda _: FULL, outs),
        scratch_shapes=list(scratch),
        compiler_params=pltpu.CompilerParams(vmem_limit_bytes=limit * MIB),
        cost_estimate=pl.CostEstimate(flops=flops, bytes_accessed=moved, transcendentals=0),
        name=name,
    )(*ins)


def held(shape, dtype):
    return pltpu.VMEM(shape, dtype)


def in_vmem(x):
    return pltpu.with_memory_space_constraint(x, pltpu.VMEM)


def in_hbm(x):
    return pltpu.with_memory_space_constraint(x, pltpu.HBM)


def swap(x, axis, distance):
    count = lax.axis_size(axis)
    return lax.ppermute(x, axis, [(i, i ^ distance) for i in range(count)])


def sent_apart(x, axis):
    count = lax.axis_size(axis)
    if count <= 4:
        return [x] + [swap(x, axis, d) for d in range(1, count)]
    d = 1
    while d < count:
        x = x + swap(x, axis, d)
        d *= 2
    return [x]


def exchange(blocks, axis):
    far_first = {d: swap(blocks[d], axis, d) for d in range(len(blocks) - 1, 0, -1)}
    return [blocks[0]] + [far_first[d] for d in range(1, len(blocks))]


def gather(x, axis):
    count = lax.axis_size(axis)
    blocks = {0: x}
    d = count // 2
    while d:
        blocks |= {k ^ d: swap(b, axis, d) for k, b in blocks.items()}
        d //= 2
    return [blocks[k] for k in range(count)]


def halving_order(count):
    bits = count.bit_length() - 1
    return [sum(((k >> b) & 1) << (bits - 1 - b) for b in range(bits)) for k in range(count)]


class Halves:
    def __init__(self, source, start, target, sems, g):
        half = target.shape[0] // 2
        self.copies = [
            pltpu.make_async_copy(source.at[start + k * half : start + (k + 1) * half], target.at[pl.ds(k * half, half)], sems.at[g, k])
            for k in range(2)
        ]

    def start(self):
        for k, copy in enumerate(self.copies):
            copy.start(priority=k)

    def wait(self):
        for copy in self.copies:
            copy.wait()


def fetch_kernel(w_ref, *refs):
    share_ref, sems = refs[-2:]
    fetch = Halves(w_ref, 0, share_ref, sems, 0)
    fetch.start()
    fetch.wait()


def fetch(w, rows, after):
    return call(
        fetch_kernel,
        held((rows, w.shape[1]), w.dtype),
        (in_hbm(w), *after),
        [ANY] * (1 + len(after)),
        "fetch_query_weight",
        scratch=[pltpu.SemaphoreType.DMA((1, 2))],
        moved=2 * rows * w.shape[1],
    )


def row_blocks(rows):
    tiles = rows // LANES
    step = max(1, tiles // 6)
    blocks = [step]
    while tiles - sum(blocks) > step:
        blocks.append(step)
    last = tiles - sum(blocks)
    blocks += [last - last // 3, last // 3] if last > 2 else [last]
    return [LANES * n for n in blocks]


def project_kernel(many, width_all, count, narrow_count, *refs):
    stat_refs, refs = refs[:many], refs[many:]
    x_ref, gain_ref, w_ref, kv_ref, first_ref, kept_ref, sent_ref, normed, own, *blocks, sems = refs
    rows, width = x_ref.shape
    half = rows // 2
    block = rows // count
    sub_width = width // narrow_count
    sizes = [ref.shape[0] for ref in (first_ref, *blocks)]
    starts = [sum(sizes[:g]) for g in range(len(sizes))]
    fetches = [Halves(w_ref, start, ref, sems, g) for g, (start, ref) in enumerate(zip(starts[1:], blocks))]
    ahead = 3
    for fetch in fetches[:ahead]:
        fetch.start()
    me, narrow = lax.axis_index("wide"), lax.axis_index("narrow")
    stats = stat_refs[0][...]
    for ref in stat_refs[1:]:
        stats = stats + ref[...]
    row = lax.broadcasted_iota(jnp.int32, (rows, rows), 0)
    column = lax.broadcasted_iota(jnp.int32, (rows, rows), 1)
    sums = jnp.sum(jnp.where(row == column, stats[0:1, :], 0.0), axis=1, keepdims=True)
    squares = jnp.sum(jnp.where(row == column, stats[1:2, :], 0.0), axis=1, keepdims=True)
    center = sums / width_all
    spread = squares / width_all - center * center
    inverse = lax.rsqrt(spread + 1e-05)
    gain = gain_ref[...].reshape(1, width)
    order = halving_order(count)
    for j in range(count):
        pick = slice(j * block, (j + 1) * block)
        place = jnp.int32(0)
        for k, d in enumerate(order):
            place = jnp.where((me ^ d) == j, k, place)
        place = pl.multiple_of(place * block, 16)
        scaled = (x_ref[pick, :].astype(jnp.float32) - center[pick]) * inverse[pick] * gain
        normed[pl.ds(place, block), :] = scaled.astype(jnp.bfloat16)
    for j in range(narrow_count):
        @pl.when(narrow == j)
        def _(j=j):
            own[...] = normed[:, j * sub_width : (j + 1) * sub_width]

    queries = w_ref.shape[1]

    def products(source, start):
        got = jnp.dot(normed[:, start : start + source.shape[0]], source[...], preferred_element_type=jnp.float32)
        if start:
            kept_ref[:, :queries] += got[:half, :]
            sent_ref[:, :queries] += got[half:, :]
        else:
            kept_ref[:, :queries] = got[:half, :]
            sent_ref[:, :queries] = got[half:, :]

    fresh = jnp.dot(own[...], kv_ref[...], preferred_element_type=jnp.float32)
    kept_ref[:, queries:] = fresh[:half, :]
    sent_ref[:, queries:] = fresh[half:, :]
    products(first_ref, 0)
    for g, fetch in enumerate(fetches):
        fetch.wait()
        if g + ahead < len(fetches):
            fetches[g + ahead].start()
        products(blocks[g], starts[g + 1])


def project(stats, x, gain, w, kv, first, width_all, count, narrow_count):
    rows, width = x.shape
    queries = w.shape[1]
    blocks = row_blocks(width)[1:]
    half = jax.ShapeDtypeStruct((rows // 2, queries + kv.shape[1]), jnp.float32)
    return call(
        functools.partial(project_kernel, len(stats), width_all, count, narrow_count),
        (half, half),
        (*stats, x, gain, in_hbm(w), in_vmem(kv), in_vmem(first)),
        [FULL] * (len(stats) + 2) + [ANY] + [FULL] * 2,
        "project",
        scratch=[
            pltpu.VMEM((rows, width), jnp.bfloat16),
            pltpu.VMEM((rows, width // narrow_count), jnp.bfloat16),
            *[pltpu.VMEM((n, queries), jnp.bfloat16) for n in blocks],
            pltpu.SemaphoreType.DMA((len(blocks), 2)),
        ],
        limit=36,
        flops=2 * rows * width * queries,
        moved=2 * sum(blocks) * queries,
    )


def fold_kernel(kept_ref, came_ref, still_ref, sent_ref):
    half = still_ref.shape[0]
    still_ref[...] = kept_ref[:half, :] + came_ref[:half, :]
    sent_ref[...] = kept_ref[half:, :] + came_ref[half:, :]


def fold(kept, came):
    half = jax.ShapeDtypeStruct((kept.shape[0] // 2, kept.shape[1]), jnp.float32)
    return call(
        fold_kernel,
        (half, half),
        (kept, came),
        [FULL] * 2,
        "fold",
        flops=BESIDE,
    )


def split_kernel(queries, kept_ref, came_ref, *refs):
    out_refs, slots = refs[:-1], refs[-1]
    count = len(out_refs)
    narrow = lax.axis_index("narrow")
    total = kept_ref[...] + came_ref[...]
    rows, columns = total.shape[0] // count, total.shape[1]
    half = slots.shape[1]
    fresh = total[:, queries:]
    low = fresh - fresh.astype(jnp.bfloat16).astype(jnp.float32)
    for j in range(count):
        mine = slice(j * rows, (j + 1) * rows)
        slots[j * PAD : j * PAD + rows, :] = total[mine, :half]
        slots[j * PAD + rows : (j + 1) * PAD, : columns - half] = total[mine, half:]
        slots[j * PAD + rows : (j + 1) * PAD, columns - half :] = low[mine, :]
    for d, out_ref in enumerate(out_refs):
        out_ref[...] = slots[pl.ds(pl.multiple_of((narrow ^ d) * PAD, PAD), PAD), :].astype(jnp.bfloat16)


def attend_kernel(head_dim, count, lengths_ref, *refs):
    came_refs, kv_ref = refs[:count][::-1], refs[count]
    out_refs, (heads, contexts) = refs[count + 1 : 2 * count + 1], refs[2 * count + 1 :]
    rows, positions = kv_ref.shape[0], kv_ref.shape[1]
    half = came_refs[0].shape[1]
    queries = 2 * out_refs[0].shape[1]
    each = queries // head_dim
    slabs = head_dim // LANES
    group = each // 2
    half_heads = count * group
    scaling = 1.0 / math.sqrt(head_dim)
    terms = 0.0
    for d, ref in enumerate(came_refs):
        for c in range(0, half, LANES):
            both = ref[:, c : c + LANES].astype(jnp.float32)
            for column, part in ((c, both[:rows, :]), (half + c, both[rows:, :])):
                if column < queries:
                    h = column // head_dim
                    at = ((h // group) * half_heads + d * group + h % group) * PAD
                    heads[column % head_dim // LANES, at : at + rows, :] = part
        terms = terms + ref[:, queries - half :].astype(jnp.float32)[rows:, :]
    pair = 2 * head_dim
    fresh = terms[:, :pair] + terms[:, pair:]
    fresh = fresh.astype(jnp.bfloat16).astype(jnp.float32)
    place = lax.broadcasted_iota(jnp.int32, (2 * half_heads, positions), 1)
    for r in range(rows):
        query = jnp.concatenate([heads[k, pl.ds(r, 2 * half_heads, stride=PAD), :] for k in range(slabs)], axis=1)
        scores = (
            lax.dot_general(
                query.astype(jnp.bfloat16),
                kv_ref[r, :, :head_dim],
                (((1,), (1,)), ((), ())),
                preferred_element_type=jnp.float32,
            )
            * scaling
        )
        own_score = jnp.sum(query * fresh[r : r + 1, :head_dim], axis=1, keepdims=True) * scaling
        valid = place < lengths_ref[:, r : r + 1]
        top = jnp.maximum(jnp.max(jnp.where(valid, scores, -jnp.inf), axis=1, keepdims=True), own_score)
        weights = jnp.where(valid, jnp.exp(scores - top), 0.0)
        own_weight = jnp.exp(own_score - top)
        total = jnp.sum(weights, axis=1, keepdims=True) + own_weight
        numer = jnp.dot(weights.astype(jnp.bfloat16), kv_ref[r, :, head_dim:], preferred_element_type=jnp.float32)
        numer = numer + own_weight.astype(jnp.bfloat16).astype(jnp.float32) * fresh[r : r + 1, head_dim:]
        context = numer / total
        for k in range(slabs):
            for side in range(2):
                contexts[k, pl.ds(side * rows + r, half_heads, stride=PAD), :] = context[
                    side * half_heads : (side + 1) * half_heads, k * LANES : (k + 1) * LANES
                ]
    for d, ref in enumerate(out_refs):
        for h in range(group):
            at = (d * group + h) * PAD
            for k in range(slabs):
                start = h * head_dim + k * LANES
                ref[:, start : start + LANES] = contexts[k, at : at + PAD, :].astype(jnp.bfloat16)


def attend(lengths, came, kv, head_dim, queries):
    count = len(came)
    all_heads = count * queries // head_dim
    slabs = head_dim // LANES
    return call(
        functools.partial(attend_kernel, head_dim, count),
        [jax.ShapeDtypeStruct((PAD, queries // 2), jnp.bfloat16)] * count,
        (lengths, *came[::-1], in_vmem(kv)),
        [FULL] * (count + 2),
        "attend",
        scratch=[
            pltpu.VMEM((slabs, all_heads * PAD, LANES), jnp.float32),
            pltpu.VMEM((slabs, all_heads // 2 * PAD, LANES), jnp.float32),
        ],
        limit=8,
        flops=BESIDE,
    )


def join_kernel(*refs):
    count = len(refs) - 2
    out_ref, joined = refs[-2:]
    half = joined.shape[1]
    rows = out_ref.shape[0] // count
    for d in range(count):
        at = pl.ds(pl.multiple_of((lax.axis_index("narrow") ^ d) * PAD, PAD), PAD)
        joined[at, :] = refs[count - 1 - d][...].astype(jnp.float32)
    for side in range(2):
        came = [joined[j * PAD + side * rows : j * PAD + (side + 1) * rows, :] for j in range(count)]
        out_ref[:, side * half : (side + 1) * half] = jnp.concatenate(came, axis=0).astype(jnp.bfloat16)


def code(x, ref):
    largest = jnp.maximum(jnp.max(jnp.abs(x), axis=1, keepdims=True), TINY)
    power = jnp.floor(jnp.log2(largest)) + 1.0
    steps = jnp.round(x * (STEPS * jnp.exp2(-power)))
    ref[:, : x.shape[1]] = steps.astype(jnp.int32).astype(jnp.int16)
    ref[:, x.shape[1] :] = jnp.broadcast_to(power, (x.shape[0], LANES)).astype(jnp.int32).astype(jnp.int16)


def decode(ref, width):
    power = ref[:, width:].astype(jnp.int32).astype(jnp.float32)[:, 0:1]
    return ref[:, :width].astype(jnp.int32).astype(jnp.float32) * (jnp.exp2(power) * (1.0 / STEPS))


def output_kernel(start, count, narrow_count, *refs):
    x_refs, w_ref, (sums_ref, sent_ref) = refs[:count], refs[count], refs[-2:]
    block = x_refs[0].shape[0]
    ratio = count // narrow_count
    places = []
    for d in range(count):
        wide = lax.axis_index("wide") ^ d
        apart = (wide // ratio) ^ lax.axis_index("narrow")
        place = jnp.int32(0)
        for k, distance in enumerate(halving_order(narrow_count)):
            place = jnp.where(apart == distance, k, place)
        places.append(pl.multiple_of((place * ratio + wide % ratio) * block, block))
    x = jnp.concatenate([ref[...] for ref in x_refs], axis=0)
    got = jnp.dot(x, w_ref[:, start : start + sums_ref.shape[1]], preferred_element_type=jnp.float32)
    for d, place in enumerate(places):
        sums_ref[pl.ds(place, block), :] = got[d * block : (d + 1) * block, :]
    code(sums_ref[sums_ref.shape[0] // 2 :, :], sent_ref)


def output_part(blocks, w, start, columns, narrow_count, after):
    count = len(blocks)
    block, depth = blocks[0].shape
    rows = count * block
    return call(
        functools.partial(output_kernel, start, count, narrow_count),
        (
            jax.ShapeDtypeStruct((rows, columns), jnp.float32),
            jax.ShapeDtypeStruct((rows // 2, columns + LANES), jnp.int16),
        ),
        (*blocks, in_vmem(w), *after),
        [FULL] * (count + 1) + [ANY] * len(after),
        "output_part",
        limit=8,
        flops=2 * rows * depth * columns,
        moved=2 * rows * depth,
    )


def halve_kernel(sums_ref, came_ref, *refs):
    still_ref, sent_ref = refs[-2:]
    half = still_ref.shape[0]
    total = sums_ref[: 2 * half, :] + decode(came_ref, sums_ref.shape[1])
    still_ref[...] = total[:half, :]
    code(total[half:, :], sent_ref)


def halve(sums, came, after):
    rows, columns = came.shape[0], sums.shape[1]
    return call(
        halve_kernel,
        (
            jax.ShapeDtypeStruct((rows // 2, columns), jnp.float32),
            jax.ShapeDtypeStruct((rows // 2, columns + LANES), jnp.int16),
        ),
        (sums, came, *after),
        [FULL, FULL] + [ANY] * len(after),
        "halve",
        moved=16 * rows * columns,
    )


def finish_kernel(start, kept_ref, came_ref, *refs):
    out_ref, done, sem = refs[-3:]
    width = kept_ref.shape[1]
    done[...] = (kept_ref[...] + decode(came_ref, width)).astype(jnp.bfloat16)
    copy = pltpu.make_async_copy(done, out_ref.at[:, start : start + width], sem)
    copy.start()
    copy.wait()


def finish(kept, came, start, columns, result):
    rows, width = kept.shape
    return pl.pallas_call(
        functools.partial(finish_kernel, start),
        out_shape=pltpu.HBM((rows, columns), jnp.bfloat16),
        in_specs=[FULL, FULL] + [ANY] * (result is not None),
        out_specs=ANY,
        scratch_shapes=[pltpu.VMEM((rows, width), jnp.bfloat16), pltpu.SemaphoreType.DMA],
        input_output_aliases={} if result is None else {2: 0},
        compiler_params=pltpu.CompilerParams(vmem_limit_bytes=4 * MIB),
        cost_estimate=pl.CostEstimate(flops=0, bytes_accessed=8 * rows * width, transcendentals=0),
        name="finish",
    )(kept, came, *([] if result is None else [in_hbm(result)]))


def local(activations, norm_gain, query_weight, kv_weight, out_weight, kv_cache, lengths):
    wide_count = lax.axis_size("wide")
    narrow_count = lax.axis_size("narrow")
    own_rows, head_dim = kv_cache.shape[0], kv_cache.shape[2] // 2
    assert PAD == 2 * own_rows
    rows, width = activations.shape
    queries = query_weight.shape[1]
    columns = out_weight.shape[1]
    values = activations.astype(jnp.float32)
    stats = jnp.stack([jnp.sum(values, axis=1), jnp.sum(values * values, axis=1)])
    first_part = fetch(query_weight, row_blocks(width)[0], [stats])
    kept, sent = project(
        sent_apart(stats, "wide"),
        activations,
        norm_gain,
        query_weight,
        kv_weight,
        first_part,
        width * wide_count,
        wide_count,
        narrow_count,
    )
    d = 1
    while 2 * d < wide_count:
        kept, sent = fold(kept, swap(sent, "wide", d))
        d *= 2
    split = call(
        functools.partial(split_kernel, queries),
        [jax.ShapeDtypeStruct((PAD, queries // 2 + 2 * head_dim), jnp.bfloat16)] * narrow_count,
        (kept, swap(sent, "wide", d)),
        [FULL] * 2,
        "split",
        scratch=[pltpu.VMEM((narrow_count * PAD, queries // 2 + 2 * head_dim), jnp.float32)],
        flops=BESIDE,
    )
    context = attend(lengths[None], exchange(split, "narrow"), kv_cache, head_dim, queries)
    returned = call(
        join_kernel,
        jax.ShapeDtypeStruct((narrow_count * own_rows, queries), jnp.bfloat16),
        exchange(context, "narrow")[::-1],
        [FULL] * narrow_count,
        "join",
        scratch=[pltpu.VMEM((narrow_count * PAD, queries // 2), jnp.float32)],
        flops=BESIDE,
    )
    gathered = gather(returned, "wide")
    ends = [columns // LANES * k // 18 * LANES for k in (0,7,15,18)]
    cut_sums, halved, last = [], [], []

    def exchange_cut(kept, sent, after):
        d = 1
        while 2 * d < narrow_count:
            kept, sent = halve(kept, swap(sent, "narrow", d), after)
            after = []
            d *= 2
        halved.append(kept)
        cut_sums.append((kept, swap(sent, "narrow", d)))

    for start, end in zip(ends, ends[1:]):
        kept, sent = output_part(gathered, out_weight, start, end - start, narrow_count, halved[-1:])
        if last:
            exchange_cut(*last, [kept])
        last = (kept, sent)
    result = finish(*cut_sums[0], ends[0], columns, None)
    exchange_cut(*last, [in_hbm(result)])
    for cut, start in zip(cut_sums[1:], ends[1:]):
        result = finish(*cut, start, columns, result)
    return result


def solution(mesh):
    return jax.shard_map(
        local,
        mesh=mesh,
        in_specs=(
            P("groups", "wide"),
            P("wide"),
            P("wide", "narrow"),
            P(("wide", "narrow"), None),
            P("narrow", "wide"),
            P(("groups", "wide", "narrow"), None, None),
            P(("groups", "wide", "narrow")),
        ),
        out_specs=P(("groups", "narrow"), "wide"),
        check_vma=False,
    )
```

```python
import functools
import math

import jax
import jax.numpy as jnp
from jax import lax
from jax.experimental import pallas as pl
from jax.experimental.pallas import tpu as pltpu
from jax.sharding import PartitionSpec as P

MIB = 1 << 20
FULL = pl.BlockSpec(memory_space=pltpu.VMEM)
ANY = pl.BlockSpec(memory_space=pl.ANY)
STEPS = 32700.0
TINY = 1e-37
LANES = 128
PAD = 8
BESIDE = 5 * 10**9


def call(kernel, outs, ins, specs, name, scratch=(), limit=4, flops=0, moved=0):
    return pl.pallas_call(
        kernel,
        out_shape=outs,
        in_specs=specs,
        out_specs=jax.tree.map(lambda _: FULL, outs),
        scratch_shapes=list(scratch),
        compiler_params=pltpu.CompilerParams(vmem_limit_bytes=limit * MIB),
        cost_estimate=pl.CostEstimate(flops=flops, bytes_accessed=moved, transcendentals=0),
        name=name,
    )(*ins)


def held(shape, dtype):
    return pltpu.VMEM(shape, dtype)


def in_vmem(x):
    return pltpu.with_memory_space_constraint(x, pltpu.VMEM)


def in_hbm(x):
    return pltpu.with_memory_space_constraint(x, pltpu.HBM)


def swap(x, axis, distance):
    count = lax.axis_size(axis)
    return lax.ppermute(x, axis, [(i, i ^ distance) for i in range(count)])


def sent_apart(x, axis):
    count = lax.axis_size(axis)
    if count <= 4:
        return [x] + [swap(x, axis, d) for d in range(1, count)]
    d = 1
    while d < count:
        x = x + swap(x, axis, d)
        d *= 2
    return [x]


def start_order(count):
    return sorted(range(1, count), key=lambda d: (d != count // 2, -d))


def exchange(blocks, axis):
    return [swap(blocks[d], axis, d) for d in start_order(len(blocks))] + [blocks[0]]


def by_distance(came):
    order = start_order(len(came)) + [0]
    return [came[order.index(d)] for d in range(len(came))]


def gather(x, axis):
    count = lax.axis_size(axis)
    blocks = {0: x}
    d = count // 2
    while d:
        blocks |= {k ^ d: swap(b, axis, d) for k, b in blocks.items()}
        d //= 2
    return [blocks[k] for k in range(count)]


def halving_order(count):
    bits = count.bit_length() - 1
    return [sum(((k >> b) & 1) << (bits - 1 - b) for b in range(bits)) for k in range(count)]


def fetch_kernel(w_ref, *refs):
    share_ref, sem = refs[-2:]
    fetch = pltpu.make_async_copy(w_ref.at[: share_ref.shape[0]], share_ref, sem)
    fetch.start()
    fetch.wait()


def fetch(w, rows, after):
    return call(
        fetch_kernel,
        held((rows, w.shape[1]), w.dtype),
        (in_hbm(w), *after),
        [ANY] * (1 + len(after)),
        "fetch_query_weight",
        scratch=[pltpu.SemaphoreType.DMA],
        moved=2 * rows * w.shape[1],
    )


def row_blocks(rows):
    tiles = rows // LANES
    step = max(1, tiles // 6)
    blocks = [step]
    while tiles - sum(blocks) > step:
        blocks.append(step)
    last = tiles - sum(blocks)
    blocks += [last - last // 3, last // 3] if last > 2 else [last]
    return [LANES * n for n in blocks]


def project_kernel(many, width_all, count, narrow_count, *refs):
    stat_refs, refs = refs[:many], refs[many:]
    x_ref, gain_ref, w_ref, kv_ref, first_ref, kept_ref, sent_ref, normed, own, *blocks, sems = refs
    rows, width = x_ref.shape
    half = rows // 2
    block = rows // count
    sub_width = width // narrow_count
    sizes = [ref.shape[0] for ref in (first_ref, *blocks)]
    starts = [sum(sizes[:g]) for g in range(len(sizes))]
    fetches = [
        pltpu.make_async_copy(w_ref.at[start : start + size], ref, sems.at[g])
        for g, (start, size, ref) in enumerate(zip(starts[1:], sizes[1:], blocks))
    ]
    ahead = 3
    for fetch in fetches[:ahead]:
        fetch.start()
    me, narrow = lax.axis_index("wide"), lax.axis_index("narrow")
    stats = stat_refs[0][...]
    for ref in stat_refs[1:]:
        stats = stats + ref[...]
    row = lax.broadcasted_iota(jnp.int32, (rows, rows), 0)
    column = lax.broadcasted_iota(jnp.int32, (rows, rows), 1)
    sums = jnp.sum(jnp.where(row == column, stats[0:1, :], 0.0), axis=1, keepdims=True)
    squares = jnp.sum(jnp.where(row == column, stats[1:2, :], 0.0), axis=1, keepdims=True)
    center = sums / width_all
    spread = squares / width_all - center * center
    inverse = lax.rsqrt(spread + 1e-05)
    gain = gain_ref[...].reshape(1, width)
    order = halving_order(count)
    for j in range(count):
        pick = slice(j * block, (j + 1) * block)
        place = jnp.int32(0)
        for k, d in enumerate(order):
            place = jnp.where((me ^ d) == j, k, place)
        place = pl.multiple_of(place * block, 16)
        scaled = (x_ref[pick, :].astype(jnp.float32) - center[pick]) * inverse[pick] * gain
        normed[pl.ds(place, block), :] = scaled.astype(jnp.bfloat16)
    for j in range(narrow_count):
        @pl.when(narrow == j)
        def _(j=j):
            own[...] = normed[:, j * sub_width : (j + 1) * sub_width]

    queries = w_ref.shape[1]

    def products(source, start):
        got = jnp.dot(normed[:, start : start + source.shape[0]], source[...], preferred_element_type=jnp.float32)
        if start:
            kept_ref[:, :queries] += got[:half, :]
            sent_ref[:, :queries] += got[half:, :]
        else:
            kept_ref[:, :queries] = got[:half, :]
            sent_ref[:, :queries] = got[half:, :]

    fresh = jnp.dot(own[...], kv_ref[...], preferred_element_type=jnp.float32)
    kept_ref[:, queries:] = fresh[:half, :]
    sent_ref[:, queries:] = fresh[half:, :]
    products(first_ref, 0)
    for g, fetch in enumerate(fetches):
        fetch.wait()
        if g + ahead < len(fetches):
            fetches[g + ahead].start()
        products(blocks[g], starts[g + 1])


def project(stats, x, gain, w, kv, first, width_all, count, narrow_count):
    rows, width = x.shape
    queries = w.shape[1]
    blocks = row_blocks(width)[1:]
    half = jax.ShapeDtypeStruct((rows // 2, queries + kv.shape[1]), jnp.float32)
    return call(
        functools.partial(project_kernel, len(stats), width_all, count, narrow_count),
        (half, half),
        (*stats, x, gain, in_hbm(w), in_vmem(kv), in_vmem(first)),
        [FULL] * (len(stats) + 2) + [ANY] + [FULL] * 2,
        "project",
        scratch=[
            pltpu.VMEM((rows, width), jnp.bfloat16),
            pltpu.VMEM((rows, width // narrow_count), jnp.bfloat16),
            *[pltpu.VMEM((n, queries), jnp.bfloat16) for n in blocks],
            pltpu.SemaphoreType.DMA((len(blocks),)),
        ],
        limit=36,
        flops=2 * rows * width * queries,
        moved=2 * sum(blocks) * queries,
    )


def fold_kernel(kept_ref, came_ref, still_ref, sent_ref):
    half = still_ref.shape[0]
    still_ref[...] = kept_ref[:half, :] + came_ref[:half, :]
    sent_ref[...] = kept_ref[half:, :] + came_ref[half:, :]


def fold(kept, came):
    half = jax.ShapeDtypeStruct((kept.shape[0] // 2, kept.shape[1]), jnp.float32)
    return call(
        fold_kernel,
        (half, half),
        (kept, came),
        [FULL] * 2,
        "fold",
        flops=BESIDE,
    )


def split_kernel(queries, kept_ref, came_ref, *refs):
    out_refs, slots = refs[:-1], refs[-1]
    count = len(out_refs)
    narrow = lax.axis_index("narrow")
    total = kept_ref[...] + came_ref[...]
    rows, columns = total.shape[0] // count, total.shape[1]
    half = slots.shape[1]
    fresh = total[:, queries:]
    low = fresh - fresh.astype(jnp.bfloat16).astype(jnp.float32)
    for j in range(count):
        mine = slice(j * rows, (j + 1) * rows)
        slots[j * PAD : j * PAD + rows, :] = total[mine, :half]
        slots[j * PAD + rows : (j + 1) * PAD, : columns - half] = total[mine, half:]
        slots[j * PAD + rows : (j + 1) * PAD, columns - half :] = low[mine, :]
    for d, out_ref in enumerate(out_refs):
        out_ref[...] = slots[pl.ds(pl.multiple_of((narrow ^ d) * PAD, PAD), PAD), :].astype(jnp.bfloat16)


def attend_kernel(head_dim, count, lengths_ref, *refs):
    came_refs, kv_ref = by_distance(refs[:count]), refs[count]
    out_refs, (heads, contexts) = refs[count + 1 : 2 * count + 1], refs[2 * count + 1 :]
    rows, positions = kv_ref.shape[0], kv_ref.shape[1]
    half = came_refs[0].shape[1]
    queries = 2 * out_refs[0].shape[1]
    each = queries // head_dim
    slabs = head_dim // LANES
    group = each // 2
    half_heads = count * group
    scaling = 1.0 / math.sqrt(head_dim)
    terms = 0.0
    for d, ref in enumerate(came_refs):
        for c in range(0, half, LANES):
            both = ref[:, c : c + LANES].astype(jnp.float32)
            for column, part in ((c, both[:rows, :]), (half + c, both[rows:, :])):
                if column < queries:
                    h = column // head_dim
                    at = ((h // group) * half_heads + d * group + h % group) * PAD
                    heads[column % head_dim // LANES, at : at + rows, :] = part
        terms = terms + ref[:, queries - half :].astype(jnp.float32)[rows:, :]
    pair = 2 * head_dim
    fresh = terms[:, :pair] + terms[:, pair:]
    fresh = fresh.astype(jnp.bfloat16).astype(jnp.float32)
    place = lax.broadcasted_iota(jnp.int32, (2 * half_heads, positions), 1)
    for r in range(rows):
        query = jnp.concatenate([heads[k, pl.ds(r, 2 * half_heads, stride=PAD), :] for k in range(slabs)], axis=1)
        scores = (
            lax.dot_general(
                query.astype(jnp.bfloat16),
                kv_ref[r, :, :head_dim],
                (((1,), (1,)), ((), ())),
                preferred_element_type=jnp.float32,
            )
            * scaling
        )
        own_score = jnp.sum(query * fresh[r : r + 1, :head_dim], axis=1, keepdims=True) * scaling
        valid = place < lengths_ref[:, r : r + 1]
        top = jnp.maximum(jnp.max(jnp.where(valid, scores, -jnp.inf), axis=1, keepdims=True), own_score)
        weights = jnp.where(valid, jnp.exp(scores - top), 0.0)
        own_weight = jnp.exp(own_score - top)
        total = jnp.sum(weights, axis=1, keepdims=True) + own_weight
        numer = jnp.dot(weights.astype(jnp.bfloat16), kv_ref[r, :, head_dim:], preferred_element_type=jnp.float32)
        numer = numer + own_weight.astype(jnp.bfloat16).astype(jnp.float32) * fresh[r : r + 1, head_dim:]
        context = numer / total
        for k in range(slabs):
            for side in range(2):
                contexts[k, pl.ds(side * rows + r, half_heads, stride=PAD), :] = context[
                    side * half_heads : (side + 1) * half_heads, k * LANES : (k + 1) * LANES
                ]
    for d, ref in enumerate(out_refs):
        for h in range(group):
            at = (d * group + h) * PAD
            for k in range(slabs):
                start = h * head_dim + k * LANES
                ref[:, start : start + LANES] = contexts[k, at : at + PAD, :].astype(jnp.bfloat16)


def attend(lengths, came, kv, head_dim, queries):
    count = len(came)
    all_heads = count * queries // head_dim
    slabs = head_dim // LANES
    return call(
        functools.partial(attend_kernel, head_dim, count),
        [jax.ShapeDtypeStruct((PAD, queries // 2), jnp.bfloat16)] * count,
        (lengths, *came, in_vmem(kv)),
        [FULL] * (count + 2),
        "attend",
        scratch=[
            pltpu.VMEM((slabs, all_heads * PAD, LANES), jnp.float32),
            pltpu.VMEM((slabs, all_heads // 2 * PAD, LANES), jnp.float32),
        ],
        limit=8,
        flops=BESIDE,
    )


def join_kernel(*refs):
    count = len(refs) - 2
    out_ref, joined = refs[-2:]
    half = joined.shape[1]
    rows = out_ref.shape[0] // count
    for d, ref in enumerate(by_distance(refs[:count])):
        at = pl.ds(pl.multiple_of((lax.axis_index("narrow") ^ d) * PAD, PAD), PAD)
        joined[at, :] = ref[...].astype(jnp.float32)
    for side in range(2):
        came = [joined[j * PAD + side * rows : j * PAD + (side + 1) * rows, :] for j in range(count)]
        out_ref[:, side * half : (side + 1) * half] = jnp.concatenate(came, axis=0).astype(jnp.bfloat16)


def code(x, ref):
    largest = jnp.maximum(jnp.max(jnp.abs(x), axis=1, keepdims=True), TINY)
    power = jnp.floor(jnp.log2(largest)) + 1.0
    steps = jnp.round(x * (STEPS * jnp.exp2(-power)))
    ref[:, : x.shape[1]] = steps.astype(jnp.int32).astype(jnp.int16)
    ref[:, x.shape[1] :] = jnp.broadcast_to(power, (x.shape[0], LANES)).astype(jnp.int32).astype(jnp.int16)


def decode(ref, width):
    power = ref[:, width:].astype(jnp.int32).astype(jnp.float32)[:, 0:1]
    return ref[:, :width].astype(jnp.int32).astype(jnp.float32) * (jnp.exp2(power) * (1.0 / STEPS))


def output_kernel(start, count, narrow_count, *refs):
    x_refs, w_ref, (sums_ref, sent_ref) = refs[:count], refs[count], refs[-2:]
    block = x_refs[0].shape[0]
    ratio = count // narrow_count
    places = []
    for d in range(count):
        wide = lax.axis_index("wide") ^ d
        apart = (wide // ratio) ^ lax.axis_index("narrow")
        place = jnp.int32(0)
        for k, distance in enumerate(halving_order(narrow_count)):
            place = jnp.where(apart == distance, k, place)
        places.append(pl.multiple_of((place * ratio + wide % ratio) * block, block))
    x = jnp.concatenate([ref[...] for ref in x_refs], axis=0)
    got = jnp.dot(x, w_ref[:, start : start + sums_ref.shape[1]], preferred_element_type=jnp.float32)
    for d, place in enumerate(places):
        sums_ref[pl.ds(place, block), :] = got[d * block : (d + 1) * block, :]
    code(sums_ref[sums_ref.shape[0] // 2 :, :], sent_ref)


def output_part(blocks, w, start, columns, narrow_count, after):
    count = len(blocks)
    block, depth = blocks[0].shape
    rows = count * block
    return call(
        functools.partial(output_kernel, start, count, narrow_count),
        (
            jax.ShapeDtypeStruct((rows, columns), jnp.float32),
            jax.ShapeDtypeStruct((rows // 2, columns + LANES), jnp.int16),
        ),
        (*blocks, in_vmem(w), *after),
        [FULL] * (count + 1) + [ANY] * len(after),
        "output_part",
        limit=8,
        flops=2 * rows * depth * columns,
        moved=2 * rows * depth,
    )


def halve_kernel(sums_ref, came_ref, *refs):
    still_ref, sent_ref = refs[-2:]
    half = still_ref.shape[0]
    total = sums_ref[: 2 * half, :] + decode(came_ref, sums_ref.shape[1])
    still_ref[...] = total[:half, :]
    code(total[half:, :], sent_ref)


def halve(sums, came, after):
    rows, columns = came.shape[0], sums.shape[1]
    return call(
        halve_kernel,
        (
            jax.ShapeDtypeStruct((rows // 2, columns), jnp.float32),
            jax.ShapeDtypeStruct((rows // 2, columns + LANES), jnp.int16),
        ),
        (sums, came, *after),
        [FULL, FULL] + [ANY] * len(after),
        "halve",
        moved=16 * rows * columns,
    )


def finish_kernel(start, kept_ref, came_ref, *refs):
    out_ref, done, sem = refs[-3:]
    width = kept_ref.shape[1]
    done[...] = (kept_ref[...] + decode(came_ref, width)).astype(jnp.bfloat16)
    copy = pltpu.make_async_copy(done, out_ref.at[:, start : start + width], sem)
    copy.start()
    copy.wait()


def finish(kept, came, start, columns, result):
    rows, width = kept.shape
    return pl.pallas_call(
        functools.partial(finish_kernel, start),
        out_shape=pltpu.HBM((rows, columns), jnp.bfloat16),
        in_specs=[FULL, FULL] + [ANY] * (result is not None),
        out_specs=ANY,
        scratch_shapes=[pltpu.VMEM((rows, width), jnp.bfloat16), pltpu.SemaphoreType.DMA],
        input_output_aliases={} if result is None else {2: 0},
        compiler_params=pltpu.CompilerParams(vmem_limit_bytes=4 * MIB),
        cost_estimate=pl.CostEstimate(flops=0, bytes_accessed=8 * rows * width, transcendentals=0),
        name="finish",
    )(kept, came, *([] if result is None else [in_hbm(result)]))


def local(activations, norm_gain, query_weight, kv_weight, out_weight, kv_cache, lengths):
    wide_count = lax.axis_size("wide")
    narrow_count = lax.axis_size("narrow")
    own_rows, head_dim = kv_cache.shape[0], kv_cache.shape[2] // 2
    assert PAD == 2 * own_rows
    rows, width = activations.shape
    queries = query_weight.shape[1]
    columns = out_weight.shape[1]
    values = activations.astype(jnp.float32)
    stats = jnp.stack([jnp.sum(values, axis=1), jnp.sum(values * values, axis=1)])
    first_part = fetch(query_weight, row_blocks(width)[0], [stats])
    kept, sent = project(
        sent_apart(stats, "wide"),
        activations,
        norm_gain,
        query_weight,
        kv_weight,
        first_part,
        width * wide_count,
        wide_count,
        narrow_count,
    )
    d = 1
    while 2 * d < wide_count:
        kept, sent = fold(kept, swap(sent, "wide", d))
        d *= 2
    split = call(
        functools.partial(split_kernel, queries),
        [jax.ShapeDtypeStruct((PAD, queries // 2 + 2 * head_dim), jnp.bfloat16)] * narrow_count,
        (kept, swap(sent, "wide", d)),
        [FULL] * 2,
        "split",
        scratch=[pltpu.VMEM((narrow_count * PAD, queries // 2 + 2 * head_dim), jnp.float32)],
        flops=BESIDE,
    )
    context = attend(lengths[None], exchange(split, "narrow"), kv_cache, head_dim, queries)
    returned = call(
        join_kernel,
        jax.ShapeDtypeStruct((narrow_count * own_rows, queries), jnp.bfloat16),
        exchange(context, "narrow"),
        [FULL] * narrow_count,
        "join",
        scratch=[pltpu.VMEM((narrow_count * PAD, queries // 2), jnp.float32)],
        flops=BESIDE,
    )
    gathered = gather(returned, "wide")
    ends = [columns // LANES * k // 18 * LANES for k in (0,7,15,18)]
    cut_sums, halved, last = [], [], []

    def exchange_cut(kept, sent, after):
        d = 1
        while 2 * d < narrow_count:
            kept, sent = halve(kept, swap(sent, "narrow", d), after)
            after = []
            d *= 2
        halved.append(kept)
        cut_sums.append((kept, swap(sent, "narrow", d)))

    for start, end in zip(ends, ends[1:]):
        kept, sent = output_part(gathered, out_weight, start, end - start, narrow_count, halved[-1:])
        if last:
            exchange_cut(*last, [kept])
        last = (kept, sent)
    result = finish(*cut_sums[0], ends[0], columns, None)
    exchange_cut(*last, [in_hbm(result)])
    for cut, start in zip(cut_sums[1:], ends[1:]):
        result = finish(*cut, start, columns, result)
    return result


def solution(mesh):
    return jax.shard_map(
        local,
        mesh=mesh,
        in_specs=(
            P("groups", "wide"),
            P("wide"),
            P("wide", "narrow"),
            P(("wide", "narrow"), None),
            P("narrow", "wide"),
            P(("groups", "wide", "narrow"), None, None),
            P(("groups", "wide", "narrow")),
        ),
        out_specs=P(("groups", "narrow"), "wide"),
        check_vma=False,
    )
```

```python
import functools
import math

import jax
import jax.numpy as jnp
from jax import lax
from jax.experimental import pallas as pl
from jax.experimental.pallas import tpu as pltpu
from jax.sharding import PartitionSpec as P

MIB = 1 << 20
FULL = pl.BlockSpec(memory_space=pltpu.VMEM)
ANY = pl.BlockSpec(memory_space=pl.ANY)
STEPS = 32700.0
TINY = 1e-37
LANES = 128
PAD = 8
BESIDE = 5 * 10**9


def call(kernel, outs, ins, specs, name, scratch=(), limit=4, flops=0, moved=0):
    return pl.pallas_call(
        kernel,
        out_shape=outs,
        in_specs=specs,
        out_specs=jax.tree.map(lambda _: FULL, outs),
        scratch_shapes=list(scratch),
        compiler_params=pltpu.CompilerParams(vmem_limit_bytes=limit * MIB),
        cost_estimate=pl.CostEstimate(flops=flops, bytes_accessed=moved, transcendentals=0),
        name=name,
    )(*ins)


def held(shape, dtype):
    return pltpu.VMEM(shape, dtype)


def in_vmem(x):
    return pltpu.with_memory_space_constraint(x, pltpu.VMEM)


def in_hbm(x):
    return pltpu.with_memory_space_constraint(x, pltpu.HBM)


def swap(x, axis, distance):
    count = lax.axis_size(axis)
    return lax.ppermute(x, axis, [(i, i ^ distance) for i in range(count)])


def sent_apart(x, axis):
    count = lax.axis_size(axis)
    if count <= 4:
        return [x] + [swap(x, axis, d) for d in range(1, count)]
    d = 1
    while d < count:
        x = x + swap(x, axis, d)
        d *= 2
    return [x]


def start_order(count, half_first):
    return sorted(range(1, count), key=lambda d: (half_first and d != count // 2, -d))


def exchange(blocks, axis, half_first=False):
    return [swap(blocks[d], axis, d) for d in start_order(len(blocks), half_first)] + [blocks[0]]


def by_distance(came, half_first=False):
    order = start_order(len(came), half_first) + [0]
    return [came[order.index(d)] for d in range(len(came))]


def gather(x, axis):
    count = lax.axis_size(axis)
    blocks = {0: x}
    d = count // 2
    while d:
        blocks |= {k ^ d: swap(b, axis, d) for k, b in blocks.items()}
        d //= 2
    return [blocks[k] for k in range(count)]


def halving_order(count):
    bits = count.bit_length() - 1
    return [sum(((k >> b) & 1) << (bits - 1 - b) for b in range(bits)) for k in range(count)]


def fetch_kernel(w_ref, *refs):
    share_ref, sem = refs[-2:]
    fetch = pltpu.make_async_copy(w_ref.at[: share_ref.shape[0]], share_ref, sem)
    fetch.start()
    fetch.wait()


def fetch(w, rows, after):
    return call(
        fetch_kernel,
        held((rows, w.shape[1]), w.dtype),
        (in_hbm(w), *after),
        [ANY] * (1 + len(after)),
        "fetch_query_weight",
        scratch=[pltpu.SemaphoreType.DMA],
        moved=2 * rows * w.shape[1],
    )


def row_blocks(rows):
    tiles = rows // LANES
    step = max(1, tiles // 6)
    blocks = [step]
    while tiles - sum(blocks) > step:
        blocks.append(step)
    last = tiles - sum(blocks)
    blocks += [last - last // 3, last // 3] if last > 2 else [last]
    return [LANES * n for n in blocks]


def project_kernel(many, width_all, count, narrow_count, *refs):
    stat_refs, refs = refs[:many], refs[many:]
    x_ref, gain_ref, w_ref, kv_ref, first_ref, kept_ref, sent_ref, normed, own, *blocks, sems = refs
    rows, width = x_ref.shape
    half = rows // 2
    block = rows // count
    sub_width = width // narrow_count
    sizes = [ref.shape[0] for ref in (first_ref, *blocks)]
    starts = [sum(sizes[:g]) for g in range(len(sizes))]
    fetches = [
        pltpu.make_async_copy(w_ref.at[start : start + size], ref, sems.at[g])
        for g, (start, size, ref) in enumerate(zip(starts[1:], sizes[1:], blocks))
    ]
    ahead = 3
    for fetch in fetches[:ahead]:
        fetch.start()
    me, narrow = lax.axis_index("wide"), lax.axis_index("narrow")
    stats = stat_refs[0][...]
    for ref in stat_refs[1:]:
        stats = stats + ref[...]
    row = lax.broadcasted_iota(jnp.int32, (rows, rows), 0)
    column = lax.broadcasted_iota(jnp.int32, (rows, rows), 1)
    sums = jnp.sum(jnp.where(row == column, stats[0:1, :], 0.0), axis=1, keepdims=True)
    squares = jnp.sum(jnp.where(row == column, stats[1:2, :], 0.0), axis=1, keepdims=True)
    center = sums / width_all
    spread = squares / width_all - center * center
    inverse = lax.rsqrt(spread + 1e-05)
    gain = gain_ref[...].reshape(1, width)
    order = halving_order(count)
    for j in range(count):
        pick = slice(j * block, (j + 1) * block)
        place = jnp.int32(0)
        for k, d in enumerate(order):
            place = jnp.where((me ^ d) == j, k, place)
        place = pl.multiple_of(place * block, 16)
        scaled = (x_ref[pick, :].astype(jnp.float32) - center[pick]) * inverse[pick] * gain
        normed[pl.ds(place, block), :] = scaled.astype(jnp.bfloat16)
    for j in range(narrow_count):
        @pl.when(narrow == j)
        def _(j=j):
            own[...] = normed[:, j * sub_width : (j + 1) * sub_width]

    queries = w_ref.shape[1]

    def products(source, start):
        got = jnp.dot(normed[:, start : start + source.shape[0]], source[...], preferred_element_type=jnp.float32)
        if start:
            kept_ref[:, :queries] += got[:half, :]
            sent_ref[:, :queries] += got[half:, :]
        else:
            kept_ref[:, :queries] = got[:half, :]
            sent_ref[:, :queries] = got[half:, :]

    fresh = jnp.dot(own[...], kv_ref[...], preferred_element_type=jnp.float32)
    kept_ref[:, queries:] = fresh[:half, :]
    sent_ref[:, queries:] = fresh[half:, :]
    products(first_ref, 0)
    for g, fetch in enumerate(fetches):
        fetch.wait()
        if g + ahead < len(fetches):
            fetches[g + ahead].start()
        products(blocks[g], starts[g + 1])


def project(stats, x, gain, w, kv, first, width_all, count, narrow_count):
    rows, width = x.shape
    queries = w.shape[1]
    blocks = row_blocks(width)[1:]
    half = jax.ShapeDtypeStruct((rows // 2, queries + kv.shape[1]), jnp.float32)
    return call(
        functools.partial(project_kernel, len(stats), width_all, count, narrow_count),
        (half, half),
        (*stats, x, gain, in_hbm(w), in_vmem(kv), in_vmem(first)),
        [FULL] * (len(stats) + 2) + [ANY] + [FULL] * 2,
        "project",
        scratch=[
            pltpu.VMEM((rows, width), jnp.bfloat16),
            pltpu.VMEM((rows, width // narrow_count), jnp.bfloat16),
            *[pltpu.VMEM((n, queries), jnp.bfloat16) for n in blocks],
            pltpu.SemaphoreType.DMA((len(blocks),)),
        ],
        limit=36,
        flops=2 * rows * width * queries,
        moved=2 * sum(blocks) * queries,
    )


def fold_kernel(kept_ref, came_ref, still_ref, sent_ref):
    half = still_ref.shape[0]
    still_ref[...] = kept_ref[:half, :] + came_ref[:half, :]
    sent_ref[...] = kept_ref[half:, :] + came_ref[half:, :]


def fold(kept, came):
    half = jax.ShapeDtypeStruct((kept.shape[0] // 2, kept.shape[1]), jnp.float32)
    return call(
        fold_kernel,
        (half, half),
        (kept, came),
        [FULL] * 2,
        "fold",
        flops=BESIDE,
    )


def split_kernel(queries, kept_ref, came_ref, *refs):
    out_refs, slots = refs[:-1], refs[-1]
    count = len(out_refs)
    narrow = lax.axis_index("narrow")
    total = kept_ref[...] + came_ref[...]
    rows, columns = total.shape[0] // count, total.shape[1]
    half = slots.shape[1]
    fresh = total[:, queries:]
    low = fresh - fresh.astype(jnp.bfloat16).astype(jnp.float32)
    for j in range(count):
        mine = slice(j * rows, (j + 1) * rows)
        slots[j * PAD : j * PAD + rows, :] = total[mine, :half]
        slots[j * PAD + rows : (j + 1) * PAD, : columns - half] = total[mine, half:]
        slots[j * PAD + rows : (j + 1) * PAD, columns - half :] = low[mine, :]
    for d, out_ref in enumerate(out_refs):
        out_ref[...] = slots[pl.ds(pl.multiple_of((narrow ^ d) * PAD, PAD), PAD), :].astype(jnp.bfloat16)


def attend_kernel(head_dim, count, lengths_ref, *refs):
    came_refs, kv_ref = by_distance(refs[:count]), refs[count]
    out_refs, (heads, contexts) = refs[count + 1 : 2 * count + 1], refs[2 * count + 1 :]
    rows, positions = kv_ref.shape[0], kv_ref.shape[1]
    half = came_refs[0].shape[1]
    queries = 2 * out_refs[0].shape[1]
    each = queries // head_dim
    slabs = head_dim // LANES
    group = each // 2
    half_heads = count * group
    scaling = 1.0 / math.sqrt(head_dim)
    terms = 0.0
    for d, ref in enumerate(came_refs):
        for c in range(0, half, LANES):
            both = ref[:, c : c + LANES].astype(jnp.float32)
            for column, part in ((c, both[:rows, :]), (half + c, both[rows:, :])):
                if column < queries:
                    h = column // head_dim
                    at = ((h // group) * half_heads + d * group + h % group) * PAD
                    heads[column % head_dim // LANES, at : at + rows, :] = part
        terms = terms + ref[:, queries - half :].astype(jnp.float32)[rows:, :]
    pair = 2 * head_dim
    fresh = terms[:, :pair] + terms[:, pair:]
    fresh = fresh.astype(jnp.bfloat16).astype(jnp.float32)
    place = lax.broadcasted_iota(jnp.int32, (2 * half_heads, positions), 1)
    for r in range(rows):
        query = jnp.concatenate([heads[k, pl.ds(r, 2 * half_heads, stride=PAD), :] for k in range(slabs)], axis=1)
        scores = (
            lax.dot_general(
                query.astype(jnp.bfloat16),
                kv_ref[r, :, :head_dim],
                (((1,), (1,)), ((), ())),
                preferred_element_type=jnp.float32,
            )
            * scaling
        )
        own_score = jnp.sum(query * fresh[r : r + 1, :head_dim], axis=1, keepdims=True) * scaling
        valid = place < lengths_ref[:, r : r + 1]
        top = jnp.maximum(jnp.max(jnp.where(valid, scores, -jnp.inf), axis=1, keepdims=True), own_score)
        weights = jnp.where(valid, jnp.exp(scores - top), 0.0)
        own_weight = jnp.exp(own_score - top)
        total = jnp.sum(weights, axis=1, keepdims=True) + own_weight
        numer = jnp.dot(weights.astype(jnp.bfloat16), kv_ref[r, :, head_dim:], preferred_element_type=jnp.float32)
        numer = numer + own_weight.astype(jnp.bfloat16).astype(jnp.float32) * fresh[r : r + 1, head_dim:]
        context = numer / total
        for k in range(slabs):
            for side in range(2):
                contexts[k, pl.ds(side * rows + r, half_heads, stride=PAD), :] = context[
                    side * half_heads : (side + 1) * half_heads, k * LANES : (k + 1) * LANES
                ]
    for d, ref in enumerate(out_refs):
        for h in range(group):
            at = (d * group + h) * PAD
            for k in range(slabs):
                start = h * head_dim + k * LANES
                ref[:, start : start + LANES] = contexts[k, at : at + PAD, :].astype(jnp.bfloat16)


def attend(lengths, came, kv, head_dim, queries):
    count = len(came)
    all_heads = count * queries // head_dim
    slabs = head_dim // LANES
    return call(
        functools.partial(attend_kernel, head_dim, count),
        [jax.ShapeDtypeStruct((PAD, queries // 2), jnp.bfloat16)] * count,
        (lengths, *came, in_vmem(kv)),
        [FULL] * (count + 2),
        "attend",
        scratch=[
            pltpu.VMEM((slabs, all_heads * PAD, LANES), jnp.float32),
            pltpu.VMEM((slabs, all_heads // 2 * PAD, LANES), jnp.float32),
        ],
        limit=8,
        flops=BESIDE,
    )


def join_kernel(*refs):
    count = len(refs) - 2
    out_ref, joined = refs[-2:]
    half = joined.shape[1]
    rows = out_ref.shape[0] // count
    for d, ref in enumerate(by_distance(refs[:count], half_first=True)):
        at = pl.ds(pl.multiple_of((lax.axis_index("narrow") ^ d) * PAD, PAD), PAD)
        joined[at, :] = ref[...].astype(jnp.float32)
    for side in range(2):
        came = [joined[j * PAD + side * rows : j * PAD + (side + 1) * rows, :] for j in range(count)]
        out_ref[:, side * half : (side + 1) * half] = jnp.concatenate(came, axis=0).astype(jnp.bfloat16)


def code(x, ref):
    largest = jnp.maximum(jnp.max(jnp.abs(x), axis=1, keepdims=True), TINY)
    power = jnp.floor(jnp.log2(largest)) + 1.0
    steps = jnp.round(x * (STEPS * jnp.exp2(-power)))
    ref[:, : x.shape[1]] = steps.astype(jnp.int32).astype(jnp.int16)
    ref[:, x.shape[1] :] = jnp.broadcast_to(power, (x.shape[0], LANES)).astype(jnp.int32).astype(jnp.int16)


def decode(ref, width):
    power = ref[:, width:].astype(jnp.int32).astype(jnp.float32)[:, 0:1]
    return ref[:, :width].astype(jnp.int32).astype(jnp.float32) * (jnp.exp2(power) * (1.0 / STEPS))


def output_kernel(start, count, narrow_count, *refs):
    x_refs, w_ref, (sums_ref, sent_ref) = refs[:count], refs[count], refs[-2:]
    block = x_refs[0].shape[0]
    ratio = count // narrow_count
    places = []
    for d in range(count):
        wide = lax.axis_index("wide") ^ d
        apart = (wide // ratio) ^ lax.axis_index("narrow")
        place = jnp.int32(0)
        for k, distance in enumerate(halving_order(narrow_count)):
            place = jnp.where(apart == distance, k, place)
        places.append(pl.multiple_of((place * ratio + wide % ratio) * block, block))
    x = jnp.concatenate([ref[...] for ref in x_refs], axis=0)
    got = jnp.dot(x, w_ref[:, start : start + sums_ref.shape[1]], preferred_element_type=jnp.float32)
    for d, place in enumerate(places):
        sums_ref[pl.ds(place, block), :] = got[d * block : (d + 1) * block, :]
    code(sums_ref[sums_ref.shape[0] // 2 :, :], sent_ref)


def output_part(blocks, w, start, columns, narrow_count, after):
    count = len(blocks)
    block, depth = blocks[0].shape
    rows = count * block
    return call(
        functools.partial(output_kernel, start, count, narrow_count),
        (
            jax.ShapeDtypeStruct((rows, columns), jnp.float32),
            jax.ShapeDtypeStruct((rows // 2, columns + LANES), jnp.int16),
        ),
        (*blocks, in_vmem(w), *after),
        [FULL] * (count + 1) + [ANY] * len(after),
        "output_part",
        limit=8,
        flops=2 * rows * depth * columns,
        moved=2 * rows * depth,
    )


def halve_kernel(sums_ref, came_ref, *refs):
    still_ref, sent_ref = refs[-2:]
    half = still_ref.shape[0]
    total = sums_ref[: 2 * half, :] + decode(came_ref, sums_ref.shape[1])
    still_ref[...] = total[:half, :]
    code(total[half:, :], sent_ref)


def halve(sums, came, after):
    rows, columns = came.shape[0], sums.shape[1]
    return call(
        halve_kernel,
        (
            jax.ShapeDtypeStruct((rows // 2, columns), jnp.float32),
            jax.ShapeDtypeStruct((rows // 2, columns + LANES), jnp.int16),
        ),
        (sums, came, *after),
        [FULL, FULL] + [ANY] * len(after),
        "halve",
        moved=16 * rows * columns,
    )


def finish_kernel(start, kept_ref, came_ref, *refs):
    out_ref, done, sem = refs[-3:]
    width = kept_ref.shape[1]
    done[...] = (kept_ref[...] + decode(came_ref, width)).astype(jnp.bfloat16)
    copy = pltpu.make_async_copy(done, out_ref.at[:, start : start + width], sem)
    copy.start()
    copy.wait()


def finish(kept, came, start, columns, result):
    rows, width = kept.shape
    return pl.pallas_call(
        functools.partial(finish_kernel, start),
        out_shape=pltpu.HBM((rows, columns), jnp.bfloat16),
        in_specs=[FULL, FULL] + [ANY] * (result is not None),
        out_specs=ANY,
        scratch_shapes=[pltpu.VMEM((rows, width), jnp.bfloat16), pltpu.SemaphoreType.DMA],
        input_output_aliases={} if result is None else {2: 0},
        compiler_params=pltpu.CompilerParams(vmem_limit_bytes=4 * MIB),
        cost_estimate=pl.CostEstimate(flops=0, bytes_accessed=8 * rows * width, transcendentals=0),
        name="finish",
    )(kept, came, *([] if result is None else [in_hbm(result)]))


def local(activations, norm_gain, query_weight, kv_weight, out_weight, kv_cache, lengths):
    wide_count = lax.axis_size("wide")
    narrow_count = lax.axis_size("narrow")
    own_rows, head_dim = kv_cache.shape[0], kv_cache.shape[2] // 2
    assert PAD == 2 * own_rows
    rows, width = activations.shape
    queries = query_weight.shape[1]
    columns = out_weight.shape[1]
    values = activations.astype(jnp.float32)
    stats = jnp.stack([jnp.sum(values, axis=1), jnp.sum(values * values, axis=1)])
    first_part = fetch(query_weight, row_blocks(width)[0], [stats])
    kept, sent = project(
        sent_apart(stats, "wide"),
        activations,
        norm_gain,
        query_weight,
        kv_weight,
        first_part,
        width * wide_count,
        wide_count,
        narrow_count,
    )
    d = 1
    while 2 * d < wide_count:
        kept, sent = fold(kept, swap(sent, "wide", d))
        d *= 2
    split = call(
        functools.partial(split_kernel, queries),
        [jax.ShapeDtypeStruct((PAD, queries // 2 + 2 * head_dim), jnp.bfloat16)] * narrow_count,
        (kept, swap(sent, "wide", d)),
        [FULL] * 2,
        "split",
        scratch=[pltpu.VMEM((narrow_count * PAD, queries // 2 + 2 * head_dim), jnp.float32)],
        flops=BESIDE,
    )
    context = attend(lengths[None], exchange(split, "narrow"), kv_cache, head_dim, queries)
    returned = call(
        join_kernel,
        jax.ShapeDtypeStruct((narrow_count * own_rows, queries), jnp.bfloat16),
        exchange(context, "narrow", half_first=True),
        [FULL] * narrow_count,
        "join",
        scratch=[pltpu.VMEM((narrow_count * PAD, queries // 2), jnp.float32)],
        flops=BESIDE,
    )
    gathered = gather(returned, "wide")
    ends = [columns // LANES * k // 18 * LANES for k in (0,7,15,18)]
    cut_sums, halved, last = [], [], []

    def exchange_cut(kept, sent, after):
        d = 1
        while 2 * d < narrow_count:
            kept, sent = halve(kept, swap(sent, "narrow", d), after)
            after = []
            d *= 2
        halved.append(kept)
        cut_sums.append((kept, swap(sent, "narrow", d)))

    for start, end in zip(ends, ends[1:]):
        kept, sent = output_part(gathered, out_weight, start, end - start, narrow_count, halved[-1:])
        if last:
            exchange_cut(*last, [kept])
        last = (kept, sent)
    result = finish(*cut_sums[0], ends[0], columns, None)
    exchange_cut(*last, [in_hbm(result)])
    for cut, start in zip(cut_sums[1:], ends[1:]):
        result = finish(*cut, start, columns, result)
    return result


def solution(mesh):
    return jax.shard_map(
        local,
        mesh=mesh,
        in_specs=(
            P("groups", "wide"),
            P("wide"),
            P("wide", "narrow"),
            P(("wide", "narrow"), None),
            P("narrow", "wide"),
            P(("groups", "wide", "narrow"), None, None),
            P(("groups", "wide", "narrow")),
        ),
        out_specs=P(("groups", "narrow"), "wide"),
        check_vma=False,
    )
```

```python
import functools
import math

import jax
import jax.numpy as jnp
from jax import lax
from jax.experimental import pallas as pl
from jax.experimental.pallas import tpu as pltpu
from jax.sharding import PartitionSpec as P

MIB = 1 << 20
FULL = pl.BlockSpec(memory_space=pltpu.VMEM)
ANY = pl.BlockSpec(memory_space=pl.ANY)
STEPS = 32700.0
TINY = 1e-37
LANES = 128
PAD = 8
BESIDE = 5 * 10**9


def call(kernel, outs, ins, specs, name, scratch=(), limit=4, flops=0, moved=0):
    return pl.pallas_call(
        kernel,
        out_shape=outs,
        in_specs=specs,
        out_specs=jax.tree.map(lambda _: FULL, outs),
        scratch_shapes=list(scratch),
        compiler_params=pltpu.CompilerParams(vmem_limit_bytes=limit * MIB),
        cost_estimate=pl.CostEstimate(flops=flops, bytes_accessed=moved, transcendentals=0),
        name=name,
    )(*ins)


def held(shape, dtype):
    return pltpu.VMEM(shape, dtype)


def in_vmem(x):
    return pltpu.with_memory_space_constraint(x, pltpu.VMEM)


def in_hbm(x):
    return pltpu.with_memory_space_constraint(x, pltpu.HBM)


def swap(x, axis, distance):
    count = lax.axis_size(axis)
    return lax.ppermute(x, axis, [(i, i ^ distance) for i in range(count)])


def sent_apart(x, axis):
    count = lax.axis_size(axis)
    if count <= 4:
        return [x] + [swap(x, axis, d) for d in range(1, count)]
    d = 1
    while d < count:
        x = x + swap(x, axis, d)
        d *= 2
    return [x]


def start_order(count):
    return sorted(range(1, count), key=lambda d: (d != count // 2, -d))


def exchange(blocks, axis):
    return [swap(blocks[d], axis, d) for d in start_order(len(blocks))] + [blocks[0]]


def by_distance(came):
    order = start_order(len(came)) + [0]
    return [came[order.index(d)] for d in range(len(came))]


def gather(x, axis):
    count = lax.axis_size(axis)
    blocks = {0: x}
    d = count // 2
    while d:
        blocks |= {k ^ d: swap(b, axis, d) for k, b in blocks.items()}
        d //= 2
    return [blocks[k] for k in range(count)]


def halving_order(count):
    bits = count.bit_length() - 1
    return [sum(((k >> b) & 1) << (bits - 1 - b) for b in range(bits)) for k in range(count)]


def fetch_kernel(w_ref, *refs):
    share_ref, sem = refs[-2:]
    fetch = pltpu.make_async_copy(w_ref.at[: share_ref.shape[0]], share_ref, sem)
    fetch.start()
    fetch.wait()


def fetch(w, rows, after):
    return call(
        fetch_kernel,
        held((rows, w.shape[1]), w.dtype),
        (in_hbm(w), *after),
        [ANY] * (1 + len(after)),
        "fetch_query_weight",
        scratch=[pltpu.SemaphoreType.DMA],
        moved=2 * rows * w.shape[1],
    )


def row_blocks(rows):
    tiles = rows // LANES
    step = max(1, tiles // 6)
    blocks = [step]
    while tiles - sum(blocks) > step:
        blocks.append(step)
    last = tiles - sum(blocks)
    blocks += [last - last // 3, last // 3] if last > 2 else [last]
    return [LANES * n for n in blocks]


def project_kernel(many, streamed, width_all, count, narrow_count, *refs):
    stat_refs, refs = refs[:many], refs[many:]
    x_ref, gain_ref, w_ref, kv_ref, first_ref, *sum_refs, normed, own = refs[: len(refs) - 1 - streamed]
    blocks, sems = refs[len(refs) - 1 - streamed : -1], refs[-1]
    rows, width = x_ref.shape
    half = rows // 2
    block = rows // count
    sub_width = width // narrow_count
    sizes = [ref.shape[0] for ref in (first_ref, *blocks)]
    starts = [sum(sizes[:g]) for g in range(len(sizes))]
    fetches = [
        pltpu.make_async_copy(w_ref.at[start : start + size], ref, sems.at[g])
        for g, (start, size, ref) in enumerate(zip(starts[1:], sizes[1:], blocks))
    ]
    ahead = 3
    for fetch in fetches[:ahead]:
        fetch.start()
    me, narrow = lax.axis_index("wide"), lax.axis_index("narrow")
    stats = stat_refs[0][...]
    for ref in stat_refs[1:]:
        stats = stats + ref[...]
    row = lax.broadcasted_iota(jnp.int32, (rows, rows), 0)
    column = lax.broadcasted_iota(jnp.int32, (rows, rows), 1)
    sums = jnp.sum(jnp.where(row == column, stats[0:1, :], 0.0), axis=1, keepdims=True)
    squares = jnp.sum(jnp.where(row == column, stats[1:2, :], 0.0), axis=1, keepdims=True)
    center = sums / width_all
    spread = squares / width_all - center * center
    inverse = lax.rsqrt(spread + 1e-05)
    gain = gain_ref[...].reshape(1, width)
    order = halving_order(count)
    for j in range(count):
        pick = slice(j * block, (j + 1) * block)
        place = jnp.int32(0)
        for k, d in enumerate(order):
            place = jnp.where((me ^ d) == j, k, place)
        place = pl.multiple_of(place * block, 16)
        scaled = (x_ref[pick, :].astype(jnp.float32) - center[pick]) * inverse[pick] * gain
        normed[pl.ds(place, block), :] = scaled.astype(jnp.bfloat16)
    for j in range(narrow_count):
        @pl.when(narrow == j)
        def _(j=j):
            own[...] = normed[:, j * sub_width : (j + 1) * sub_width]

    queries = w_ref.shape[1]
    cut = queries // 2

    def products(source, start):
        got = jnp.dot(normed[:, start : start + source.shape[0]], source[...], preferred_element_type=jnp.float32)
        for ref, side, columns in zip(sum_refs, (0, 0, 1, 1), (slice(0, cut), slice(cut, queries)) * 2):
            part = got[side * half : (side + 1) * half, columns]
            if start:
                ref[:, :cut] += part
            else:
                ref[:, :cut] = part

    fresh = jnp.dot(own[...], kv_ref[...], preferred_element_type=jnp.float32)
    sum_refs[0][:, cut:] = fresh[:half, :]
    sum_refs[2][:, cut:] = fresh[half:, :]
    products(first_ref, 0)
    for g, fetch in enumerate(fetches):
        fetch.wait()
        if g + ahead < len(fetches):
            fetches[g + ahead].start()
        products(blocks[g], starts[g + 1])


def project(stats, x, gain, w, kv, first, width_all, count, narrow_count):
    rows, width = x.shape
    queries = w.shape[1]
    blocks = row_blocks(width)[1:]
    halves = [jax.ShapeDtypeStruct((rows // 2, queries // 2 + n), jnp.float32) for n in (kv.shape[1], 0)]
    return call(
        functools.partial(project_kernel, len(stats), len(blocks), width_all, count, narrow_count),
        halves * 2,
        (*stats, x, gain, in_hbm(w), in_vmem(kv), in_vmem(first)),
        [FULL] * (len(stats) + 2) + [ANY] + [FULL] * 2,
        "project",
        scratch=[
            pltpu.VMEM((rows, width), jnp.bfloat16),
            pltpu.VMEM((rows, width // narrow_count), jnp.bfloat16),
            *[pltpu.VMEM((n, queries), jnp.bfloat16) for n in blocks],
            pltpu.SemaphoreType.DMA((len(blocks),)),
        ],
        limit=36,
        flops=2 * rows * width * queries,
        moved=2 * sum(blocks) * queries,
    )


def fold_kernel(kept_ref, came_ref, *refs):
    still_ref, sent_ref = refs[-2:]
    half = still_ref.shape[0]
    still_ref[...] = kept_ref[:half, :] + came_ref[:half, :]
    sent_ref[...] = kept_ref[half:, :] + came_ref[half:, :]


def fold(kept, came, after):
    half = jax.ShapeDtypeStruct((kept.shape[0] // 2, kept.shape[1]), jnp.float32)
    return call(
        fold_kernel,
        (half, half),
        (kept, came, *after),
        [FULL] * 2 + [ANY] * len(after),
        "fold",
        flops=BESIDE,
    )


def split_kernel(queries, kept_ref, came_ref, kept_2_ref, came_2_ref, *refs):
    out_refs, slots = refs[:-1], refs[-1]
    count = len(out_refs)
    narrow = lax.axis_index("narrow")
    first, second = kept_ref[...] + came_ref[...], kept_2_ref[...] + came_2_ref[...]
    cut = second.shape[1]
    total = jnp.concatenate([first[:, :cut], second, first[:, cut:]], axis=1)
    rows, columns = total.shape[0] // count, total.shape[1]
    half = slots.shape[1]
    fresh = total[:, queries:]
    low = fresh - fresh.astype(jnp.bfloat16).astype(jnp.float32)
    for j in range(count):
        mine = slice(j * rows, (j + 1) * rows)
        slots[j * PAD : j * PAD + rows, :] = total[mine, :half]
        slots[j * PAD + rows : (j + 1) * PAD, : columns - half] = total[mine, half:]
        slots[j * PAD + rows : (j + 1) * PAD, columns - half :] = low[mine, :]
    for d, out_ref in enumerate(out_refs):
        out_ref[...] = slots[pl.ds(pl.multiple_of((narrow ^ d) * PAD, PAD), PAD), :].astype(jnp.bfloat16)


def attend_kernel(head_dim, count, lengths_ref, *refs):
    came_refs, kv_ref = by_distance(refs[:count]), refs[count]
    out_refs, (heads, contexts) = refs[count + 1 : 2 * count + 1], refs[2 * count + 1 :]
    rows, positions = kv_ref.shape[0], kv_ref.shape[1]
    half = came_refs[0].shape[1]
    queries = 2 * out_refs[0].shape[1]
    each = queries // head_dim
    slabs = head_dim // LANES
    group = each // 2
    half_heads = count * group
    scaling = 1.0 / math.sqrt(head_dim)
    terms = 0.0
    for d, ref in enumerate(came_refs):
        for c in range(0, half, LANES):
            both = ref[:, c : c + LANES].astype(jnp.float32)
            for column, part in ((c, both[:rows, :]), (half + c, both[rows:, :])):
                if column < queries:
                    h = column // head_dim
                    at = ((h // group) * half_heads + d * group + h % group) * PAD
                    heads[column % head_dim // LANES, at : at + rows, :] = part
        terms = terms + ref[:, queries - half :].astype(jnp.float32)[rows:, :]
    pair = 2 * head_dim
    fresh = terms[:, :pair] + terms[:, pair:]
    fresh = fresh.astype(jnp.bfloat16).astype(jnp.float32)
    place = lax.broadcasted_iota(jnp.int32, (2 * half_heads, positions), 1)
    for r in range(rows):
        query = jnp.concatenate([heads[k, pl.ds(r, 2 * half_heads, stride=PAD), :] for k in range(slabs)], axis=1)
        scores = (
            lax.dot_general(
                query.astype(jnp.bfloat16),
                kv_ref[r, :, :head_dim],
                (((1,), (1,)), ((), ())),
                preferred_element_type=jnp.float32,
            )
            * scaling
        )
        own_score = jnp.sum(query * fresh[r : r + 1, :head_dim], axis=1, keepdims=True) * scaling
        valid = place < lengths_ref[:, r : r + 1]
        top = jnp.maximum(jnp.max(jnp.where(valid, scores, -jnp.inf), axis=1, keepdims=True), own_score)
        weights = jnp.where(valid, jnp.exp(scores - top), 0.0)
        own_weight = jnp.exp(own_score - top)
        total = jnp.sum(weights, axis=1, keepdims=True) + own_weight
        numer = jnp.dot(weights.astype(jnp.bfloat16), kv_ref[r, :, head_dim:], preferred_element_type=jnp.float32)
        numer = numer + own_weight.astype(jnp.bfloat16).astype(jnp.float32) * fresh[r : r + 1, head_dim:]
        context = numer / total
        for k in range(slabs):
            for side in range(2):
                contexts[k, pl.ds(side * rows + r, half_heads, stride=PAD), :] = context[
                    side * half_heads : (side + 1) * half_heads, k * LANES : (k + 1) * LANES
                ]
    for d, ref in enumerate(out_refs):
        for h in range(group):
            at = (d * group + h) * PAD
            for k in range(slabs):
                start = h * head_dim + k * LANES
                ref[:, start : start + LANES] = contexts[k, at : at + PAD, :].astype(jnp.bfloat16)


def attend(lengths, came, kv, head_dim, queries):
    count = len(came)
    all_heads = count * queries // head_dim
    slabs = head_dim // LANES
    return call(
        functools.partial(attend_kernel, head_dim, count),
        [jax.ShapeDtypeStruct((PAD, queries // 2), jnp.bfloat16)] * count,
        (lengths, *came, in_vmem(kv)),
        [FULL] * (count + 2),
        "attend",
        scratch=[
            pltpu.VMEM((slabs, all_heads * PAD, LANES), jnp.float32),
            pltpu.VMEM((slabs, all_heads // 2 * PAD, LANES), jnp.float32),
        ],
        limit=8,
        flops=BESIDE,
    )


def join_kernel(*refs):
    count = len(refs) - 2
    out_ref, joined = refs[-2:]
    half = joined.shape[1]
    rows = out_ref.shape[0] // count
    for d, ref in enumerate(by_distance(refs[:count])):
        at = pl.ds(pl.multiple_of((lax.axis_index("narrow") ^ d) * PAD, PAD), PAD)
        joined[at, :] = ref[...].astype(jnp.float32)
    for side in range(2):
        came = [joined[j * PAD + side * rows : j * PAD + (side + 1) * rows, :] for j in range(count)]
        out_ref[:, side * half : (side + 1) * half] = jnp.concatenate(came, axis=0).astype(jnp.bfloat16)


def code(x, ref):
    largest = jnp.maximum(jnp.max(jnp.abs(x), axis=1, keepdims=True), TINY)
    power = jnp.floor(jnp.log2(largest)) + 1.0
    steps = jnp.round(x * (STEPS * jnp.exp2(-power)))
    ref[:, : x.shape[1]] = steps.astype(jnp.int32).astype(jnp.int16)
    ref[:, x.shape[1] :] = jnp.broadcast_to(power, (x.shape[0], LANES)).astype(jnp.int32).astype(jnp.int16)


def decode(ref, width):
    power = ref[:, width:].astype(jnp.int32).astype(jnp.float32)[:, 0:1]
    return ref[:, :width].astype(jnp.int32).astype(jnp.float32) * (jnp.exp2(power) * (1.0 / STEPS))


def output_kernel(start, count, narrow_count, *refs):
    x_refs, w_ref, (sums_ref, sent_ref) = refs[:count], refs[count], refs[-2:]
    block = x_refs[0].shape[0]
    ratio = count // narrow_count
    places = []
    for d in range(count):
        wide = lax.axis_index("wide") ^ d
        apart = (wide // ratio) ^ lax.axis_index("narrow")
        place = jnp.int32(0)
        for k, distance in enumerate(halving_order(narrow_count)):
            place = jnp.where(apart == distance, k, place)
        places.append(pl.multiple_of((place * ratio + wide % ratio) * block, block))
    x = jnp.concatenate([ref[...] for ref in x_refs], axis=0)
    got = jnp.dot(x, w_ref[:, start : start + sums_ref.shape[1]], preferred_element_type=jnp.float32)
    for d, place in enumerate(places):
        sums_ref[pl.ds(place, block), :] = got[d * block : (d + 1) * block, :]
    code(sums_ref[sums_ref.shape[0] // 2 :, :], sent_ref)


def output_part(blocks, w, start, columns, narrow_count, after):
    count = len(blocks)
    block, depth = blocks[0].shape
    rows = count * block
    return call(
        functools.partial(output_kernel, start, count, narrow_count),
        (
            jax.ShapeDtypeStruct((rows, columns), jnp.float32),
            jax.ShapeDtypeStruct((rows // 2, columns + LANES), jnp.int16),
        ),
        (*blocks, in_vmem(w), *after),
        [FULL] * (count + 1) + [ANY] * len(after),
        "output_part",
        limit=8,
        flops=2 * rows * depth * columns,
        moved=2 * rows * depth,
    )


def halve_kernel(sums_ref, came_ref, *refs):
    still_ref, sent_ref = refs[-2:]
    half = still_ref.shape[0]
    total = sums_ref[: 2 * half, :] + decode(came_ref, sums_ref.shape[1])
    still_ref[...] = total[:half, :]
    code(total[half:, :], sent_ref)


def halve(sums, came, after):
    rows, columns = came.shape[0], sums.shape[1]
    return call(
        halve_kernel,
        (
            jax.ShapeDtypeStruct((rows // 2, columns), jnp.float32),
            jax.ShapeDtypeStruct((rows // 2, columns + LANES), jnp.int16),
        ),
        (sums, came, *after),
        [FULL, FULL] + [ANY] * len(after),
        "halve",
        moved=16 * rows * columns,
    )


def finish_kernel(start, kept_ref, came_ref, *refs):
    out_ref, done, sem = refs[-3:]
    width = kept_ref.shape[1]
    done[...] = (kept_ref[...] + decode(came_ref, width)).astype(jnp.bfloat16)
    copy = pltpu.make_async_copy(done, out_ref.at[:, start : start + width], sem)
    copy.start()
    copy.wait()


def finish(kept, came, start, columns, result):
    rows, width = kept.shape
    return pl.pallas_call(
        functools.partial(finish_kernel, start),
        out_shape=pltpu.HBM((rows, columns), jnp.bfloat16),
        in_specs=[FULL, FULL] + [ANY] * (result is not None),
        out_specs=ANY,
        scratch_shapes=[pltpu.VMEM((rows, width), jnp.bfloat16), pltpu.SemaphoreType.DMA],
        input_output_aliases={} if result is None else {2: 0},
        compiler_params=pltpu.CompilerParams(vmem_limit_bytes=4 * MIB),
        cost_estimate=pl.CostEstimate(flops=0, bytes_accessed=8 * rows * width, transcendentals=0),
        name="finish",
    )(kept, came, *([] if result is None else [in_hbm(result)]))


def local(activations, norm_gain, query_weight, kv_weight, out_weight, kv_cache, lengths):
    wide_count = lax.axis_size("wide")
    narrow_count = lax.axis_size("narrow")
    own_rows, head_dim = kv_cache.shape[0], kv_cache.shape[2] // 2
    assert PAD == 2 * own_rows
    rows, width = activations.shape
    queries = query_weight.shape[1]
    columns = out_weight.shape[1]
    values = activations.astype(jnp.float32)
    stats = jnp.stack([jnp.sum(values, axis=1), jnp.sum(values * values, axis=1)])
    first_part = fetch(query_weight, row_blocks(width)[0], [stats])
    kept, kept_2, sent, sent_2 = project(
        sent_apart(stats, "wide"),
        activations,
        norm_gain,
        query_weight,
        kv_weight,
        first_part,
        width * wide_count,
        wide_count,
        narrow_count,
    )
    d = 1
    while 2 * d < wide_count:
        kept, sent = fold(kept, swap(sent, "wide", d), [])
        kept_2, sent_2 = fold(kept_2, swap(sent_2, "wide", d), [kept])
        d *= 2
    split = call(
        functools.partial(split_kernel, queries),
        [jax.ShapeDtypeStruct((PAD, queries // 2 + 2 * head_dim), jnp.bfloat16)] * narrow_count,
        (kept, swap(sent, "wide", d), kept_2, swap(sent_2, "wide", d)),
        [FULL] * 4,
        "split",
        scratch=[pltpu.VMEM((narrow_count * PAD, queries // 2 + 2 * head_dim), jnp.float32)],
        flops=BESIDE,
    )
    context = attend(lengths[None], exchange(split, "narrow"), kv_cache, head_dim, queries)
    returned = call(
        join_kernel,
        jax.ShapeDtypeStruct((narrow_count * own_rows, queries), jnp.bfloat16),
        exchange(context, "narrow"),
        [FULL] * narrow_count,
        "join",
        scratch=[pltpu.VMEM((narrow_count * PAD, queries // 2), jnp.float32)],
        flops=BESIDE,
    )
    gathered = gather(returned, "wide")
    ends = [columns // LANES * k // 18 * LANES for k in (0,7,15,18)]
    cut_sums, halved, last = [], [], []

    def exchange_cut(kept, sent, after):
        d = 1
        while 2 * d < narrow_count:
            kept, sent = halve(kept, swap(sent, "narrow", d), after)
            after = []
            d *= 2
        halved.append(kept)
        cut_sums.append((kept, swap(sent, "narrow", d)))

    for start, end in zip(ends, ends[1:]):
        kept, sent = output_part(gathered, out_weight, start, end - start, narrow_count, halved[-1:])
        if last:
            exchange_cut(*last, [kept])
        last = (kept, sent)
    result = finish(*cut_sums[0], ends[0], columns, None)
    exchange_cut(*last, [in_hbm(result)])
    for cut, start in zip(cut_sums[1:], ends[1:]):
        result = finish(*cut, start, columns, result)
    return result


def solution(mesh):
    return jax.shard_map(
        local,
        mesh=mesh,
        in_specs=(
            P("groups", "wide"),
            P("wide"),
            P("wide", "narrow"),
            P(("wide", "narrow"), None),
            P("narrow", "wide"),
            P(("groups", "wide", "narrow"), None, None),
            P(("groups", "wide", "narrow")),
        ),
        out_specs=P(("groups", "narrow"), "wide"),
        check_vma=False,
    )
```

```python
import functools
import math

import jax
import jax.numpy as jnp
from jax import lax
from jax.experimental import pallas as pl
from jax.experimental.pallas import tpu as pltpu
from jax.sharding import PartitionSpec as P

MIB = 1 << 20
FULL = pl.BlockSpec(memory_space=pltpu.VMEM)
ANY = pl.BlockSpec(memory_space=pl.ANY)
STEPS = 32700.0
TINY = 1e-33
LANES = 128
PAD = 8
PIECES = 4
BESIDE = 5 * 10**9


def call(kernel, outs, ins, specs, name, scratch=(), limit=4, flops=0, moved=0):
    return pl.pallas_call(
        kernel,
        out_shape=outs,
        in_specs=specs,
        out_specs=jax.tree.map(lambda _: FULL, outs),
        scratch_shapes=list(scratch),
        compiler_params=pltpu.CompilerParams(vmem_limit_bytes=limit * MIB),
        cost_estimate=pl.CostEstimate(flops=flops, bytes_accessed=moved, transcendentals=0),
        name=name,
    )(*ins)


def held(shape, dtype):
    return pltpu.VMEM(shape, dtype)


def in_vmem(x):
    return pltpu.with_memory_space_constraint(x, pltpu.VMEM)


def in_hbm(x):
    return pltpu.with_memory_space_constraint(x, pltpu.HBM)


def swap(x, axis, distance):
    count = lax.axis_size(axis)
    return lax.ppermute(x, axis, [(i, i ^ distance) for i in range(count)])


def sent_apart(x, axis, entries):
    count = lax.axis_size(axis)
    if count <= 4:
        return [x] + [swap(x, axis, d) for d in range(1, count)]
    d = 1
    while d < count:
        other = swap(x, axis, d)
        between = (x[0] - other[0]) * (x[0] - other[0]) / (2 * entries * d)
        x = jnp.stack([x[0] + other[0], x[1] + other[1] + between])
        d *= 2
    return [x]


def start_order(count):
    return sorted(range(1, count), key=lambda d: (d != count // 2, -d))


def exchange(blocks, axis):
    return [swap(blocks[d], axis, d) for d in start_order(len(blocks))] + [blocks[0]]


def by_distance(came):
    order = start_order(len(came)) + [0]
    return [came[order.index(d)] for d in range(len(came))]


def gather(x, axis):
    count = lax.axis_size(axis)
    blocks = {0: x}
    d = count // 2
    while d:
        blocks |= {k ^ d: swap(b, axis, d) for k, b in blocks.items()}
        d //= 2
    return [blocks[k] for k in range(count)]


def halving_order(count):
    bits = count.bit_length() - 1
    return [sum(((k >> b) & 1) << (bits - 1 - b) for b in range(bits)) for k in range(count)]


def stats_kernel(x_ref, out_ref, copied, sems):
    rows, width = x_ref.shape
    step = rows // PIECES
    pieces = [pl.ds(p * step, step) for p in range(PIECES)]
    copies = [pltpu.make_async_copy(x_ref.at[at], copied.at[at], sems.at[p]) for p, at in enumerate(pieces)]
    for copy in copies:
        copy.start()
    totals, squares = [], []
    for copy, at in zip(copies, pieces):
        copy.wait()
        parts = [copied[at, c : c + LANES].astype(jnp.float32) for c in range(0, width, LANES)]
        total = jnp.sum(functools.reduce(jnp.add, parts), axis=1, keepdims=True)
        apart = [part - total / width for part in parts]
        square = jnp.sum(functools.reduce(jnp.add, [part * part for part in apart]), axis=1, keepdims=True)
        totals.append(total)
        squares.append(square)
    row = lax.broadcasted_iota(jnp.int32, (rows, rows), 0)
    column = lax.broadcasted_iota(jnp.int32, (rows, rows), 1)
    for k, sums in enumerate((totals, squares)):
        sums = jnp.where(row == column, jnp.concatenate(sums, axis=0), 0.0)
        out_ref[k : k + 1, :] = jnp.sum(sums, axis=0, keepdims=True)


def row_sums(x):
    return call(
        stats_kernel,
        jax.ShapeDtypeStruct((2, x.shape[0]), jnp.float32),
        (in_hbm(x),),
        [ANY],
        "row_sums",
        scratch=[pltpu.VMEM(x.shape, x.dtype), pltpu.SemaphoreType.DMA((PIECES,))],
        moved=2 * x.size,
    )


def fetch_kernel(w_ref, *refs):
    share_ref, sem = refs[-2:]
    fetch = pltpu.make_async_copy(w_ref.at[: share_ref.shape[0]], share_ref, sem)
    fetch.start()
    fetch.wait()


def fetch(w, rows, after):
    return call(
        fetch_kernel,
        held((rows, w.shape[1]), w.dtype),
        (in_hbm(w), *after),
        [ANY] * (1 + len(after)),
        "fetch_query_weight",
        scratch=[pltpu.SemaphoreType.DMA],
        moved=2 * rows * w.shape[1],
    )


def row_blocks(rows):
    tiles = rows // LANES
    step = max(1, tiles // 6)
    blocks = [step]
    while tiles - sum(blocks) > step:
        blocks.append(step)
    last = tiles - sum(blocks)
    blocks += [last - last // 3, last // 3] if last > 2 else [last]
    return [LANES * n for n in blocks]


def project_kernel(many, streamed, width_all, count, narrow_count, *refs):
    stat_refs, refs = refs[:many], refs[many:]
    x_ref, gain_ref, w_ref, kv_ref, first_ref, *sum_refs, normed, own = refs[: len(refs) - 1 - streamed]
    blocks, sems = refs[len(refs) - 1 - streamed : -1], refs[-1]
    rows, width = x_ref.shape
    half = rows // 2
    block = rows // count
    sub_width = width // narrow_count
    sizes = [ref.shape[0] for ref in (first_ref, *blocks)]
    starts = [sum(sizes[:g]) for g in range(len(sizes))]
    fetches = [
        pltpu.make_async_copy(w_ref.at[start : start + size], ref, sems.at[g])
        for g, (start, size, ref) in enumerate(zip(starts[1:], sizes[1:], blocks))
    ]
    ahead = 3
    for fetch in fetches[:ahead]:
        fetch.start()
    me, narrow = lax.axis_index("wide"), lax.axis_index("narrow")
    parts = [ref[...] for ref in stat_refs]
    entries = width_all // many
    centers = sum(part[0:1, :] for part in parts) / width_all
    spreads = 0.0
    for part in parts:
        off = part[0:1, :] / entries - centers
        spreads = spreads + part[1:2, :] + entries * (off * off)
    row = lax.broadcasted_iota(jnp.int32, (rows, rows), 0)
    column = lax.broadcasted_iota(jnp.int32, (rows, rows), 1)
    center = jnp.sum(jnp.where(row == column, centers, 0.0), axis=1, keepdims=True)
    spread = jnp.sum(jnp.where(row == column, spreads / width_all, 0.0), axis=1, keepdims=True)
    inverse = lax.rsqrt(spread + 1e-05)
    gain = gain_ref[...].reshape(1, width)
    order = halving_order(count)
    for j in range(count):
        pick = slice(j * block, (j + 1) * block)
        place = jnp.int32(0)
        for k, d in enumerate(order):
            place = jnp.where((me ^ d) == j, k, place)
        place = pl.multiple_of(place * block, 16)
        scaled = (x_ref[pick, :].astype(jnp.float32) - center[pick]) * inverse[pick] * gain
        normed[pl.ds(place, block), :] = scaled.astype(jnp.bfloat16)
    for j in range(narrow_count):
        @pl.when(narrow == j)
        def _(j=j):
            own[...] = normed[:, j * sub_width : (j + 1) * sub_width]

    queries = w_ref.shape[1]
    cut = queries // 2

    def products(source, start):
        got = jnp.dot(normed[:, start : start + source.shape[0]], source[...], preferred_element_type=jnp.float32)
        for ref, side, columns in zip(sum_refs, (0, 0, 1, 1), (slice(0, cut), slice(cut, queries)) * 2):
            part = got[side * half : (side + 1) * half, columns]
            if start:
                ref[:, :cut] += part
            else:
                ref[:, :cut] = part

    fresh = jnp.dot(own[...], kv_ref[...], preferred_element_type=jnp.float32)
    sum_refs[0][:, cut:] = fresh[:half, :]
    sum_refs[2][:, cut:] = fresh[half:, :]
    products(first_ref, 0)
    for g, fetch in enumerate(fetches):
        fetch.wait()
        if g + ahead < len(fetches):
            fetches[g + ahead].start()
        products(blocks[g], starts[g + 1])


def project(stats, x, gain, w, kv, first, width_all, count, narrow_count):
    rows, width = x.shape
    queries = w.shape[1]
    blocks = row_blocks(width)[1:]
    halves = [jax.ShapeDtypeStruct((rows // 2, queries // 2 + n), jnp.float32) for n in (kv.shape[1], 0)]
    return call(
        functools.partial(project_kernel, len(stats), len(blocks), width_all, count, narrow_count),
        halves * 2,
        (*stats, x, gain, in_hbm(w), in_vmem(kv), in_vmem(first)),
        [FULL] * (len(stats) + 2) + [ANY] + [FULL] * 2,
        "project",
        scratch=[
            pltpu.VMEM((rows, width), jnp.bfloat16),
            pltpu.VMEM((rows, width // narrow_count), jnp.bfloat16),
            *[pltpu.VMEM((n, queries), jnp.bfloat16) for n in blocks],
            pltpu.SemaphoreType.DMA((len(blocks),)),
        ],
        limit=36,
        flops=2 * rows * width * queries,
        moved=2 * sum(blocks) * queries,
    )


def fold_kernel(kept_ref, came_ref, *refs):
    still_ref, sent_ref = refs[-2:]
    half = still_ref.shape[0]
    still_ref[...] = kept_ref[:half, :] + came_ref[:half, :]
    sent_ref[...] = kept_ref[half:, :] + came_ref[half:, :]


def fold(kept, came, after):
    half = jax.ShapeDtypeStruct((kept.shape[0] // 2, kept.shape[1]), jnp.float32)
    return call(
        fold_kernel,
        (half, half),
        (kept, came, *after),
        [FULL] * 2 + [ANY] * len(after),
        "fold",
        flops=BESIDE,
    )


def split_kernel(queries, kept_ref, came_ref, kept_2_ref, came_2_ref, *refs):
    out_refs, slots = refs[:-1], refs[-1]
    count = len(out_refs)
    narrow = lax.axis_index("narrow")
    first, second = kept_ref[...] + came_ref[...], kept_2_ref[...] + came_2_ref[...]
    cut = second.shape[1]
    total = jnp.concatenate([first[:, :cut], second, first[:, cut:]], axis=1)
    rows, columns = total.shape[0] // count, total.shape[1]
    half = slots.shape[1]
    fresh = total[:, queries:]
    low = fresh - fresh.astype(jnp.bfloat16).astype(jnp.float32)
    for j in range(count):
        mine = slice(j * rows, (j + 1) * rows)
        slots[j * PAD : j * PAD + rows, :] = total[mine, :half]
        slots[j * PAD + rows : (j + 1) * PAD, : columns - half] = total[mine, half:]
        slots[j * PAD + rows : (j + 1) * PAD, columns - half :] = low[mine, :]
    for d, out_ref in enumerate(out_refs):
        out_ref[...] = slots[pl.ds(pl.multiple_of((narrow ^ d) * PAD, PAD), PAD), :].astype(jnp.bfloat16)


def attend_kernel(head_dim, count, lengths_ref, *refs):
    came_refs, kv_ref = by_distance(refs[:count]), refs[count]
    out_refs, (heads, contexts) = refs[count + 1 : 2 * count + 1], refs[2 * count + 1 :]
    rows, positions = kv_ref.shape[0], kv_ref.shape[1]
    half = came_refs[0].shape[1]
    queries = 2 * out_refs[0].shape[1]
    each = queries // head_dim
    slabs = head_dim // LANES
    group = each // 2
    half_heads = count * group
    scaling = 1.0 / math.sqrt(head_dim)
    terms = 0.0
    for d, ref in enumerate(came_refs):
        for c in range(0, half, LANES):
            both = ref[:, c : c + LANES].astype(jnp.float32)
            for column, part in ((c, both[:rows, :]), (half + c, both[rows:, :])):
                if column < queries:
                    h = column // head_dim
                    at = ((h // group) * half_heads + d * group + h % group) * PAD
                    heads[column % head_dim // LANES, at : at + rows, :] = part
        terms = terms + ref[:, queries - half :].astype(jnp.float32)[rows:, :]
    pair = 2 * head_dim
    fresh = terms[:, :pair] + terms[:, pair:]
    fresh = fresh.astype(jnp.bfloat16).astype(jnp.float32)
    place = lax.broadcasted_iota(jnp.int32, (2 * half_heads, positions), 1)
    for r in range(rows):
        query = jnp.concatenate([heads[k, pl.ds(r, 2 * half_heads, stride=PAD), :] for k in range(slabs)], axis=1)
        scores = (
            lax.dot_general(
                query.astype(jnp.bfloat16),
                kv_ref[r, :, :head_dim],
                (((1,), (1,)), ((), ())),
                preferred_element_type=jnp.float32,
            )
            * scaling
        )
        own_score = jnp.sum(query * fresh[r : r + 1, :head_dim], axis=1, keepdims=True) * scaling
        valid = place < lengths_ref[:, r : r + 1]
        top = jnp.maximum(jnp.max(jnp.where(valid, scores, -jnp.inf), axis=1, keepdims=True), own_score)
        weights = jnp.where(valid, jnp.exp(scores - top), 0.0)
        own_weight = jnp.exp(own_score - top)
        total = jnp.sum(weights, axis=1, keepdims=True) + own_weight
        numer = jnp.dot(weights.astype(jnp.bfloat16), kv_ref[r, :, head_dim:], preferred_element_type=jnp.float32)
        numer = numer + own_weight.astype(jnp.bfloat16).astype(jnp.float32) * fresh[r : r + 1, head_dim:]
        context = numer / total
        for k in range(slabs):
            for side in range(2):
                contexts[k, pl.ds(side * rows + r, half_heads, stride=PAD), :] = context[
                    side * half_heads : (side + 1) * half_heads, k * LANES : (k + 1) * LANES
                ]
    for d, ref in enumerate(out_refs):
        for h in range(group):
            at = (d * group + h) * PAD
            for k in range(slabs):
                start = h * head_dim + k * LANES
                ref[:, start : start + LANES] = contexts[k, at : at + PAD, :].astype(jnp.bfloat16)


def attend(lengths, came, kv, head_dim, queries):
    count = len(came)
    all_heads = count * queries // head_dim
    slabs = head_dim // LANES
    return call(
        functools.partial(attend_kernel, head_dim, count),
        [jax.ShapeDtypeStruct((PAD, queries // 2), jnp.bfloat16)] * count,
        (lengths, *came, in_vmem(kv)),
        [FULL] * (count + 2),
        "attend",
        scratch=[
            pltpu.VMEM((slabs, all_heads * PAD, LANES), jnp.float32),
            pltpu.VMEM((slabs, all_heads // 2 * PAD, LANES), jnp.float32),
        ],
        limit=8,
        flops=BESIDE,
    )


def join_kernel(*refs):
    count = len(refs) - 2
    out_ref, joined = refs[-2:]
    half = joined.shape[1]
    rows = out_ref.shape[0] // count
    for d, ref in enumerate(by_distance(refs[:count])):
        at = pl.ds(pl.multiple_of((lax.axis_index("narrow") ^ d) * PAD, PAD), PAD)
        joined[at, :] = ref[...].astype(jnp.float32)
    for side in range(2):
        came = [joined[j * PAD + side * rows : j * PAD + (side + 1) * rows, :] for j in range(count)]
        out_ref[:, side * half : (side + 1) * half] = jnp.concatenate(came, axis=0).astype(jnp.bfloat16)


def code(x, ref):
    largest = jnp.maximum(jnp.max(jnp.abs(x), axis=1, keepdims=True), TINY)
    power = jnp.floor(jnp.log2(largest)) + 1.0
    steps = jnp.round(x * (STEPS * jnp.exp2(-power)))
    ref[:, : x.shape[1]] = steps.astype(jnp.int32).astype(jnp.int16)
    ref[:, x.shape[1] :] = jnp.broadcast_to(power, (x.shape[0], LANES)).astype(jnp.int32).astype(jnp.int16)


def decode(ref, width):
    power = ref[:, width:].astype(jnp.int32).astype(jnp.float32)[:, 0:1]
    return ref[:, :width].astype(jnp.int32).astype(jnp.float32) * (jnp.exp2(power) * (1.0 / STEPS))


def output_kernel(start, count, narrow_count, *refs):
    x_refs, w_ref, (sums_ref, sent_ref) = refs[:count], refs[count], refs[-2:]
    block = x_refs[0].shape[0]
    ratio = count // narrow_count
    places = []
    for d in range(count):
        wide = lax.axis_index("wide") ^ d
        apart = (wide // ratio) ^ lax.axis_index("narrow")
        place = jnp.int32(0)
        for k, distance in enumerate(halving_order(narrow_count)):
            place = jnp.where(apart == distance, k, place)
        places.append(pl.multiple_of((place * ratio + wide % ratio) * block, block))
    x = jnp.concatenate([ref[...] for ref in x_refs], axis=0)
    got = jnp.dot(x, w_ref[:, start : start + sums_ref.shape[1]], preferred_element_type=jnp.float32)
    for d, place in enumerate(places):
        sums_ref[pl.ds(place, block), :] = got[d * block : (d + 1) * block, :]
    code(sums_ref[sums_ref.shape[0] // 2 :, :], sent_ref)


def output_part(blocks, w, start, columns, narrow_count, after):
    count = len(blocks)
    block, depth = blocks[0].shape
    rows = count * block
    return call(
        functools.partial(output_kernel, start, count, narrow_count),
        (
            jax.ShapeDtypeStruct((rows, columns), jnp.float32),
            jax.ShapeDtypeStruct((rows // 2, columns + LANES), jnp.int16),
        ),
        (*blocks, in_vmem(w), *after),
        [FULL] * (count + 1) + [ANY] * len(after),
        "output_part",
        limit=8,
        flops=2 * rows * depth * columns,
        moved=2 * rows * depth,
    )


def halve_kernel(sums_ref, came_ref, *refs):
    still_ref, sent_ref = refs[-2:]
    half = still_ref.shape[0]
    total = sums_ref[: 2 * half, :] + decode(came_ref, sums_ref.shape[1])
    still_ref[...] = total[:half, :]
    code(total[half:, :], sent_ref)


def halve(sums, came, after):
    rows, columns = came.shape[0], sums.shape[1]
    return call(
        halve_kernel,
        (
            jax.ShapeDtypeStruct((rows // 2, columns), jnp.float32),
            jax.ShapeDtypeStruct((rows // 2, columns + LANES), jnp.int16),
        ),
        (sums, came, *after),
        [FULL, FULL] + [ANY] * len(after),
        "halve",
        moved=16 * rows * columns,
    )


def finish_kernel(start, kept_ref, came_ref, *refs):
    out_ref, done, sem = refs[-3:]
    width = kept_ref.shape[1]
    done[...] = (kept_ref[...] + decode(came_ref, width)).astype(jnp.bfloat16)
    copy = pltpu.make_async_copy(done, out_ref.at[:, start : start + width], sem)
    copy.start()
    copy.wait()


def finish(kept, came, start, columns, result):
    rows, width = kept.shape
    return pl.pallas_call(
        functools.partial(finish_kernel, start),
        out_shape=pltpu.HBM((rows, columns), jnp.bfloat16),
        in_specs=[FULL, FULL] + [ANY] * (result is not None),
        out_specs=ANY,
        scratch_shapes=[pltpu.VMEM((rows, width), jnp.bfloat16), pltpu.SemaphoreType.DMA],
        input_output_aliases={} if result is None else {2: 0},
        compiler_params=pltpu.CompilerParams(vmem_limit_bytes=4 * MIB),
        cost_estimate=pl.CostEstimate(flops=0, bytes_accessed=8 * rows * width, transcendentals=0),
        name="finish",
    )(kept, came, *([] if result is None else [in_hbm(result)]))


def local(activations, norm_gain, query_weight, kv_weight, out_weight, kv_cache, lengths):
    wide_count = lax.axis_size("wide")
    narrow_count = lax.axis_size("narrow")
    own_rows, head_dim = kv_cache.shape[0], kv_cache.shape[2] // 2
    assert PAD == 2 * own_rows
    rows, width = activations.shape
    queries = query_weight.shape[1]
    columns = out_weight.shape[1]
    stats = row_sums(activations)
    first_part = fetch(query_weight, row_blocks(width)[0], [stats])
    kept, kept_2, sent, sent_2 = project(
        sent_apart(stats, "wide", width),
        activations,
        norm_gain,
        query_weight,
        kv_weight,
        first_part,
        width * wide_count,
        wide_count,
        narrow_count,
    )
    d = 1
    while 2 * d < wide_count:
        kept, sent = fold(kept, swap(sent, "wide", d), [])
        kept_2, sent_2 = fold(kept_2, swap(sent_2, "wide", d), [kept])
        d *= 2
    split = call(
        functools.partial(split_kernel, queries),
        [jax.ShapeDtypeStruct((PAD, queries // 2 + 2 * head_dim), jnp.bfloat16)] * narrow_count,
        (kept, swap(sent, "wide", d), kept_2, swap(sent_2, "wide", d)),
        [FULL] * 4,
        "split",
        scratch=[pltpu.VMEM((narrow_count * PAD, queries // 2 + 2 * head_dim), jnp.float32)],
        flops=BESIDE,
    )
    context = attend(lengths[None], exchange(split, "narrow"), kv_cache, head_dim, queries)
    returned = call(
        join_kernel,
        jax.ShapeDtypeStruct((narrow_count * own_rows, queries), jnp.bfloat16),
        exchange(context, "narrow"),
        [FULL] * narrow_count,
        "join",
        scratch=[pltpu.VMEM((narrow_count * PAD, queries // 2), jnp.float32)],
        flops=BESIDE,
    )
    gathered = gather(returned, "wide")
    ends = [columns // LANES * k // 18 * LANES for k in (0,7,15,18)]
    cut_sums, halved, last = [], [], []

    def exchange_cut(kept, sent, after):
        d = 1
        while 2 * d < narrow_count:
            kept, sent = halve(kept, swap(sent, "narrow", d), after)
            after = []
            d *= 2
        halved.append(kept)
        cut_sums.append((kept, swap(sent, "narrow", d)))

    for start, end in zip(ends, ends[1:]):
        kept, sent = output_part(gathered, out_weight, start, end - start, narrow_count, halved[-1:])
        if last:
            exchange_cut(*last, [kept])
        last = (kept, sent)
    result = finish(*cut_sums[0], ends[0], columns, None)
    exchange_cut(*last, [in_hbm(result)])
    for cut, start in zip(cut_sums[1:], ends[1:]):
        result = finish(*cut, start, columns, result)
    return result


def solution(mesh):
    return jax.shard_map(
        local,
        mesh=mesh,
        in_specs=(
            P("groups", "wide"),
            P("wide"),
            P("wide", "narrow"),
            P(("wide", "narrow"), None),
            P("narrow", "wide"),
            P(("groups", "wide", "narrow"), None, None),
            P(("groups", "wide", "narrow")),
        ),
        out_specs=P(("groups", "narrow"), "wide"),
        check_vma=False,
    )
```
